32 devices in a mesh: dp: 8 (over y, x, core), seq: 4 (over z).
Axes of the slice: x: 2, y: 2, z: 4, core: 2. Of those that a mesh axis runs over, the one named last changes fastest.
Arguments:
- hidden_in: bfloat16 [8192, 1536], P(('dp', 'seq')), may hold values from -6 to 6
- segment_ids: int32 [8192], P(('dp', 'seq')), may hold values from 0 to 4, as said below
- position_ids: int32 [8192], P(('dp', 'seq')), may hold values from 0 to 767, as said below
- out_grad: bfloat16 [8192, 1536], P(('dp', 'seq')), may hold values from -6 to 6
- attn_norm: bfloat16 [1536], P('dp'), may hold values from 0.5 to 1.5
- w_query: bfloat16 [1536, 1536], P('dp'), may hold values from -0.15625 to 0.15625
- w_key: bfloat16 [1536, 256], P('dp'), may hold values from -0.15625 to 0.15625
- w_value: bfloat16 [1536, 256], P('dp'), may hold values from -0.15625 to 0.15625
- b_query: bfloat16 [1536], P('dp'), may hold values from -3 to 3
- b_key: bfloat16 [256], P('dp'), may hold values from -3 to 3
- b_value: bfloat16 [256], P('dp'), may hold values from -3 to 3
- w_out: bfloat16 [1536, 1536], P(None, 'dp'), may hold values from -1.25 to 1.25
- mlp_norm: bfloat16 [1536], P('dp'), may hold values from 0.5 to 1.5
- w_gate: bfloat16 [1536, 8960], P('dp', 'seq'), may hold values from -0.15625 to 0.15625
- w_up: bfloat16 [1536, 8960], P('dp', 'seq'), may hold values from -0.15625 to 0.15625
- w_down: bfloat16 [1536, 8960], P('dp', 'seq'), may hold values from -0.25 to 0.25
Outputs:
- block_out: bfloat16 [8192, 1536], P(('dp', 'seq'))
- input_grad: float32 [8192, 1536], P(('dp', 'seq'))
- attn_norm_grad: float32 [1536], P('dp')
- w_query_grad: float32 [1536, 1536], P('dp')
- w_key_grad: float32 [1536, 256], P('dp')
- w_value_grad: float32 [1536, 256], P('dp')
- b_query_grad: float32 [1536], P('dp')
- b_key_grad: float32 [256], P('dp')
- b_value_grad: float32 [256], P('dp')
- w_out_grad: float32 [1536, 1536], P(None, 'dp')
- mlp_norm_grad: float32 [1536], P('dp')
- w_gate_grad: float32 [1536, 8960], P('dp', 'seq')
- w_up_grad: float32 [1536, 8960], P('dp', 'seq')
- w_down_grad: float32 [1536, 8960], P('dp', 'seq')
The draws below stay inside these ranges and needn't reach their ends.
Inputs may be any that keep to these rules, and one draw needn't show every extreme that they name: `segment_ids`: within each row of 1024 tokens the ids start at 0 and never fall; one segment runs from a token among the row's first 256 to one among its last 256. `position_ids`: A position is 0 at the first token of its segment; from each token to the next inside the segment it rises by 1 or 2 until it reaches the maximum, and stays there. Every row reaches the maximum.
All inputs are finite; a program needn't handle non-finite values.
Results may differ from the reference program's by a relative error of at most 0.025.
Values may be sent and summed in bfloat16 or wider, within the bound.
A program may use at most 256 MiB of HBM per device.

```python
import jax
import jax.numpy as jnp
from jax import lax

D = 1536
HEADS = 12
KV_HEADS = 2
HD = 128
FF = 8960
TOK_DEV = 256
ROW = 1024
ROWS = 8
TOKENS = 8192
N_SEQ = 4


def packed_layout(key):
    subkeys = jax.random.split(jax.random.fold_in(key, 71), 5)
    half_block = TOK_DEV // 2 + 1
    long_start = jax.random.randint(subkeys[0], (ROWS, 1), 2, half_block)
    first_cut = jax.random.randint(subkeys[1], (ROWS, 1), 1, long_start)
    long_end = ROW - jax.random.randint(subkeys[2], (ROWS, 1), 2, half_block)
    last_cut = long_end + jax.random.randint(subkeys[3], (ROWS, 1), 1, ROW - long_end)
    token_index = jnp.arange(ROW, dtype=jnp.int32)[None, :]
    segment = (token_index >= first_cut).astype(jnp.int32) + (token_index >= long_start).astype(jnp.int32)
    segment = segment + (token_index >= long_end).astype(jnp.int32) + (token_index >= last_cut).astype(jnp.int32)
    seg_start = jnp.where(token_index >= last_cut, last_cut, jnp.where(token_index >= long_end, long_end, jnp.where(token_index >= long_start, long_start, jnp.where(token_index >= first_cut, first_cut, 0))))
    seg_start = jnp.broadcast_to(seg_start, (ROWS, ROW)).astype(jnp.int32)
    steps_up = 1 + (jax.random.randint(subkeys[4], (ROWS, ROW), 0, 4) == 0).astype(jnp.int32)
    running = jnp.cumsum(steps_up, axis=1).astype(jnp.int32)
    position = running - jnp.take_along_axis(running, seg_start, axis=1)
    position = jnp.minimum(position, ROW - TOK_DEV - 1)
    return (segment.reshape(TOKENS).astype(jnp.int32), position.reshape(TOKENS).astype(jnp.int32))


def draw_segment_ids(key, part):
    return packed_layout(key)[0]


def draw_position_ids(key, part):
    return packed_layout(key)[1]


def raised(result, key, source, target, parts, factor):
    def block_of(dim):
        return (jnp.arange(result.shape[dim]) // (result.shape[dim] // parts)).reshape((-1,) + (1,) * (result.ndim - 1 - dim))

    first = jax.random.permutation(key, parts)[block_of(target)]
    far = (block_of(target) + parts // 2) % parts
    return jnp.where((block_of(source) == first) | (block_of(source) == far), factor * result, result)


def shard_levels(stream_key, extent, cuts, smallest, top_value):
    loudness = 1.0
    for axis_at, parts in cuts:
        heights = jax.random.uniform(jax.random.fold_in(jax.random.fold_in(stream_key, 6), axis_at), (parts,), jnp.float32, smallest / len(cuts), top_value / len(cuts))
        loudness = loudness * jnp.repeat(jnp.exp(heights), extent[axis_at] // parts).reshape((-1,) + (1,) * (len(extent) - 1 - axis_at))
    return loudness


def normal_values(own_key, shape, spread, reach, shards=(), held_as=jnp.bfloat16):
    result = jax.random.normal(own_key, shape, jnp.float32) * spread
    if len(shards) > 0:
        result = shard_levels(own_key, shape, shards, -0.22, 0.18) * result
    return jnp.clip(result, min=-reach, max=reach).astype(held_as)


def noise_with(key, dims, deviation, limit, cuts, heavy, held_as=jnp.bfloat16):
    result = deviation * jax.random.normal(key, dims, jnp.float32)
    if cuts:
        result = result * shard_levels(key, dims, cuts, -0.22, 0.18)
    return jnp.clip(raised(result, jax.random.fold_in(key, 3), *heavy), -limit, limit).astype(held_as)


def setup_inputs(seed: int = 0) -> dict:
    streams_of = jax.random.split(jax.random.key(seed), 17)
    return {
        "hidden_in": noise_with(streams_of[0], (TOKENS, D), 1.0, 6.0, ((0, 32),), (0, 1, 32, 2.75)),
        "segment_ids": draw_segment_ids(jax.random.fold_in(streams_of[16], 71), 0),
        "position_ids": draw_position_ids(jax.random.fold_in(streams_of[16], 71), 0),
        "out_grad": noise_with(streams_of[3], (TOKENS, D), 1.0, 6.0, ((0, 32),), (0, 1, 32, 2.75)),
        "attn_norm": jnp.clip(1.0 + 0.1 * jax.random.normal(streams_of[4], (D,), jnp.float32), 0.5, 1.5).astype(jnp.bfloat16),
        "w_query": normal_values(streams_of[5], (D, HEADS * HD), D ** -0.5, 0.15625, ((0, 8),)),
        "w_key": normal_values(streams_of[6], (D, KV_HEADS * HD), D ** -0.5, 0.15625, ((0, 8),)),
        "w_value": normal_values(streams_of[7], (D, KV_HEADS * HD), D ** -0.5, 0.15625, ((0, 8),)),
        "b_query": normal_values(streams_of[8], (HEADS * HD,), 0.5, 3.0, ((0, 8),)),
        "b_key": normal_values(streams_of[9], (KV_HEADS * HD,), 0.5, 3.0, ((0, 8),)),
        "b_value": normal_values(streams_of[10], (KV_HEADS * HD,), 0.5, 3.0, ((0, 8),)),
        "w_out": normal_values(streams_of[11], (HEADS * HD, D), (HEADS * HD // 64) ** -0.5, 1.25, ((1, 8),)),
        "mlp_norm": jnp.clip(1.0 + 0.1 * jax.random.normal(streams_of[12], (D,), jnp.float32), 0.5, 1.5).astype(jnp.bfloat16),
        "w_gate": normal_values(streams_of[13], (D, FF), D ** -0.5, 0.15625, ((0, 8), (1, 4))),
        "w_up": normal_values(streams_of[14], (D, FF), D ** -0.5, 0.15625, ((0, 8), (1, 4))),
        "w_down": normal_values(streams_of[15], (D, FF), (FF // 16) ** -0.5, 0.25, ((0, 8), (1, 4))),
    }


@jax.custom_vjp
def low(v):
    return lax.optimization_barrier(v.astype(jnp.bfloat16)).astype(jnp.float32)

@jax.custom_vjp
def low_back(v):
    return v

def low_keep(v):
    return (low(v), None)

def low_pass(kept, grad):
    return (grad,)

def back_keep(v):
    return (v, None)

def back_low(kept, grad):
    return (low(grad),)
low.defvjp(low_keep, low_pass)
low_back.defvjp(back_keep, back_low)
EPS = 1e-06
ROPE_BASE = 1000000.0
NEG_FILL = -1e+30
PRECISE = lax.Precision.HIGHEST

def product(left, right):
    return jnp.dot(left, right, precision=PRECISE)

def rms_scale(values, gain):
    factor = lax.rsqrt(lax.optimization_barrier(jnp.mean(values * values, axis=-1, keepdims=True)) + EPS)
    return values * factor * gain

def rope_tables(positions):
    half_dim = HD // 2
    inv_freq = ROPE_BASE ** (-(jnp.arange(half_dim).astype(jnp.float32) * 2.0 / HD))
    angles = positions.astype(jnp.float32)[:, None] * inv_freq[None, :]
    cosine_tab = jnp.cos(angles)
    sine_tab = jnp.sin(angles)
    return (jnp.concatenate([cosine_tab, cosine_tab], axis=-1), jnp.concatenate([sine_tab, sine_tab], axis=-1))

def rotate(values, cosine_tab, sine_tab):
    half_dim = values.shape[-1] // 2
    turned = jnp.concatenate([-values[..., half_dim:], values[..., :half_dim]], axis=-1)
    return values * cosine_tab[:, None, :] + turned * sine_tab[:, None, :]

def row_forward(params, row_in, row_seg, row_pos):
    attn_norm, w_query, w_key, w_value, b_query, b_key, b_value, w_out, mlp_norm, w_gate, w_up, w_down = params
    heads_lane = HEADS // N_SEQ
    kv_group = N_SEQ // KV_HEADS
    normed = low(rms_scale(row_in, attn_norm))
    query = low_back(product(normed, w_query) + b_query)
    key_pre = low_back(product(normed, w_key) + b_key)
    value_pre = low_back(product(normed, w_value) + b_value)
    cosine_tab, sine_tab = rope_tables(row_pos)
    query_rot = low_back(low(rotate(query.reshape(ROW, HEADS, HD), cosine_tab, sine_tab)))
    key_rot = low(rotate(key_pre.reshape(ROW, KV_HEADS, HD), cosine_tab, sine_tab))
    value_low = low(value_pre.reshape(ROW, KV_HEADS, HD))
    lane_head = (jnp.arange(N_SEQ) // kv_group).astype(jnp.int32)
    key_lanes = low_back(key_rot[:, lane_head, :])
    value_lanes = low_back(value_low[:, lane_head, :])
    query_lanes = query_rot.reshape(ROW, N_SEQ, heads_lane, HD)
    block_rows = min(512, ROW)
    block_count = ROW // block_rows
    key_index = jnp.arange(ROW).astype(jnp.int32)

    def attend(block_id):
        start = (block_id * block_rows).astype(jnp.int32)
        query_block = lax.dynamic_slice_in_dim(query_lanes, start, block_rows, 0)
        seg_block = lax.dynamic_slice_in_dim(row_seg, start, block_rows, 0)
        query_index = start + jnp.arange(block_rows).astype(jnp.int32)
        scores = low_back(jnp.einsum('qlhd,kld->lhqk', query_block, key_lanes, precision=PRECISE) * HD ** (-0.5))
        keep_mask = (seg_block[:, None] == row_seg[None, :]) & (query_index[:, None] >= key_index[None, :])
        scores = jnp.where(keep_mask[None, None], scores, NEG_FILL)
        attn_prob = low(jax.nn.softmax(scores, axis=-1))
        return jnp.einsum('lhqk,kld->qlhd', attn_prob, value_lanes, precision=PRECISE)
    attended = lax.map(jax.checkpoint(attend), jnp.arange(block_count).astype(jnp.int32))
    attended = low_back(low(attended.reshape(ROW, HEADS * HD)))
    resid = row_in + low_back(product(attended, w_out))
    mlp_in = low(rms_scale(resid, mlp_norm))
    gate_act = low_back(product(mlp_in, w_gate))
    up_act = low_back(product(mlp_in, w_up))
    hidden = low(jax.nn.silu(gate_act) * up_act)
    return resid + low_back(jnp.dot(hidden, w_down.T, precision=PRECISE))

def reference(hidden_in, segment_ids, position_ids, out_grad, attn_norm, w_query, w_key, w_value, b_query, b_key, b_value, w_out, mlp_norm, w_gate, w_up, w_down):
    params = tuple((array.astype(jnp.float32) for array in (attn_norm, w_query, w_key, w_value, b_query, b_key, b_value, w_out, mlp_norm, w_gate, w_up, w_down)))
    seg_rows = segment_ids.reshape(ROWS, ROW)
    pos_rows = position_ids.reshape(ROWS, ROW)

    def forward(input_f32, *params_f32):
        rows_in = input_f32.reshape(ROWS, ROW, D)

        def row_step(carry, items):
            return (carry, row_forward(params_f32, items[0], items[1], items[2]))
        carry_out, rows_out = lax.scan(jax.checkpoint(row_step), jnp.zeros((), jnp.float32), (rows_in, seg_rows, pos_rows))
        return rows_out.reshape(TOKENS, D)
    block_out, pull_back = jax.vjp(forward, hidden_in.astype(jnp.float32), *params)
    grads = pull_back(out_grad.astype(jnp.float32))
    return (block_out.astype(jnp.bfloat16), grads[0], grads[1], grads[2], grads[3], grads[4], grads[5], grads[6], grads[7], grads[8], grads[9], grads[10], grads[11], grads[12])
```

```python
import jax
import jax.numpy as jnp
from jax import lax
from jax.experimental import pallas as pl
from jax.experimental.pallas import tpu as pltpu
from jax.sharding import PartitionSpec as P

HEADS = 12
KV_HEADS = 2
HD = 128


EPS = 1e-06
ROPE_BASE = 1000000.0
NEG_FILL = -1e30


def rope_tables(positions, head_dim):
    half_dim = head_dim // 2
    inv_freq = ROPE_BASE ** (-(jnp.arange(half_dim).astype(jnp.float32) * 2.0 / head_dim))
    angles = positions.astype(jnp.float32)[:, None] * inv_freq[None, :]
    cosine_tab = jnp.cos(angles)
    sine_tab = jnp.sin(angles)
    return (
        jnp.concatenate([cosine_tab, cosine_tab], axis=-1),
        jnp.concatenate([sine_tab, sine_tab], axis=-1),
    )


def rotate(values, cosine_tab, sine_tab):
    half_dim = values.shape[-1] // 2
    turned = jnp.concatenate([-values[..., half_dim:], values[..., :half_dim]], axis=-1)
    return values * cosine_tab[:, None, :] + turned * sine_tab[:, None, :]


def rotate_back(grads, cosine_tab, sine_tab):
    half_dim = grads.shape[-1] // 2
    scaled = grads * sine_tab[:, None, :]
    return grads * cosine_tab[:, None, :] + jnp.concatenate(
        [scaled[..., half_dim:], -scaled[..., :half_dim]], axis=-1
    )


def norm_factor(values):
    return lax.rsqrt(jnp.mean(values * values, axis=-1, keepdims=True) + EPS)


def norm_back(grad_in, values, factor, gain):
    scaled = grad_in * gain
    return factor * scaled - values * factor**3 * jnp.mean(scaled * values, axis=-1, keepdims=True)


def contract_rows(left, right):
    return lax.dot_general(
        left, right, (((0,), (0,)), ((), ())), preferred_element_type=jnp.float32
    )


def contract_cols(left, right):
    return lax.dot_general(
        left, right, (((1,), (1,)), ((), ())), preferred_element_type=jnp.float32
    )


def masked_scores(query_block, keys_all, seg_block, seg_all, start, scale):
    scores = (
        jnp.einsum("qhd,kd->hqk", query_block, keys_all, preferred_element_type=jnp.float32) * scale
    )
    query_index = start + jnp.arange(query_block.shape[0], dtype=jnp.int32)
    key_index = jnp.arange(keys_all.shape[0], dtype=jnp.int32)
    keep_mask = (seg_block[:, None] == seg_all[None, :]) & (
        query_index[:, None] >= key_index[None, :]
    )
    return jnp.where(keep_mask[None], scores, NEG_FILL)


MESH_ID = pl.DeviceIdType.MESH
LANES = 4
BF16 = jnp.bfloat16
F32 = jnp.float32


def nn(left, right):
    return jnp.dot(left, right, preferred_element_type=F32)


def nt(left, right):
    return lax.dot_general(left, right, (((1,), (1,)), ((), ())), preferred_element_type=F32)


def rows_of(index, size):
    return pl.ds(pl.multiple_of(index * size, size), size)


def digit(codes, lane):
    return lax.rem(lax.shift_right_logical(jnp.int32(codes), 2 * lane), 4)


def order_of(step, lane):
    tables = ((0, 1, 2, 3), (1, 0, 2, 3), (2, 3, 1, 0), (3, 2, 1, 0))
    codes = [sum(tables[k][i] * 4**k for k in range(LANES)) for i in range(LANES)]
    out = digit(codes[0], lane)
    for i in range(1, LANES):
        out = jnp.where(step == i, digit(codes[i], lane), out)
    return out


def ff_kernel(
    x_hbm, og_hbm, wg_hbm, wu_hbm, wd_hbm,
    mo_ref, gm_ref, gw_hbm,
    xb, og, wg, wu, wd, hid, gg, gu, pb, rb, rf,
    load_sem, ag_send, ag_recv, rb_send, rb_recv, rf_send, rf_recv, out_sem,
):
    lane = lax.axis_index("seq")
    tok, width = x_hbm.shape
    units = wg_hbm.shape[1]
    tile = 512
    full_tiles = units // tile
    tail = units - full_tiles * tile
    wtile = 384
    has_left, has_right = lane > 0, lane < LANES - 1
    is_end = jnp.logical_or(lane == 0, lane == LANES - 1)
    is_mid = jnp.logical_not(is_end)
    left, right = jnp.maximum(lane - 1, 0), jnp.minimum(lane + 1, LANES - 1)

    loads = [
        pltpu.make_async_copy(src, dst, load_sem.at[k])
        for k, (src, dst) in enumerate(
            ((wg_hbm, wg), (wu_hbm, wu), (wd_hbm, wd), (og_hbm, og))
        )
    ]
    own = pltpu.make_async_copy(x_hbm, xb.at[rows_of(lane, tok)], load_sem.at[4])
    own.start()
    for copy in loads:
        copy.start()

    barrier = pltpu.get_barrier_semaphore()

    @pl.when(has_left)
    def _():
        pl.semaphore_signal(barrier, 1, device_id={"seq": left}, device_id_type=MESH_ID)

    @pl.when(has_right)
    def _():
        pl.semaphore_signal(barrier, 1, device_id={"seq": right}, device_id_type=MESH_ID)

    @pl.when(is_end)
    def _():
        pl.semaphore_wait(barrier, 1)

    @pl.when(is_mid)
    def _():
        pl.semaphore_wait(barrier, 2)

    own.wait()

    def gather_copy(block, way):
        part = xb.at[rows_of(block, tok)]
        return pltpu.make_async_remote_copy(
            part, part, ag_send.at[way, block], ag_recv.at[block],
            device_id={"seq": right if way == 0 else left}, device_id_type=MESH_ID,
        )

    @pl.when(has_right)
    def _():
        gather_copy(lane, 0).start()

    @pl.when(has_left)
    def _():
        gather_copy(lane, 1).start()

    def arrivals(step):
        @pl.when(lane - step >= 0)
        def _():
            block = jnp.maximum(lane - step, 0)
            gather_copy(block, 0).wait_recv()

            @pl.when(has_right)
            def _():
                gather_copy(block, 0).start()

        @pl.when(lane + step < LANES)
        def _():
            block = jnp.minimum(lane + step, LANES - 1)
            gather_copy(block, 1).wait_recv()

            @pl.when(has_left)
            def _():
                gather_copy(block, 1).start()

    def sum_send(part, landing, send, recv, block):
        goes_left = block < lane
        target = jnp.where(goes_left, left, right)
        slot = jnp.where(jnp.logical_and(goes_left, target == block), LANES, block)
        return pltpu.make_async_remote_copy(
            part.at[rows_of(block, tok), pl.ds(0, width)], landing.at[rows_of(slot, tok)],
            send.at[block], recv.at[slot],
            device_id={"seq": target}, device_id_type=MESH_ID,
        )

    def sum_arrived(part, landing, send, recv, slot):
        pltpu.make_async_remote_copy(
            landing.at[rows_of(slot, tok)], landing.at[rows_of(slot, tok)],
            send.at[0], recv.at[slot], device_id={"seq": left}, device_id_type=MESH_ID,
        ).wait_recv()

    def sum_pass(part, landing, send, recv, block):
        @pl.when(is_mid)
        def _():
            sum_arrived(part, landing, send, recv, block)

            def add(i, carry):
                mine = pl.ds(pl.multiple_of(block * tok + i * 32, 32), 32)
                total = part[mine, :width].astype(F32) + landing[mine, :].astype(F32)
                part[mine, :width] = total.astype(BF16)
                return carry

            lax.fori_loop(0, tok // 32, add, 0)
            sum_send(part, landing, send, recv, block).start()

    def sum_last(part, landing, send, recv, out):
        def begin(i, carry):
            here = pl.ds(pl.multiple_of(i * 32, 32), 32)
            mine = pl.ds(pl.multiple_of(lane * tok + i * 32, 32), 32)
            out[here, :] = part[mine, :width].astype(F32)
            return carry

        lax.fori_loop(0, tok // 32, begin, 0)

        def take(slot):
            sum_arrived(part, landing, send, recv, slot)

            def add(i, carry):
                here = pl.ds(pl.multiple_of(i * 32, 32), 32)
                there = pl.ds(pl.multiple_of(slot * tok + i * 32, 32), 32)
                out[here, :] = out[here, :] + landing[there, :].astype(F32)
                return carry

            lax.fori_loop(0, tok // 32, add, 0)

        @pl.when(has_left)
        def _():
            take(lane)

        @pl.when(has_right)
        def _():
            take(jnp.int32(LANES))

    back = (pb, rb, rb_send, rb_recv)
    ahead = (wg, rf, rf_send, rf_recv)
    for copy in loads:
        copy.wait()

    def block_step(step, carry):
        block = order_of(step, lane)
        mine = rows_of(block, tok)

        def act(cols):
            gate = nn(xb[mine, :], wg[:, cols])
            up = nn(xb[mine, :], wu[:, cols])
            grad = nn(og[mine, :], wd[:, cols])
            sig = jax.nn.sigmoid(gate)
            silu = gate * sig
            hid[mine, cols] = (silu * up).astype(BF16)
            gg[mine, cols] = (grad * up * sig * (1.0 + gate * (1.0 - sig))).astype(BF16)
            gu[mine, cols] = (grad * silu).astype(BF16)

        def act_tile(t, c):
            act(pl.ds(pl.multiple_of(t * tile, tile), tile))
            return c

        lax.fori_loop(0, full_tiles, act_tile, 0)
        if tail:
            act(pl.ds(full_tiles * tile, tail))

        @pl.when(step < LANES - 1)
        def _():
            arrivals(step + 1)

        def back_tile(t, c):
            cols = pl.ds(pl.multiple_of(t * tile, tile), tile)
            pb[mine, cols] = (nt(gg[mine, :], wg[cols, :]) + nt(gu[mine, :], wu[cols, :])).astype(BF16)
            return c

        lax.fori_loop(0, width // tile, back_tile, 0)

        @pl.when(jnp.logical_and(is_end, step > 0))
        def _():
            sum_send(*back, block).start()

        return carry

    lax.fori_loop(0, LANES, block_step, 0)

    def down_step(step, carry):
        block = order_of(LANES - 1 - step, lane)
        mine = rows_of(block, tok)

        def down_tile(t, c):
            cols = pl.ds(pl.multiple_of(t * tile, tile), tile)
            wg[mine, cols] = nt(hid[mine, :], wd[cols, :]).astype(BF16)
            return c

        lax.fori_loop(0, width // tile, down_tile, 0)

        @pl.when(jnp.logical_and(is_end, step < LANES - 1))
        def _():
            sum_send(*ahead, block).start()

        return carry

    lax.fori_loop(0, 2, down_step, 0)
    mid_near, mid_far, mid_back = 3 - lane, 6 - 3 * lane, 3 * lane - 3
    sum_pass(*back, mid_near)
    lax.fori_loop(2, LANES, down_step, 0)

    def grad_tile(k, carry):
        part = pl.ds(pl.multiple_of(k * wtile, wtile), wtile)
        turned = (pl.ds(2 * wtile, wtile), pl.ds(0, LANES * tok))
        turned_og = (pl.ds(3 * wtile, wtile), pl.ds(0, LANES * tok))
        wu[turned] = xb[:, part].T
        wu[turned_og] = og[:, part].T
        copies = []
        for which, (lhs, rhs) in enumerate(((turned, gg), (turned, gu), (turned_og, hid))):
            slot = which % 2
            stage = pl.ds(slot * wtile, wtile)
            if which >= 2:
                copies[which - 2].wait()

            def tile_of(cols):
                wu[stage, cols] = nn(wu[lhs], rhs[:, cols]).astype(BF16)

            def step(t, c):
                tile_of(pl.ds(pl.multiple_of(t * tile, tile), tile))
                return c

            lax.fori_loop(0, full_tiles, step, 0)
            if tail:
                tile_of(pl.ds(full_tiles * tile, tail))
            copy = pltpu.make_async_copy(wu.at[stage], gw_hbm.at[which, part], out_sem.at[which])
            copy.start()
            copies.append(copy)
        copies[1].wait()
        copies[2].wait()
        return carry

    wtiles = width // wtile
    lax.fori_loop(0, 1, grad_tile, 0)
    sum_pass(*back, mid_far)
    lax.fori_loop(1, wtiles - 1, grad_tile, 0)
    sum_pass(*back, mid_back)
    lax.fori_loop(wtiles - 1, wtiles, grad_tile, 0)
    sum_pass(*ahead, mid_far)
    sum_last(*back, gm_ref)
    sum_pass(*ahead, mid_back)
    sum_pass(*ahead, mid_near)
    sum_last(*ahead, mo_ref)

    for block in range(LANES):
        @pl.when(jnp.logical_and(has_right, block <= lane))
        def _(block=block):
            gather_copy(block, 0).wait_send()

        @pl.when(jnp.logical_and(has_left, block >= lane))
        def _(block=block):
            gather_copy(block, 1).wait_send()

        @pl.when(block != lane)
        def _(block=block):
            sum_send(*back, block).wait_send()
            sum_send(*ahead, block).wait_send()


def feed_forward(mlp_local, grad_rows, gate_full, up_full, down_full):
    tok, width = mlp_local.shape
    units = gate_full.shape[1]
    row = tok * LANES
    anywhere = pl.BlockSpec(memory_space=pl.ANY)
    vmem = pl.BlockSpec(memory_space=pltpu.VMEM)
    dma = pltpu.SemaphoreType.DMA
    return pl.pallas_call(
        ff_kernel,
        out_shape=(
            jax.ShapeDtypeStruct((tok, width), F32),
            jax.ShapeDtypeStruct((tok, width), F32),
            jax.ShapeDtypeStruct((3, width, units), BF16),
        ),
        in_specs=[anywhere] * 5,
        out_specs=(vmem, vmem, anywhere),
        scratch_shapes=[
            pltpu.VMEM((row, width), BF16),
            pltpu.VMEM((row, width), BF16),
            pltpu.VMEM((width, units), BF16),
            pltpu.VMEM((width, units), BF16),
            pltpu.VMEM((width, units), BF16),
            pltpu.VMEM((row, units), BF16),
            pltpu.VMEM((row, units), BF16),
            pltpu.VMEM((row, units), BF16),
            pltpu.VMEM((row, width), BF16),
            pltpu.VMEM((row + tok, width), BF16),
            pltpu.VMEM((row + tok, width), BF16),
            dma((5,)),
            dma((2, LANES)),
            dma((LANES,)),
            dma((LANES,)),
            dma((LANES + 1,)),
            dma((LANES,)),
            dma((LANES + 1,)),
            dma((3,)),
        ],
        compiler_params=pltpu.CompilerParams(
            collective_id=3, has_side_effects=True, vmem_limit_bytes=60 * 2**20
        ),
        cost_estimate=pl.CostEstimate(
            flops=18 * row * width * units, bytes_accessed=12 * width * units, transcendentals=row * units
        ),
        name="feed_forward",
    )(mlp_local, grad_rows, gate_full, up_full, down_full)


def body(
    hidden_in,
    segment_ids,
    position_ids,
    out_grad,
    attn_norm,
    w_query,
    w_key,
    w_value,
    b_query,
    b_key,
    b_value,
    w_out,
    mlp_norm,
    w_gate,
    w_up,
    w_down,
):
    lane_count = lax.axis_size("seq")
    local_tok = hidden_in.shape[0]
    row_len = local_tok * lane_count
    heads_lane = HEADS // lane_count
    kv_group = lane_count // KV_HEADS
    query_width = heads_lane * HD
    scale = HD ** (-0.5)
    gathered = (
        lax.all_gather(w_query, "dp", axis=0, tiled=True),
        lax.all_gather(w_key, "dp", axis=0, tiled=True),
        lax.all_gather(w_value, "dp", axis=0, tiled=True),
        lax.all_gather(w_out, "dp", axis=1, tiled=True),
        lax.all_gather(b_query, "dp", axis=0, tiled=True),
        lax.all_gather(b_key, "dp", axis=0, tiled=True),
        lax.all_gather(b_value, "dp", axis=0, tiled=True),
        lax.all_gather(attn_norm, "dp", axis=0, tiled=True),
        lax.all_gather(mlp_norm, "dp", axis=0, tiled=True),
    )
    (
        query_full,
        key_full,
        value_full,
        out_full,
        query_bias,
        key_bias,
        value_bias,
        attn_gain,
        mlp_gain,
    ) = gathered
    attn_gain = attn_gain.astype(jnp.float32)
    mlp_gain = mlp_gain.astype(jnp.float32)
    input_f32 = hidden_in.astype(jnp.float32)
    factor_one = norm_factor(input_f32)
    normed = (input_f32 * factor_one * attn_gain).astype(jnp.bfloat16)
    query_pre = jnp.dot(normed, query_full, preferred_element_type=jnp.float32) + query_bias.astype(
        jnp.float32
    )
    key_pre = jnp.dot(normed, key_full, preferred_element_type=jnp.float32) + key_bias.astype(
        jnp.float32
    )
    value_pre = jnp.dot(normed, value_full, preferred_element_type=jnp.float32) + value_bias.astype(
        jnp.float32
    )
    cosine_tab, sine_tab = rope_tables(position_ids, HD)
    query_rot = rotate(query_pre.reshape(local_tok, HEADS, HD), cosine_tab, sine_tab).astype(
        jnp.bfloat16
    )
    key_rot = rotate(key_pre.reshape(local_tok, KV_HEADS, HD), cosine_tab, sine_tab).astype(
        jnp.bfloat16
    )
    value_low = value_pre.reshape(local_tok, KV_HEADS, HD).astype(jnp.bfloat16)
    key_lanes = jnp.repeat(key_rot, kv_group, axis=1)
    value_lanes = jnp.repeat(value_low, kv_group, axis=1)
    outgoing = jnp.concatenate(
        [query_rot.reshape(local_tok, lane_count, query_width), key_lanes, value_lanes], axis=-1
    )
    seg_copies = jnp.broadcast_to(
        segment_ids.astype(jnp.bfloat16)[:, None], (local_tok, lane_count)
    )
    incoming, seg_incoming = (
        lax.all_to_all(outgoing, "seq", split_axis=1, concat_axis=0, tiled=True),
        lax.all_to_all(seg_copies, "seq", split_axis=1, concat_axis=0, tiled=True),
    )
    head_query = incoming[:, 0, :query_width].reshape(row_len, heads_lane, HD)
    head_key = incoming[:, 0, query_width : query_width + HD]
    head_value = incoming[:, 0, query_width + HD :]
    seg_all = seg_incoming[:, 0]
    block_rows = min(512, row_len)
    block_count = row_len // block_rows
    starts = jnp.arange(block_count, dtype=jnp.int32) * block_rows
    query_blocks = head_query.reshape(block_count, block_rows, heads_lane, HD)
    seg_blocks = seg_all.reshape(block_count, block_rows)

    def forward_block(items):
        query_block, seg_block, start = items
        scores = masked_scores(query_block, head_key, seg_block, seg_all, start, scale)
        peak = jnp.max(scores, axis=-1, keepdims=True)
        exp_scores = jnp.exp(scores - peak)
        totals = jnp.sum(exp_scores, axis=-1, keepdims=True)
        attn_prob = (exp_scores / totals).astype(jnp.bfloat16)
        out_block = jnp.einsum(
            "hqk,kd->qhd", attn_prob, head_value, preferred_element_type=jnp.float32
        ).astype(jnp.bfloat16)
        return (out_block, (peak + jnp.log(totals))[..., 0])

    out_blocks, log_sums = lax.map(forward_block, (query_blocks, seg_blocks, starts))
    attended_heads = out_blocks.reshape(row_len, 1, query_width)
    attended = lax.all_to_all(
        attended_heads, "seq", split_axis=0, concat_axis=1, tiled=True
    ).reshape(local_tok, HEADS * HD)
    resid = input_f32 + jnp.dot(attended, out_full, preferred_element_type=jnp.float32)
    factor_two = norm_factor(resid)
    mlp_local = (resid * factor_two * mlp_gain).astype(jnp.bfloat16)
    grad_rows = lax.all_gather(out_grad, "seq", axis=0, tiled=True)
    gate_full, up_full, down_full = (
        lax.all_gather(w_gate, "dp", axis=0, tiled=True),
        lax.all_gather(w_up, "dp", axis=0, tiled=True),
        lax.all_gather(w_down, "dp", axis=0, tiled=True),
    )
    mlp_out, grad_mlp_in, mlp_grads = feed_forward(
        mlp_local, grad_rows, gate_full, up_full, down_full
    )
    block_out = (resid + mlp_out).astype(jnp.bfloat16)
    gate_grad, up_grad, down_grad = (
        lax.psum_scatter(mlp_grads[k], "dp", scatter_dimension=0, tiled=True).astype(jnp.float32)
        for k in range(3)
    )
    mlp_gain_part = jnp.sum(grad_mlp_in * resid * factor_two, axis=0)
    grad_resid = out_grad.astype(jnp.float32) + norm_back(grad_mlp_in, resid, factor_two, mlp_gain)
    grad_resid_low = grad_resid.astype(jnp.bfloat16)
    out_grad_part = contract_rows(attended, grad_resid_low)
    grad_attended = contract_cols(grad_resid_low, out_full).astype(jnp.bfloat16)
    grad_heads = lax.all_to_all(
        grad_attended.reshape(local_tok, lane_count, query_width),
        "seq",
        split_axis=1,
        concat_axis=0,
        tiled=True,
    )
    grad_blocks = grad_heads.reshape(block_count, block_rows, heads_lane, HD)

    def backward_block(carry, items):
        key_acc, value_acc = carry
        query_block, grad_block, seg_block, start, log_block = items
        scores = masked_scores(query_block, head_key, seg_block, seg_all, start, scale)
        attn_prob = jnp.exp(scores - log_block[..., None])
        prob_low = attn_prob.astype(jnp.bfloat16)
        grad_prob = jnp.einsum(
            "qhd,kd->hqk", grad_block, head_value, preferred_element_type=jnp.float32
        )
        inner = jnp.sum(attn_prob * grad_prob, axis=-1, keepdims=True)
        grad_scores = (attn_prob * (grad_prob - inner)).astype(jnp.bfloat16)
        grad_query = (
            jnp.einsum("hqk,kd->qhd", grad_scores, head_key, preferred_element_type=jnp.float32)
            * scale
        ).astype(jnp.bfloat16)
        key_acc = (
            key_acc
            + jnp.einsum(
                "hqk,qhd->kd", grad_scores, query_block, preferred_element_type=jnp.float32
            )
            * scale
        )
        value_acc = value_acc + jnp.einsum(
            "hqk,qhd->kd", prob_low, grad_block, preferred_element_type=jnp.float32
        )
        return ((key_acc, value_acc), grad_query)

    zero_lane = jnp.zeros((row_len, HD), jnp.float32)
    (key_acc, value_acc), grad_query_blocks = lax.scan(
        backward_block,
        (zero_lane, zero_lane),
        (query_blocks, grad_blocks, seg_blocks, starts, log_sums),
    )
    returning = jnp.concatenate(
        [
            grad_query_blocks.reshape(row_len, query_width),
            key_acc.astype(jnp.bfloat16),
            value_acc.astype(jnp.bfloat16),
        ],
        axis=-1,
    )
    arriving = lax.all_to_all(
        returning.reshape(row_len, 1, query_width + 2 * HD),
        "seq",
        split_axis=0,
        concat_axis=1,
        tiled=True,
    )
    grad_query_rot = arriving[:, :, :query_width].reshape(local_tok, HEADS, HD).astype(jnp.float32)
    grad_key_sum = (
        arriving[:, :, query_width : query_width + HD]
        .astype(jnp.float32)
        .reshape(local_tok, KV_HEADS, kv_group, HD)
        .sum(axis=2)
    )
    grad_value_sum = (
        arriving[:, :, query_width + HD :]
        .astype(jnp.float32)
        .reshape(local_tok, KV_HEADS, kv_group, HD)
        .sum(axis=2)
    )
    grad_query_pre = (
        rotate_back(grad_query_rot, cosine_tab, sine_tab)
        .reshape(local_tok, HEADS * HD)
        .astype(jnp.bfloat16)
    )
    grad_key_pre = (
        rotate_back(grad_key_sum, cosine_tab, sine_tab)
        .reshape(local_tok, KV_HEADS * HD)
        .astype(jnp.bfloat16)
    )
    grad_value_pre = grad_value_sum.reshape(local_tok, KV_HEADS * HD).astype(jnp.bfloat16)
    grad_normed = (
        contract_cols(grad_query_pre, query_full)
        + contract_cols(grad_key_pre, key_full)
        + contract_cols(grad_value_pre, value_full)
    )
    attn_gain_part = jnp.sum(grad_normed * input_f32 * factor_one, axis=0)
    input_grad = grad_resid + norm_back(grad_normed, input_f32, factor_one, attn_gain)
    query_grad = contract_rows(normed, grad_query_pre)
    key_grad = contract_rows(normed, grad_key_pre)
    value_grad = contract_rows(normed, grad_value_pre)
    query_bias_grad = jnp.sum(grad_query_pre.astype(jnp.float32), axis=0)
    key_bias_grad = jnp.sum(grad_key_pre.astype(jnp.float32), axis=0)
    value_bias_grad = jnp.sum(grad_value_pre.astype(jnp.float32), axis=0)
    local_terms = (
        query_grad,
        key_grad,
        value_grad,
        out_grad_part,
        query_bias_grad,
        key_bias_grad,
        value_bias_grad,
        attn_gain_part,
        mlp_gain_part,
    )
    partials = lax.psum(
        (
            local_terms[0],
            local_terms[1],
            local_terms[2],
            local_terms[3],
            local_terms[4],
            local_terms[5],
            local_terms[6],
            local_terms[7],
            local_terms[8],
        ),
        "seq",
    )
    return (
        block_out,
        input_grad,
        lax.psum_scatter(partials[7], "dp", scatter_dimension=0, tiled=True),
        lax.psum_scatter(partials[0], "dp", scatter_dimension=0, tiled=True),
        lax.psum_scatter(partials[1], "dp", scatter_dimension=0, tiled=True),
        lax.psum_scatter(partials[2], "dp", scatter_dimension=0, tiled=True),
        lax.psum_scatter(partials[4], "dp", scatter_dimension=0, tiled=True),
        lax.psum_scatter(partials[5], "dp", scatter_dimension=0, tiled=True),
        lax.psum_scatter(partials[6], "dp", scatter_dimension=0, tiled=True),
        lax.psum_scatter(partials[3], "dp", scatter_dimension=1, tiled=True),
        lax.psum_scatter(partials[8], "dp", scatter_dimension=0, tiled=True),
        gate_grad,
        up_grad,
        down_grad,
    )


def solution(mesh):
    return jax.shard_map(
        body,
        mesh=mesh,
        in_specs=(
            P(("dp", "seq"), None),
            P(("dp", "seq")),
            P(("dp", "seq")),
            P(("dp", "seq"), None),
            P("dp"),
            P("dp", None),
            P("dp", None),
            P("dp", None),
            P("dp"),
            P("dp"),
            P("dp"),
            P(None, "dp"),
            P("dp"),
            P("dp", "seq"),
            P("dp", "seq"),
            P("dp", "seq"),
        ),
        out_specs=(
            P(("dp", "seq"), None),
            P(("dp", "seq"), None),
            P("dp"),
            P("dp", None),
            P("dp", None),
            P("dp", None),
            P("dp"),
            P("dp"),
            P("dp"),
            P(None, "dp"),
            P("dp"),
            P("dp", "seq"),
            P("dp", "seq"),
            P("dp", "seq"),
        ),
        check_vma=False,
    )
```

```python
import functools

import jax
import jax.numpy as jnp
import numpy as np
from jax import lax
from jax.experimental import pallas as pl
from jax.experimental.pallas import tpu as pltpu
from jax.sharding import PartitionSpec as P

HEADS = 12
KV_HEADS = 2
HD = 128
EPS = 1e-06
ROPE_BASE = 1000000.0
NEG_FILL = -1e30
MESH_ID = pl.DeviceIdType.MESH
LANES = 4
BF16 = jnp.bfloat16
F32 = jnp.float32


def nn(left, right):
    return jnp.dot(left, right, preferred_element_type=F32)


def nt(left, right):
    return lax.dot_general(left, right, (((1,), (1,)), ((), ())), preferred_element_type=F32)


def rows_of(index, size):
    return pl.ds(pl.multiple_of(index * size, size), size)


def digit(codes, lane):
    return lax.rem(lax.shift_right_logical(jnp.int32(codes), 2 * lane), 4)


def order_of(step, lane):
    tables = ((0, 1, 2, 3), (1, 0, 2, 3), (2, 3, 1, 0), (3, 2, 1, 0))
    codes = [sum(tables[k][i] * 4**k for k in range(LANES)) for i in range(LANES)]
    out = digit(codes[0], lane)
    for i in range(1, LANES):
        out = jnp.where(step == i, digit(codes[i], lane), out)
    return out


def flipped(chip, mask):
    out = chip
    for bit in range(8):
        if mask >> bit & 1:
            out = out + (1 - 2 * lax.rem(chip // 2**bit, 2)) * 2**bit
    return out


def meet_all(chips):
    dp, lane = lax.axis_index("dp"), lax.axis_index("seq")
    chip, core = dp // 2, lax.rem(dp, 2)
    barrier = pltpu.get_barrier_semaphore()
    for mask in range(1, chips):
        pl.semaphore_signal(
            barrier, 1, device_id={"dp": 2 * flipped(chip, mask) + core}, device_id_type=MESH_ID
        )
    pl.semaphore_signal(barrier, 1, device_id={"dp": 2 * chip + 1 - core}, device_id_type=MESH_ID)
    for step in range(1, LANES):
        pl.semaphore_signal(
            barrier, 1, device_id={"seq": lax.rem(lane + step, LANES)}, device_id_type=MESH_ID
        )
    pl.semaphore_wait(barrier, chips + LANES - 1)


class Gather:
    def __init__(self, chips, shard, full, send, fwd, recv, half_send, half_recv, halves=True):
        self.dp = lax.axis_index("dp")
        self.chip, self.core = self.dp // 2, lax.rem(self.dp, 2)
        self.chips, self.shard, self.full = chips, shard, full
        self.send, self.fwd, self.recv = send, fwd, recv
        self.half_send, self.half_recv = half_send, half_recv
        self.rows = shard.shape[0]
        self.square = chips == 4 and halves
        self.masks = (1, 2) if self.square else tuple(range(1, chips))

    def device(self, mask, other=False):
        return 2 * flipped(self.chip, mask) + (1 - self.core if other else self.core)

    def to(self, src, dst, send, recv, target):
        return pltpu.make_async_remote_copy(
            src, dst, send, recv, device_id={"dp": target}, device_id_type=MESH_ID
        )

    def own_copy(self, mask):
        return self.to(
            self.shard, self.full.at[rows_of(self.dp, self.rows)], self.send.at[mask],
            self.recv.at[self.dp], self.device(mask) if mask else self.device(0, True),
        )

    def hand_on(self, source):
        part = self.full.at[rows_of(source, self.rows)]
        return self.to(part, part, self.fwd.at[source // 2], self.recv.at[source], self.device(0, True))

    def half_copy(self, source, half, target):
        size = self.rows // 2
        part = self.full.at[rows_of(2 * source + half, size)]
        return self.to(part, part, self.half_send.at[half], self.half_recv.at[half], target)

    def begin(self):
        for mask in self.masks + (0,):
            self.own_copy(mask).start()

    def relay(self):
        for mask in self.masks:
            source = self.device(mask)
            self.hand_on(source).wait_recv()
            if self.square:
                self.half_copy(source, mask - 1, self.device(3 - mask)).start()
            self.hand_on(source).start()

    def relay_across(self):
        if self.square:
            source = self.device(3)
            for half in range(2):
                self.half_copy(source, half, self.device(1)).wait_recv()
            self.hand_on(source).start()

    def end(self):
        for mask in range(self.chips):
            self.hand_on(self.device(mask, True)).wait_recv()
        for mask in self.masks + (0,):
            self.own_copy(mask).wait_send()
        for mask in range(1, self.chips):
            self.hand_on(self.device(mask)).wait_send()
        if self.square:
            for half in range(2):
                self.half_copy(self.device(half + 1), half, self.device(2 - half)).wait_send()


def spread(out, shards, devices, first, size, count):
    width = out.shape[1]
    column = lax.broadcasted_iota(jnp.int32, (HD, width), 1)
    value = lax.broadcasted_iota(jnp.int32, (HD, width), 0)
    owner = lax.broadcasted_iota(jnp.int32, (devices, width), 1) // size
    mine = owner == lax.broadcasted_iota(jnp.int32, (devices, width), 0)
    for n in range(count):
        total = jnp.zeros((devices, width), F32)
        for part in range(2 if size > HD else 1):
            place = (lax.rem(column, size) == value + part * HD).astype(F32).astype(BF16)
            row = 2 * (first + n) + part
            rows = jnp.concatenate([shards[k * 16 : k * 16 + 16, :][row : row + 1] for k in range(devices)], axis=0)
            total = total + nn(rows, place)
        out[first + n : first + n + 1, :] = jnp.sum(jnp.where(mine, total, 0.0), axis=0, keepdims=True)


def front_kernel(
    chips,
    x_hbm, ids_hbm, freq_ref, og_hbm, vec_hbm, wq_hbm, wk_hbm, wv_hbm, wo_hbm, wg_hbm, wu_hbm, wd_hbm,
    resid_ref, mlp_ref, vecs_ref, qkv_ref, att_ref, lse_ref, cos_ref, sin_ref, segc_ref, segr_ref,
    nrm_hbm, ogf, vecf, wqkvf, wof, wgf, wuf, wdf,
    xb, ids, nrm, wqkv, wo, vecb, ab, own_vec, own_qkv, own_wo, own_gate, own_up, own_down, own_og,
    load_sem, dp_send, dp_fwd, dp_recv, half_send, half_recv, x_send, x_recv, i_send, i_recv, o_send, o_recv, a_send, a_recv,
):
    dp, lane = lax.axis_index("dp"), lax.axis_index("seq")
    chip, core = dp // 2, lax.rem(dp, 2)
    sibling = 2 * chip + 1 - core
    tok, width = x_hbm.shape
    heads = qkv_ref.shape[1] // HD - 2
    has_left, has_right = lane > 0, lane < LANES - 1
    left, right = jnp.maximum(lane - 1, 0), jnp.minimum(lane + 1, LANES - 1)
    here = rows_of(lane, tok)

    first_loads = [
        pltpu.make_async_copy(x_hbm, xb.at[here], load_sem.at[0]),
        pltpu.make_async_copy(ids_hbm, ids.at[lane], load_sem.at[1]),
        pltpu.make_async_copy(og_hbm, own_og, load_sem.at[2]),
    ]
    shards = (vec_hbm, own_qkv, wo_hbm, wg_hbm, wu_hbm, wd_hbm)
    fulls = (vecf, wqkvf, wof, wgf, wuf, wdf)
    own_parts = (own_vec, own_qkv, own_wo, own_gate, own_up, own_down)
    own_loads = [
        pltpu.make_async_copy(s, v, load_sem.at[3 + k])
        for k, (s, v) in enumerate(zip(shards, own_parts))
        if k != 1
    ]
    kv_at = pl.multiple_of(lane * KV_HEADS // LANES * HD, HD)
    qkv_loads = [
        pltpu.make_async_copy(
            wq_hbm.at[:, pl.ds(pl.multiple_of(lane * heads * HD, HD), heads * HD)],
            own_qkv.at[:, pl.ds(0, heads * HD)], load_sem.at[4],
        ),
        pltpu.make_async_copy(
            wk_hbm.at[:, pl.ds(kv_at, HD)], own_qkv.at[:, pl.ds(heads * HD, HD)], load_sem.at[13]
        ),
        pltpu.make_async_copy(
            wv_hbm.at[:, pl.ds(kv_at, HD)], own_qkv.at[:, pl.ds((heads + 1) * HD, HD)], load_sem.at[14]
        ),
    ]
    own_copies = [
        pltpu.make_async_copy(v, f.at[rows_of(dp, v.shape[0])], load_sem.at[3 + k])
        for k, (v, f) in enumerate(zip(own_parts, fulls))
    ]
    og_copy = pltpu.make_async_copy(own_og, ogf.at[here], load_sem.at[2])
    for copy in qkv_loads + first_loads + own_loads:
        copy.start()
    lse_ref[...] = jnp.zeros_like(lse_ref)
    meet_all(chips)

    gathers = [
        Gather(
            chips, shard, full, dp_send.at[k], dp_fwd.at[k], dp_recv.at[k], half_send.at[k], half_recv.at[k], k > 0
        )
        for k, (shard, full) in enumerate(zip(shards, fulls))
    ]

    def line_copy(buf, send, recv, block, way):
        part = buf(block)
        return pltpu.make_async_remote_copy(
            part, part, send.at[way, block], recv.at[block],
            device_id={"seq": right if way == 0 else left}, device_id_type=MESH_ID,
        )

    x_line = (lambda b: xb.at[rows_of(b, tok)], x_send, x_recv)
    i_line = (lambda b: ids.at[b], i_send, i_recv)
    o_line = (lambda b: ogf.at[rows_of(b, tok)], o_send, o_recv)

    def line_begin(*lines):
        @pl.when(has_right)
        def _():
            for line in lines:
                line_copy(*line, lane, 0).start()

        @pl.when(has_left)
        def _():
            for line in lines:
                line_copy(*line, lane, 1).start()

    def line_step(step, *lines):
        @pl.when(lane - step >= 0)
        def _():
            block = jnp.maximum(lane - step, 0)
            for line in lines:
                line_copy(*line, block, 0).wait_recv()

            @pl.when(has_right)
            def _():
                for line in lines:
                    line_copy(*line, block, 0).start()

        @pl.when(lane + step < LANES)
        def _():
            block = jnp.minimum(lane + step, LANES - 1)
            for line in lines:
                line_copy(*line, block, 1).wait_recv()

            @pl.when(has_left)
            def _():
                for line in lines:
                    line_copy(*line, block, 1).start()

    def line_end(*lines):
        for block in range(LANES):
            @pl.when(jnp.logical_and(has_right, block <= lane))
            def _(block=block):
                for line in lines:
                    line_copy(*line, block, 0).wait_send()

            @pl.when(jnp.logical_and(has_left, block >= lane))
            def _(block=block):
                for line in lines:
                    line_copy(*line, block, 1).wait_send()

    with jax.named_scope("first_sends"):
        gathers[0].begin()
        for copy in qkv_loads:
            copy.wait()
        gathers[1].begin()
    first_loads[0].wait()
    first_loads[1].wait()
    line_begin(i_line, x_line)
    for load in own_loads:
        load.wait()
    for copy in own_copies:
        copy.start()
    first_loads[2].wait()
    og_copy.start()
    with jax.named_scope("first_relay"):
        gathers[0].relay()
        gathers[1].relay()
    gathers[2].begin()
    gathers[3].begin()
    with jax.named_scope("first_end"):
        gathers[1].relay_across()
        for copy in own_copies + [og_copy]:
            copy.wait()
        gathers[0].end()
        gathers[1].end()
    vec_load = pltpu.make_async_copy(vecf, vecb, load_sem.at[9])
    wqkv_load = pltpu.make_async_copy(wqkvf, wqkv, load_sem.at[10])
    vec_load.start()
    wqkv_load.start()
    vec_load.wait()
    devices = 2 * chips
    spread(vecs_ref, vecb, devices, 0, width // devices, 3)
    spread(vecs_ref, vecb, devices, 3, KV_HEADS * HD // devices, 2)
    wqkv_load.wait()
    bias = jnp.concatenate(
        [
            vecs_ref[2:3, pl.ds(pl.multiple_of(lane * heads * HD, HD), heads * HD)],
            vecs_ref[3:4, pl.ds(pl.multiple_of(lane * KV_HEADS // LANES * HD, HD), HD)],
            vecs_ref[4:5, pl.ds(pl.multiple_of(lane * KV_HEADS // LANES * HD, HD), HD)],
        ],
        axis=1,
    )
    lane_sign = jnp.where(lax.broadcasted_iota(jnp.int32, (1, HD), 1) < HD // 2, -1.0, 1.0)

    def block_step(step, carry):
        block = order_of(step, lane)
        mine = rows_of(block, tok)
        id_rows = ids[block].astype(F32)
        segr_ref[:, mine] = jnp.broadcast_to(id_rows[1:2, :], (8, tok))
        segc_ref[mine, :] = jnp.broadcast_to(id_rows[1:2, :], (HD, tok)).T
        angles = jnp.broadcast_to(id_rows[0:1, :], (HD, tok)).T * freq_ref[0:1, :]
        cos_ref[mine, :] = jnp.cos(angles)
        sin_ref[mine, :] = jnp.sin(angles) * lane_sign

        def norm(i, c):
            some = pl.ds(pl.multiple_of(block * tok + i * 32, 32), 32)
            x = xb[some, :].astype(F32)
            factor = lax.rsqrt(jnp.mean(x * x, axis=-1, keepdims=True) + EPS)
            nrm[some, :] = (x * factor * vecs_ref[0:1, :]).astype(BF16)
            return c

        lax.fori_loop(0, tok // 32, norm, 0)

        @pl.when(step < LANES - 1)
        def _():
            with jax.named_scope("row_arrival"):
                @pl.when(step == LANES - 2)
                def _():
                    line_begin(o_line)

                line_step(step + 1, i_line, x_line)

        @pl.when(step == 1)
        def _():
            with jax.named_scope("w_out_relay"):
                gathers[2].relay()
            gathers[4].begin()

        pre = nn(nrm[mine, :], wqkv[...]) + bias
        cosine, sine = cos_ref[mine, :], sin_ref[mine, :]
        for h in range(heads + 1):
            cols = slice(h * HD, (h + 1) * HD)
            part = pre[:, cols]
            qkv_ref[mine, cols] = (part * cosine + pltpu.roll(part, HD // 2, 1) * sine).astype(BF16)
        cols = slice((heads + 1) * HD, (heads + 2) * HD)
        qkv_ref[mine, cols] = pre[:, cols].astype(BF16)
        return carry

    lax.fori_loop(0, LANES, block_step, 0)
    nrm_copy = pltpu.make_async_copy(nrm, nrm_hbm, load_sem.at[11])
    nrm_copy.start()
    with jax.named_scope("w_out_across"):
        gathers[2].relay_across()
    with jax.named_scope("gate_relay"):
        gathers[3].relay()
    gathers[5].begin()

    def att_send(i):
        cols = pl.ds(pl.multiple_of(lane * heads * HD, HD), heads * HD)
        return pltpu.make_async_remote_copy(
            ab.at[pl.ds(i * tok, tok)], att_ref.at[:, cols], a_send.at[i], a_recv.at[lane],
            device_id={"seq": i}, device_id_type=MESH_ID,
        )

    sub = 128
    for i in (3, 0, 2, 1):
        keys = (i + 1) * tok

        def att_step(t, carry, i=i, keys=keys):
            h = t // (tok // sub)
            start = i * tok + lax.rem(t, tok // sub) * sub
            some = pl.ds(pl.multiple_of(start, sub), sub)
            cols = pl.ds(pl.multiple_of(h * HD, HD), HD)
            scores = nt(qkv_ref[some, cols], qkv_ref[0:keys, heads * HD : (heads + 1) * HD]) * HD**-0.5
            same = segc_ref[some, 0:1] == segr_ref[0:1, 0:keys]
            behind = (
                lax.broadcasted_iota(jnp.int32, (sub, keys), 0) + start
                >= lax.broadcasted_iota(jnp.int32, (sub, keys), 1)
            )
            scores = jnp.where(jnp.logical_and(same, behind), scores, NEG_FILL)
            peak = jnp.max(scores, axis=-1, keepdims=True)
            exps = jnp.exp(scores - peak)
            totals = jnp.sum(exps, axis=-1, keepdims=True)
            prob = (exps * (1.0 / totals)).astype(BF16)
            ab[some, cols] = nn(prob, qkv_ref[0:keys, (heads + 1) * HD :]).astype(BF16)
            at_head = lax.broadcasted_iota(jnp.int32, (sub, HD), 1) == h
            lse_ref[some, :] = jnp.where(at_head, peak + jnp.log(totals), lse_ref[some, :])
            return carry

        with jax.named_scope("attention"):
            lax.fori_loop(0, heads * (tok // sub), att_step, 0)

        @pl.when(lane != i)
        def _(i=i):
            att_send(i).start()

    with jax.named_scope("cotangent_1"):
        line_step(1, o_line)
    own_cols = pl.ds(pl.multiple_of(lane * heads * HD, HD), heads * HD)
    att_ref[:, own_cols] = ab[here, :]
    with jax.named_scope("gate_across"):
        gathers[3].relay_across()
    with jax.named_scope("w_out_end"):
        gathers[2].end()
    wo_load = pltpu.make_async_copy(wof, wo, load_sem.at[12])
    wo_load.start()
    wo_load.wait()
    for i in range(LANES):
        @pl.when(lane != i)
        def _(i=i):
            pltpu.make_async_remote_copy(
                ab.at[pl.ds(0, tok)], att_ref.at[:, pl.ds(i * heads * HD, heads * HD)],
                a_send.at[0], a_recv.at[i], device_id={"seq": i}, device_id_type=MESH_ID,
            ).wait_recv()

    def out_tile(t, carry):
        cols = pl.ds(pl.multiple_of(t * 512, 512), 512)
        resid_ref[:, cols] = xb[here, cols].astype(F32) + nt(att_ref[...], wo[cols, :])
        return carry

    with jax.named_scope("out_project"):
        lax.fori_loop(0, width // 512, out_tile, 0)

    def mlp_norm(i, carry):
        some = pl.ds(pl.multiple_of(i * 32, 32), 32)
        x = resid_ref[some, :]
        factor = lax.rsqrt(jnp.mean(x * x, axis=-1, keepdims=True) + EPS)
        mlp_ref[some, :] = (x * factor * vecs_ref[1:2, :]).astype(BF16)
        return carry

    lax.fori_loop(0, tok // 32, mlp_norm, 0)
    with jax.named_scope("cotangent_2"):
        line_step(2, o_line)
    with jax.named_scope("up_down_relay"):
        gathers[4].relay()
        gathers[5].relay()
    with jax.named_scope("cotangent_3"):
        line_step(3, o_line)
    with jax.named_scope("weights_end"):
        gathers[4].relay_across()
        gathers[5].relay_across()
        for which in (3, 4, 5):
            gathers[which].end()
    nrm_copy.wait()
    line_end(i_line, x_line, o_line)
    for i in range(LANES):
        @pl.when(lane != i)
        def _(i=i):
            att_send(i).wait_send()


def front(chips, hidden_in, ids, freqs, out_grad, vec, w_query, w_key, w_value, wo, w_gate, w_up, w_down):
    tok, width = hidden_in.shape
    row = tok * LANES
    qkv_width = w_query.shape[1] // LANES + 2 * HD
    own_qkv = jax.ShapeDtypeStruct((w_query.shape[0], qkv_width), BF16)
    ff = w_gate.shape[1]
    anywhere = pl.BlockSpec(memory_space=pl.ANY)
    vmem = pl.BlockSpec(memory_space=pltpu.VMEM)
    dma = pltpu.SemaphoreType.DMA
    shape = jax.ShapeDtypeStruct
    vmem_outs = [
        shape((tok, width), F32),
        shape((tok, width), BF16),
        shape((16, width), F32),
        shape((row, qkv_width), BF16),
        shape((tok, width), BF16),
        shape((row, HD), F32),
        shape((row, HD), F32),
        shape((row, HD), F32),
        shape((row, HD), F32),
        shape((8, row), F32),
    ]
    hbm_outs = [
        shape((row, width), BF16),
        shape((row, width), BF16),
        shape((2 * chips * 16, HD), BF16),
        shape((width, qkv_width), BF16),
        shape((width, width), BF16),
        shape((width, ff), BF16),
        shape((width, ff), BF16),
        shape((width, ff), BF16),
    ]
    return pl.pallas_call(
        functools.partial(front_kernel, chips),
        out_shape=vmem_outs + hbm_outs,
        in_specs=[anywhere, anywhere, vmem] + [anywhere] * 9,
        out_specs=[vmem] * len(vmem_outs) + [anywhere] * len(hbm_outs),
        scratch_shapes=[
            pltpu.VMEM((row, width), BF16),
            pltpu.VMEM((LANES, 8, tok), jnp.int32),
            pltpu.VMEM((row, width), BF16),
            pltpu.VMEM((width, qkv_width), BF16),
            pltpu.VMEM((width, width), BF16),
            pltpu.VMEM((2 * chips * 16, HD), BF16),
            pltpu.VMEM((row, qkv_width - 2 * HD), BF16),
            *[pltpu.VMEM(part.shape, BF16) for part in (vec, own_qkv, wo, w_gate, w_up, w_down, out_grad)],
            dma((15,)),
            dma((6, chips)),
            dma((6, chips)),
            dma((6, 2 * chips)),
            dma((6, 2)),
            dma((6, 2)),
            dma((2, LANES)),
            dma((LANES,)),
            dma((2, LANES)),
            dma((LANES,)),
            dma((2, LANES)),
            dma((LANES,)),
            dma((LANES,)),
            dma((LANES,)),
        ],
        compiler_params=pltpu.CompilerParams(
            collective_id=1, has_side_effects=True, vmem_limit_bytes=56 * 2**20
        ),
        cost_estimate=pl.CostEstimate(
            flops=10 * row * width * qkv_width, bytes_accessed=12 * width * ff, transcendentals=row * width
        ),
        name="front",
    )(hidden_in, ids, freqs, out_grad, vec, w_query, w_key, w_value, wo, w_gate, w_up, w_down)


def ff_kernel(
    chips,
    x_hbm, og_hbm, wg_hbm, wu_hbm, wd_hbm, wq_hbm, wk_hbm, wv_hbm, resid_hbm, own_og_hbm, wo_hbm, vecs_ref,
    mo_ref, gm_ref, vec_ref, grl_hbm, ga_hbm, gw_hbm, fpair, fland, fmid, wqf, wkf, wvf,
    xb, og, wg, wu, wd, hid, gg, gu, pb, rb, rf,
    load_sem, ag_send, ag_recv, rb_send, rb_recv, rf_send, rf_recv, out_sem,
    dp_send, dp_fwd, dp_recv, half_send, half_recv, own_sem, fp_send, fp_recv, fk_sem, fs_send, fs_recv, fl_sem,
    p1_send, p1_recv, p2_send, p2_recv, a_send, a_recv, late_sem,
):
    lane, dp = lax.axis_index("seq"), lax.axis_index("dp")
    chip, core = dp // 2, lax.rem(dp, 2)
    tok, width = x_hbm.shape
    units = wg_hbm.shape[1]
    tile = 512
    full_tiles = units // tile
    tail = units - full_tiles * tile
    wtile = 384
    has_left, has_right = lane > 0, lane < LANES - 1
    is_end = jnp.logical_or(lane == 0, lane == LANES - 1)
    is_mid = jnp.logical_not(is_end)
    left, right = jnp.maximum(lane - 1, 0), jnp.minimum(lane + 1, LANES - 1)

    loads = [
        pltpu.make_async_copy(src, dst, load_sem.at[k])
        for k, (src, dst) in enumerate(
            ((wg_hbm, wg), (wu_hbm, wu), (wd_hbm, wd), (og_hbm, og))
        )
    ]
    own = pltpu.make_async_copy(x_hbm, xb.at[rows_of(lane, tok)], load_sem.at[4])
    own.start()
    for copy in loads:
        copy.start()

    attn_shards = ((wq_hbm, wqf), (wk_hbm, wkf), (wv_hbm, wvf))
    attn_loads, attn_own, begin = [], [], 0
    for k, (shard, full) in enumerate(attn_shards):
        kept = hid.at[pl.ds(0, shard.shape[0]), pl.ds(begin, shard.shape[1])]
        attn_loads.append(pltpu.make_async_copy(shard, kept, own_sem.at[k]))
        attn_own.append(pltpu.make_async_copy(kept, full.at[rows_of(dp, shard.shape[0])], own_sem.at[k]))
        begin += shard.shape[1]
    resid_load = pltpu.make_async_copy(resid_hbm, mo_ref, late_sem.at[0])
    resid_load.start()
    vec_ref[...] = jnp.zeros_like(vec_ref)
    for copy in attn_loads:
        copy.start()
    meet_all(chips)
    gathers = [
        Gather(
            chips, shard, full, dp_send.at[k], dp_fwd.at[k], dp_recv.at[k], half_send.at[k], half_recv.at[k]
        )
        for k, (shard, full) in enumerate(attn_shards)
    ]
    own.wait()

    def gather_copy(block, way):
        part = xb.at[rows_of(block, tok)]
        return pltpu.make_async_remote_copy(
            part, part, ag_send.at[way, block], ag_recv.at[block],
            device_id={"seq": right if way == 0 else left}, device_id_type=MESH_ID,
        )

    @pl.when(has_right)
    def _():
        gather_copy(lane, 0).start()

    @pl.when(has_left)
    def _():
        gather_copy(lane, 1).start()

    def arrivals(step):
        @pl.when(lane - step >= 0)
        def _():
            block = jnp.maximum(lane - step, 0)
            gather_copy(block, 0).wait_recv()

            @pl.when(has_right)
            def _():
                gather_copy(block, 0).start()

        @pl.when(lane + step < LANES)
        def _():
            block = jnp.minimum(lane + step, LANES - 1)
            gather_copy(block, 1).wait_recv()

            @pl.when(has_left)
            def _():
                gather_copy(block, 1).start()

    def sum_send(part, landing, send, recv, block):
        goes_left = block < lane
        target = jnp.where(goes_left, left, right)
        slot = jnp.where(jnp.logical_and(goes_left, target == block), LANES, block)
        return pltpu.make_async_remote_copy(
            part.at[rows_of(block, tok), pl.ds(0, width)], landing.at[rows_of(slot, tok)],
            send.at[block], recv.at[slot],
            device_id={"seq": target}, device_id_type=MESH_ID,
        )

    def sum_arrived(part, landing, send, recv, slot):
        pltpu.make_async_remote_copy(
            landing.at[rows_of(slot, tok)], landing.at[rows_of(slot, tok)],
            send.at[0], recv.at[slot], device_id={"seq": left}, device_id_type=MESH_ID,
        ).wait_recv()

    def sum_pass(part, landing, send, recv, block):
        @pl.when(is_mid)
        def _():
            sum_arrived(part, landing, send, recv, block)

            def add(i, carry):
                mine = pl.ds(pl.multiple_of(block * tok + i * 32, 32), 32)
                total = part[mine, :width].astype(F32) + landing[mine, :].astype(F32)
                part[mine, :width] = total.astype(BF16)
                return carry

            lax.fori_loop(0, tok // 32, add, 0)
            sum_send(part, landing, send, recv, block).start()

    def sum_last(part, landing, send, recv, out, onto=False):
        def begin(i, carry):
            here = pl.ds(pl.multiple_of(i * 32, 32), 32)
            mine = pl.ds(pl.multiple_of(lane * tok + i * 32, 32), 32)
            own_part = part[mine, :width].astype(F32)
            out[here, :] = out[here, :] + own_part if onto else own_part
            return carry

        lax.fori_loop(0, tok // 32, begin, 0)

        def take(slot):
            sum_arrived(part, landing, send, recv, slot)

            def add(i, carry):
                here = pl.ds(pl.multiple_of(i * 32, 32), 32)
                there = pl.ds(pl.multiple_of(slot * tok + i * 32, 32), 32)
                out[here, :] = out[here, :] + landing[there, :].astype(F32)
                return carry

            lax.fori_loop(0, tok // 32, add, 0)

        @pl.when(has_left)
        def _():
            take(lane)

        @pl.when(has_right)
        def _():
            take(jnp.int32(LANES))

    back = (pb, rb, rb_send, rb_recv)
    ahead = (og, rf, rf_send, rf_recv)
    for gather in gathers:
        gather.begin()
    for load, copy in zip(attn_loads, attn_own):
        load.wait()
        copy.start()
    with jax.named_scope("weights_load"):
        for copy in loads + attn_own:
            copy.wait()

    def block_step(step, carry):
        block = order_of(step, lane)
        mine = rows_of(block, tok)

        def act(cols):
            gate = nn(xb[mine, :], wg[:, cols])
            up = nn(xb[mine, :], wu[:, cols])
            grad = nn(og[mine, :], wd[:, cols])
            sig = jax.nn.sigmoid(gate)
            silu = gate * sig
            hid[mine, cols] = (silu * up).astype(BF16)
            gg[mine, cols] = (grad * up * sig * (1.0 + gate * (1.0 - sig))).astype(BF16)
            gu[mine, cols] = (grad * silu).astype(BF16)

        def act_tile(t, c):
            act(pl.ds(pl.multiple_of(t * tile, tile), tile))
            return c

        with jax.named_scope("activations"):
            lax.fori_loop(0, full_tiles, act_tile, 0)
            if tail:
                act(pl.ds(full_tiles * tile, tail))

        @pl.when(step < LANES - 1)
        def _():
            with jax.named_scope("row_arrival"):
                arrivals(step + 1)

        @pl.when(step == 1)
        def _():
            with jax.named_scope("attn_relay"):
                for gather in gathers:
                    gather.relay()

        @pl.when(step == 2)
        def _():
            with jax.named_scope("attn_across"):
                for gather in gathers:
                    gather.relay_across()

        def back_tile(t, c):
            cols = pl.ds(pl.multiple_of(t * tile, tile), tile)
            pb[mine, cols] = (nt(gg[mine, :], wg[cols, :]) + nt(gu[mine, :], wu[cols, :])).astype(BF16)
            return c

        with jax.named_scope("input_grad_part"):
            lax.fori_loop(0, width // tile, back_tile, 0)

        @pl.when(jnp.logical_and(is_end, step > 0))
        def _():
            sum_send(*back, block).start()

        return carry

    lax.fori_loop(0, LANES, block_step, 0)

    def down_step(step, carry):
        block = order_of(LANES - 1 - step, lane)
        mine = rows_of(block, tok)

        def down_tile(t, c):
            cols = pl.ds(pl.multiple_of(t * tile, tile), tile)
            og[mine, cols] = nt(hid[mine, :], wd[cols, :]).astype(BF16)
            return c

        with jax.named_scope("down_part"):
            lax.fori_loop(0, width // tile, down_tile, 0)

        @pl.when(jnp.logical_and(is_end, step < LANES - 1))
        def _():
            sum_send(*ahead, block).start()

        return carry

    wtiles = width // wtile
    part_rows = width // (2 * chips)
    tile_chips = wtile // (2 * part_rows)

    square = chips == 4
    half = part_rows // 2

    def tile_at(step):
        base, mask = chip // (chips // wtiles), wtiles - 1 - step
        return lax.rem(base + mask, 2) + 2 * lax.rem(base // 2 + mask // 2, 2)

    def held(which, c):
        return rows_of(which * chips + c, part_rows)

    def pair_send(which, c, r):
        theirs = pl.ds(pl.multiple_of(which * wtile + (2 * r + 1 - core) * part_rows, 16), part_rows)
        return pltpu.make_async_remote_copy(
            wu.at[theirs], fpair.at[which, c], fp_send.at[which, c], fp_recv.at[which, c],
            device_id={"dp": 2 * chip + 1 - core}, device_id_type=MESH_ID,
        )

    def pair_keep(which, c, r):
        mine = pl.ds(pl.multiple_of(which * wtile + (2 * r + core) * part_rows, 16), part_rows)
        return pltpu.make_async_copy(wu.at[mine], wg.at[held(which, c)], fk_sem.at[which, c])

    def to_chip(src, dst, send, recv, mask):
        return pltpu.make_async_remote_copy(
            src, dst, send, recv, device_id={"dp": 2 * flipped(chip, mask) + core}, device_id_type=MESH_ID
        )

    def chip_keep(which):
        return pltpu.make_async_copy(
            wg.at[held(which, chip)], fland.at[which, 0], fl_sem.at[which]
        )

    def chip_send(which, mask):
        return to_chip(
            wg.at[held(which, flipped(chip, mask))], fland.at[which, mask], fs_send.at[which, mask],
            fs_recv.at[which, mask], mask,
        )

    def part_of(which, mask, upper):
        return wg.at[pl.ds(pl.multiple_of((which * chips + flipped(chip, mask)) * part_rows + upper * half, 16), half)]

    def first_hop(which, mask, upper):
        if mask == 3:
            landing = fmid.at[which, upper]
        else:
            landing = fland.at[which, 1, pl.ds(upper * half, half)]
        k = 2 * (mask == 3) + upper
        return to_chip(part_of(which, mask, upper), landing, p1_send.at[which, k], p1_recv.at[which, k], 1 + upper)

    def second_hop(which, upper):
        mask = 2 - upper
        return to_chip(
            part_of(which, mask, upper), fland.at[which, 2, pl.ds(upper * half, half)],
            p2_send.at[which, upper], p2_recv.at[which, upper], mask,
        )

    def load_slot(which):
        return wu.at[pl.ds(3 * wtile + which * part_rows, part_rows)]

    def add_in(which, first, rows):
        def add(i, carry):
            mine = pl.ds(pl.multiple_of(first + i * 16, 16), 16)
            other = pl.ds(pl.multiple_of(3 * wtile + which * part_rows + i * 16, 16), 16)
            wg[mine, :] = (wg[mine, :].astype(F32) + wu[other, :].astype(F32)).astype(BF16)
            return carry

        lax.fori_loop(0, rows // 16, add, 0)

    def pass_halves(upper):
        arrived = []
        for which in range(2):
            first_hop(which, 3, upper).wait_recv()
            arrived.append(
                pltpu.make_async_copy(
                    fmid.at[which, upper], wu.at[pl.ds(3 * wtile + which * part_rows, half)], load_sem.at[which]
                )
            )
            arrived[which].start()
        for which in range(2):
            arrived[which].wait()
            c = flipped(chip, 2 - upper)
            add_in(which, (which * chips + c) * part_rows + upper * half, half)
            second_hop(which, upper).start()

    def add_pairs(step):
        k = tile_at(step)
        for r in range(tile_chips):
            c = k * tile_chips + r
            arrived = []
            for which in range(2):
                pair_keep(which, c, r).wait()
                pair_send(which, c, r).wait_recv()
                arrived.append(pltpu.make_async_copy(fpair.at[which, c], load_slot(which), load_sem.at[which]))
                arrived[which].start()
            for which in range(2):
                arrived[which].wait()
                add_in(which, (which * chips + c) * part_rows, part_rows)
                if not square:
                    continue
                if step == 0:
                    first_hop(which, 3, 0).start()
                    first_hop(which, 3, 1).start()
                elif step == 1:
                    first_hop(which, 2, 1).start()
                elif step == 2:
                    first_hop(which, 1, 0).start()
                else:
                    chip_keep(which).start()

    def product(stage_ref, stage, lhs, rhs):
        def tile_of(cols):
            stage_ref[stage, cols] = nn(wu[lhs], rhs[:, cols]).astype(BF16)

        def one(t, c):
            tile_of(pl.ds(pl.multiple_of(t * tile, tile), tile))
            return c

        lax.fori_loop(0, full_tiles, one, 0)
        if tail:
            tile_of(pl.ds(full_tiles * tile, tail))

    turned = (pl.ds(2 * wtile, wtile), pl.ds(0, LANES * tok))

    def grad_tile(step):
        k = tile_at(step)
        if step:
            for which in range(2):
                for r in range(tile_chips):
                    before = tile_at(step - 1) * tile_chips + r
                    pair_send(which, before, r).wait_send()
        wu[turned] = xb[:, rows_of(k, wtile)].T
        for which, rhs in enumerate((gg, gu)):
            product(wu, pl.ds(which * wtile, wtile), turned, rhs)
            for r in range(tile_chips):
                pair_send(which, k * tile_chips + r, r).start()
                pair_keep(which, k * tile_chips + r, r).start()

    def down_grad_out(step):
        stage = rows_of(lax.rem(step, 2), wtile)
        return pltpu.make_async_copy(
            gg.at[stage], gw_hbm.at[0, rows_of(step, wtile)], out_sem.at[lax.rem(step, 2)]
        )

    def down_grad_tile(step, carry):
        @pl.when(step > 1)
        def _():
            down_grad_out(step - 2).wait()

        wu[turned] = xb[:, rows_of(step, wtile)].T
        product(gg, rows_of(lax.rem(step, 2), wtile), turned, hid)
        down_grad_out(step).start()
        return carry

    mid_near, mid_far, mid_back = 3 - lane, 6 - 3 * lane, 3 * lane - 3
    sum_pass(*back, mid_near)
    grad_tile(0)
    lax.fori_loop(0, 1, down_step, 0)
    add_pairs(0)
    lax.fori_loop(1, LANES, down_step, 0)
    wo = wd.at[:, pl.ds(0, width)]
    wo_load = pltpu.make_async_copy(wo_hbm, wo, late_sem.at[1])
    wo_load.start()
    sum_pass(*back, mid_far)
    grad_tile(1)
    add_pairs(1)
    sum_pass(*ahead, mid_far)
    grad_tile(2)
    add_pairs(2)
    sum_pass(*back, mid_back)
    grad_tile(3)
    for block in range(LANES):
        @pl.when(jnp.logical_and(has_right, block <= lane))
        def _(block=block):
            gather_copy(block, 0).wait_send()

        @pl.when(jnp.logical_and(has_left, block >= lane))
        def _(block=block):
            gather_copy(block, 1).wait_send()

    again = pltpu.make_async_copy(og_hbm, xb, load_sem.at[3])
    again.start()
    add_pairs(3)
    sum_pass(*ahead, mid_near)
    sum_pass(*ahead, mid_back)
    if square:
        pass_halves(0)
        pass_halves(1)
    else:
        for which in range(2):
            chip_keep(which).start()
            for mask in range(1, chips):
                chip_send(which, mask).start()
    sum_last(*back, gm_ref)
    for block in range(LANES):
        @pl.when(block != lane)
        def _(block=block):
            sum_send(*back, block).wait_send()

    own_og, grl, gao = (pb.at[pl.ds(k * tok, tok)] for k in range(3))
    og_load = pltpu.make_async_copy(own_og_hbm, own_og, late_sem.at[2])
    og_load.start()
    og_load.wait()
    resid_load.wait()

    def resid_rows(i, carry):
        some = pl.ds(pl.multiple_of(i * 32, 32), 32)
        values = mo_ref[some, :]
        grad_in = gm_ref[some, :]
        factor = lax.rsqrt(jnp.mean(values * values, axis=-1, keepdims=True) + EPS)
        scaled = grad_in * vecs_ref[1:2, :]
        inner = jnp.mean(scaled * values, axis=-1, keepdims=True)
        grad = own_og[some, :].astype(F32) + (factor * scaled - values * (factor * factor * factor) * inner)
        gm_ref[some, :] = grad
        grl[some, :] = grad.astype(BF16)
        vec_ref[1:2, :] = vec_ref[1:2, :] + jnp.sum(grad_in * values * factor, axis=0, keepdims=True)
        return carry

    lax.fori_loop(0, tok // 32, resid_rows, 0)
    grl_out = pltpu.make_async_copy(grl, grl_hbm, late_sem.at[2])
    grl_out.start()
    wo_load.wait()
    hw = width // LANES

    def head_cols(which):
        return pl.ds(pl.multiple_of(which * hw, hw), hw)

    def a_copy(target):
        return pltpu.make_async_remote_copy(
            gao.at[:, head_cols(target)], ga_hbm.at[rows_of(lane, tok)], a_send.at[target], a_recv.at[lane],
            device_id={"seq": target}, device_id_type=MESH_ID,
        )

    for step in range(1, LANES + 1):
        target = lax.rem(lane + step, LANES)
        gao[:, head_cols(target)] = nn(grl[...], wo[:, head_cols(target)]).astype(BF16)
        if step < LANES:
            a_copy(target).start()
    ga_own = pltpu.make_async_copy(gao.at[:, head_cols(lane)], ga_hbm.at[rows_of(lane, tok)], late_sem.at[1])
    ga_own.start()
    again.wait()
    lax.fori_loop(0, wtiles, down_grad_tile, 0)
    sum_last(*ahead, mo_ref, True)
    grl_out.wait()
    ga_own.wait()
    for step in range(1, LANES):
        other = lax.rem(lane + step, LANES)
        a_copy(other).wait_send()
        pltpu.make_async_remote_copy(
            gao.at[:, head_cols(other)], ga_hbm.at[rows_of(other, tok)], a_send.at[0], a_recv.at[other],
            device_id={"seq": other}, device_id_type=MESH_ID,
        ).wait_recv()
    for gather in gathers:
        gather.end()
    down_grad_out(wtiles - 2).wait()
    down_grad_out(wtiles - 1).wait()
    for which in range(2):
        for r in range(tile_chips):
            last = tile_at(wtiles - 1) * tile_chips + r
            pair_send(which, last, r).wait_send()
        chip_keep(which).wait()
        if square:
            for mask, upper in ((3, 0), (3, 1), (2, 1), (1, 0)):
                first_hop(which, mask, upper).wait_send()
                if mask != 3:
                    first_hop(which, mask, upper).wait_recv()
            for upper in range(2):
                second_hop(which, upper).wait()
        else:
            for mask in range(1, chips):
                chip_send(which, mask).wait()

    for block in range(LANES):
        @pl.when(block != lane)
        def _(block=block):
            sum_send(*ahead, block).wait_send()


def feed_forward(
    chips, mlp_local, grad_rows, gate_full, up_full, down_full, w_query, w_key, w_value, resid, out_grad, wo_full, vecs
):
    tok, width = mlp_local.shape
    units = gate_full.shape[1]
    row = tok * LANES
    own = width // (2 * chips)
    anywhere = pl.BlockSpec(memory_space=pl.ANY)
    vmem = pl.BlockSpec(memory_space=pltpu.VMEM)
    dma = pltpu.SemaphoreType.DMA
    shape = jax.ShapeDtypeStruct
    return pl.pallas_call(
        functools.partial(ff_kernel, chips),
        out_shape=(
            shape((tok, width), F32),
            shape((tok, width), F32),
            shape((8, width), F32),
            shape((tok, width), BF16),
            shape((row, width // LANES), BF16),
            shape((1, width, units), BF16),
            shape((2, chips, own, units), BF16),
            shape((2, 3 if chips == 4 else chips, own, units), BF16),
            shape((2, 2, own // 2, units), BF16),
            shape((width, w_query.shape[1]), BF16),
            shape((width, w_key.shape[1]), BF16),
            shape((width, w_value.shape[1]), BF16),
        ),
        in_specs=[anywhere] * 11 + [vmem],
        out_specs=(vmem, vmem, vmem) + (anywhere,) * 9,
        scratch_shapes=[
            pltpu.VMEM((row, width), BF16),
            pltpu.VMEM((row, width), BF16),
            pltpu.VMEM((width, units), BF16),
            pltpu.VMEM((width, units), BF16),
            pltpu.VMEM((width, units), BF16),
            pltpu.VMEM((row, units), BF16),
            pltpu.VMEM((row, units), BF16),
            pltpu.VMEM((row, units), BF16),
            pltpu.VMEM((row, width), BF16),
            pltpu.VMEM((row + tok, width), BF16),
            pltpu.VMEM((row + tok, width), BF16),
            dma((5,)),
            dma((2, LANES)),
            dma((LANES,)),
            dma((LANES,)),
            dma((LANES + 1,)),
            dma((LANES,)),
            dma((LANES + 1,)),
            dma((2,)),
            dma((3, chips)),
            dma((3, chips)),
            dma((3, 2 * chips)),
            dma((3, 2)),
            dma((3, 2)),
            dma((3,)),
            *[dma((2, chips))] * 5,
            dma((2,)),
            dma((2, 4)),
            dma((2, 4)),
            dma((2, 2)),
            dma((2, 2)),
            dma((LANES,)),
            dma((LANES,)),
            dma((3,)),
        ],
        compiler_params=pltpu.CompilerParams(
            collective_id=3, has_side_effects=True, vmem_limit_bytes=60 * 2**20
        ),
        cost_estimate=pl.CostEstimate(
            flops=18 * row * width * units, bytes_accessed=12 * width * units, transcendentals=row * units
        ),
        name="feed_forward",
    )(
        mlp_local, grad_rows, gate_full, up_full, down_full, w_query, w_key, w_value, resid, out_grad, wo_full, vecs
    )


def chunked(rows, body, size=32):
    lax.fori_loop(0, rows // size, lambda i, c: (body(pl.multiple_of(i * size, size)), c)[1], 0)


def tn(left, right):
    return lax.dot_general(left, right, (((0,), (0,)), ((), ())), preferred_element_type=F32)


def back_kernel(
    chips, mats,
    gr_ref, mlp_vec_ref, x_ref, vecs_ref, qkv_ref, lse_ref, cos_ref, sin_ref, segc_ref, segr_ref,
    grl_hbm, ga_hbm, att_hbm, wq_hbm, wk_hbm, wv_hbm, nrm_hbm, gw_hbm,
    ig_ref, vec_ref, woz_ref, wqz_ref, fpair, fsum, fland,
    att, wfull, nrm, grl, ga, gk, gv, g, gl, lt,
    wop, wopair, woland, wores, zin, zsum,
    wqp, wqpair, wqland, slots, vz, vd, gn,
    load_sem, g_send, g_recv, h_send, h_recv,
    po_send, po_recv, so_send, so_recv, pq_send, pq_recv, sq_send, sq_recv,
    zr_send, zr_recv, zg_send, zg_recv, zq_send, zq_recv,
    fp_send, fp_recv, fs_send, fs_recv, slot_sem, v_send, v_recv, vs_send, vs_recv,
):
    dp, lane = lax.axis_index("dp"), lax.axis_index("seq")
    chip, core = dp // 2, lax.rem(dp, 2)
    sibling = 2 * chip + 1 - core
    tok, width = x_ref.shape
    row = tok * LANES
    part_rows = width // (2 * chips)
    heads = qkv_ref.shape[1] // HD - 2
    hw = heads * HD
    gwid = hw + 2 * HD
    here = rows_of(lane, tok)

    def lane_cols(which, size):
        return pl.ds(pl.multiple_of(which * size, size), size)

    loads = [
        pltpu.make_async_copy(src, dst, load_sem.at[k])
        for k, (src, dst) in enumerate(
            (
                (grl_hbm, grl),
                (att_hbm, att),
                (ga_hbm, ga),
                (nrm_hbm, nrm),
                (wq_hbm, wfull.at[:, pl.ds(0, LANES * hw)]),
                (wk_hbm, wfull.at[:, pl.ds(LANES * hw, KV_HEADS * HD)]),
                (wv_hbm, wfull.at[:, pl.ds(LANES * hw + KV_HEADS * HD, KV_HEADS * HD)]),
            )
        )
    ]
    for copy in loads:
        copy.start()
    vec_ref[...] = mlp_vec_ref[...]
    meet_all(chips)

    def to_dp(src, dst, send, recv, target):
        return pltpu.make_async_remote_copy(
            src, dst, send, recv, device_id={"dp": target}, device_id_type=MESH_ID
        )

    def to_lane(src, dst, send, recv, target):
        return pltpu.make_async_remote_copy(
            src, dst, send, recv, device_id={"seq": target}, device_id_type=MESH_ID
        )

    def ff_pair(k, c):
        return to_dp(
            gw_hbm.at[mats[k], rows_of(2 * c + 1 - core, part_rows)], fpair.at[k, c],
            fp_send.at[k, c], fp_recv.at[k, c], sibling,
        )

    def ff_send(k, mask):
        c = flipped(chip, mask)
        return to_dp(
            fsum.at[k, c], fland.at[k, chip], fs_send.at[k, c], fs_recv.at[k, chip], 2 * c + core
        )

    for k in range(len(mats)):
        for mask in range(chips):
            ff_pair(k, flipped(chip, mask)).start()

    def ff_loads(k, mask):
        c = flipped(chip, mask)
        return [
            pltpu.make_async_copy(
                gw_hbm.at[mats[k], rows_of(2 * c + core, part_rows)], slots.at[0], slot_sem.at[0]
            ),
            pltpu.make_async_copy(fpair.at[k, c], slots.at[1], slot_sem.at[1]),
        ]

    def ff_load(k, mask):
        ff_pair(k, flipped(chip, mask)).wait_recv()
        for copy in ff_loads(k, mask):
            copy.start()

    def ff_add(k, mask):
        for copy in ff_loads(k, mask):
            copy.wait()

        def add(start):
            some = pl.ds(start, 16)
            slots[0, some, :] = (slots[0, some, :].astype(F32) + slots[1, some, :].astype(F32)).astype(BF16)

        chunked(part_rows, add, 16)
        out = pltpu.make_async_copy(
            slots.at[0], fsum.at[k, flipped(chip, mask)] if mask else fland.at[k, chip], slot_sem.at[2]
        )
        out.start()
        out.wait()
        if mask:
            ff_send(k, mask).start()

    loads[0].wait()
    loads[1].wait()

    def out_grad_tile(i, carry):
        some = lane_cols(i, 384)
        for n in range(width // 512):
            cols = slice(n * 512, (n + 1) * 512)
            wop[some, cols] = tn(grl[:, some], att[:, cols]).astype(BF16)
        return carry

    lax.fori_loop(0, width // 384, out_grad_tile, 0)

    class Sum:
        def __init__(self, partial, pair, land, pair_send, pair_recv, send, recv):
            self.partial, self.pair, self.land = partial, pair, land
            self.pair_send, self.pair_recv, self.send, self.recv = pair_send, pair_recv, send, recv

        def pair_copy(self, c):
            return to_dp(
                self.partial.at[rows_of(2 * c + 1 - core, part_rows)], self.pair.at[rows_of(c, part_rows)],
                self.pair_send.at[c], self.pair_recv.at[c], sibling,
            )

        def send_copy(self, mask):
            c = flipped(chip, mask)
            return to_dp(
                self.partial.at[rows_of(2 * c + core, part_rows)], self.land.at[rows_of(chip, part_rows)],
                self.send.at[c], self.recv.at[chip], 2 * c + core,
            )

        def begin(self):
            for mask in range(chips):
                self.pair_copy(flipped(chip, mask)).start()

        def middle(self):
            for mask in list(range(1, chips)) + [0]:
                c = flipped(chip, mask)
                self.pair_copy(c).wait_recv()

                def add(start, c=c):
                    mine = pl.ds(pl.multiple_of((2 * c + core) * part_rows + start, 16), 16)
                    other = pl.ds(pl.multiple_of(c * part_rows + start, 16), 16)
                    self.partial[mine, :] = (
                        self.partial[mine, :].astype(F32) + self.pair[other, :].astype(F32)
                    ).astype(BF16)

                chunked(part_rows, add, 16)
                if mask:
                    self.send_copy(mask).start()

        def last(self, out):
            for mask in range(1, chips):
                c = flipped(chip, mask)
                to_dp(
                    self.land.at[rows_of(c, part_rows)], self.land.at[rows_of(c, part_rows)],
                    self.send.at[0], self.recv.at[c], sibling,
                ).wait_recv()

            def add(start):
                some = pl.ds(start, 16)
                total = self.partial[pl.ds(pl.multiple_of(dp * part_rows + start, 16), 16), :].astype(F32)
                for mask in range(1, chips):
                    c = flipped(chip, mask)
                    total = total + self.land[
                        pl.ds(pl.multiple_of(c * part_rows + start, 16), 16), :
                    ].astype(F32)
                out(some, total.astype(BF16))

            chunked(part_rows, add, 16)

        def end(self):
            for mask in range(chips):
                self.pair_copy(flipped(chip, mask)).wait_send()
                if mask:
                    self.send_copy(mask).wait_send()

    out_sum = Sum(wop, wopair, woland, po_send, po_recv, so_send, so_recv)
    qkv_sum = Sum(wqp, wqpair, wqland, pq_send, pq_recv, sq_send, sq_recv)
    out_sum.begin()

    def turn(i, carry):
        some = rows_of(i, tok)
        turned = lse_ref[some, :].T
        for h in range(heads):
            lt[h, :, some] = jnp.broadcast_to(turned[h : h + 1, :], (8, tok))
        return carry

    lax.fori_loop(0, LANES, turn, 0)
    gk[...] = jnp.zeros_like(gk)
    gv[...] = jnp.zeros_like(gv)
    out_sum.middle()
    ff_turns = [(k, mask) for k in range(len(mats)) for mask in list(range(chips - 1, 0, -1)) + [0]]
    loads[2].wait()

    def out_store(some, value):
        wores[some, :] = value

    quarter = width // LANES

    def zr_copy(target):
        return to_lane(
            wores.at[:, lane_cols(target, quarter)], zin.at[lane], zr_send.at[target], zr_recv.at[lane], target
        )

    def own_out():
        out_sum.last(out_store)
        for step in range(1, LANES):
            zr_copy(lax.rem(lane + step, LANES)).start()
        zin[lane] = wores[:, lane_cols(lane, quarter)]

    def gq_copy(target):
        return to_lane(
            g.at[rows_of(target, tok), pl.ds(0, hw)],
            gl.at[:, pl.ds(pl.multiple_of(lane * gwid, HD), hw)],
            g_send.at[target], g_recv.at[lane], target,
        )

    def gkv_copy(target):
        return to_lane(
            g.at[rows_of(target, tok), pl.ds(hw, 2 * HD)],
            gl.at[:, pl.ds(pl.multiple_of(lane * gwid + hw, HD), 2 * HD)],
            h_send.at[target], h_recv.at[lane], target,
        )

    sub = 128
    scale = HD**-0.5
    for i in (3, 0, 2, 1):
        keys = (i + 1) * tok

        def att_step(t, carry, i=i, keys=keys):
            h = t // (tok // sub)
            start = i * tok + lax.rem(t, tok // sub) * sub
            some = pl.ds(pl.multiple_of(start, sub), sub)
            cols = lane_cols(h, HD)
            key, value = qkv_ref[0:keys, hw : hw + HD], qkv_ref[0:keys, hw + HD :]
            query, grad = qkv_ref[some, cols], ga[some, cols]
            scores = nt(key, query) * scale
            same = segc_ref[0:keys, 0:1] == segr_ref[0:1, some]
            behind = (
                lax.broadcasted_iota(jnp.int32, (keys, sub), 1) + start
                >= lax.broadcasted_iota(jnp.int32, (keys, sub), 0)
            )
            scores = jnp.where(jnp.logical_and(same, behind), scores, NEG_FILL)
            prob = jnp.exp(scores - lt[h, 0:1, some])
            grad_prob = nt(value, grad)
            inner = jnp.sum(prob * grad_prob, axis=0, keepdims=True)
            grad_scores = (prob * (grad_prob - inner)).astype(BF16)
            gq = (tn(grad_scores, key) * scale).astype(BF16).astype(F32)
            gk[0:keys, :] = gk[0:keys, :] + nn(grad_scores, query)
            gv[0:keys, :] = gv[0:keys, :] + nn(prob.astype(BF16), grad)
            g[some, cols] = (
                gq * cos_ref[some, :] + pltpu.roll(gq * sin_ref[some, :], HD // 2, 1)
            ).astype(BF16)
            return carry

        lax.fori_loop(0, heads * (tok // sub), att_step, 0)

        @pl.when(lane != i)
        def _(i=i):
            gq_copy(jnp.int32(i)).start()

    def close(start):
        some = pl.ds(start, 32)
        grad = (gk[some, :] * scale).astype(BF16).astype(F32)
        g[some, hw : hw + HD] = (
            grad * cos_ref[some, :] + pltpu.roll(grad * sin_ref[some, :], HD // 2, 1)
        ).astype(BF16)
        g[some, hw + HD :] = gv[some, :].astype(BF16)

    chunked(row, close)

    for step in range(1, LANES):
        gkv_copy(lax.rem(lane + step, LANES)).start()
    gl[:, lane_cols(lane, gwid)] = g[here, :]
    loads[3].wait()

    def qkv_grad_tile(i, carry):
        some = lane_cols(i, 384)
        wqp[some, :] = tn(nrm[:, some], g[...]).astype(BF16)
        return carry

    lax.fori_loop(0, width // 384, qkv_grad_tile, 0)
    qkv_sum.begin()
    sums = jnp.zeros((1, gwid), F32)
    for i in range(row // 128):
        sums = sums + jnp.sum(g[i * 128 : (i + 1) * 128, :].astype(F32), axis=0, keepdims=True)
    kv_head = lane * KV_HEADS // LANES
    vec_ref[2:3, lane_cols(lane, hw)] = sums[:, :hw]
    vec_ref[3:4, lane_cols(kv_head, HD)] = sums[:, hw : hw + HD]
    vec_ref[4:5, lane_cols(kv_head, HD)] = sums[:, hw + HD :]

    def qkv_store(some, value):
        wqz_ref[lane, some, :] = value

    def zq_copy(target):
        return to_lane(
            wqz_ref.at[lane], wqz_ref.at[lane], zq_send.at[target], zq_recv.at[lane], target
        )

    own_out()
    qkv_sum.middle()
    for turn in ff_turns:
        ff_load(*turn)
        ff_add(*turn)
    qkv_sum.last(qkv_store)
    for step in range(1, LANES):
        zq_copy(lax.rem(lane + step, LANES)).start()
    for step in range(1, LANES):
        source = lax.rem(lane + step, LANES)
        to_lane(zin.at[source], zin.at[source], zr_send.at[0], zr_recv.at[source], source).wait_recv()
    total = zin[0].astype(F32)
    for j in range(1, LANES):
        total = total + zin[j].astype(F32)
    zsum[...] = total.astype(BF16)
    woz_ref[:, lane_cols(lane, quarter)] = zsum[...]

    def zg_copy(target):
        return to_lane(
            zsum, woz_ref.at[:, lane_cols(lane, quarter)], zg_send.at[target], zg_recv.at[lane], target
        )

    for step in range(1, LANES):
        zg_copy(lax.rem(lane + step, LANES)).start()

    for copy in loads[4:]:
        copy.wait()
    for step in range(1, LANES):
        source = lax.rem(lane + step, LANES)
        for begin, size, recv in ((0, hw, g_recv), (hw, 2 * HD, h_recv)):
            to_lane(
                g.at[here, pl.ds(begin, size)], gl.at[:, pl.ds(pl.multiple_of(source * gwid + begin, HD), size)],
                g_send.at[0], recv.at[source], source,
            ).wait_recv()
    group = LANES // KV_HEADS

    def kv_total(kv, offset):
        parts = [
            gl[:, (kv * group + j) * gwid + offset : (kv * group + j) * gwid + offset + HD].astype(F32)
            for j in range(group)
        ]
        return sum(parts[1:], parts[0]).astype(BF16)

    kv_grads = [kv_total(kv, hw + offset) for offset in (0, HD) for kv in range(KV_HEADS)]
    kv_grads = jnp.concatenate(kv_grads, axis=1)

    def normed_tile(i, carry):
        some = lane_cols(i, 512)
        total = nt(kv_grads, wfull[some, LANES * hw :])
        for j in range(LANES):
            total = total + nt(gl[:, j * gwid : j * gwid + hw], wfull[some, j * hw : (j + 1) * hw])
        gn[:, some] = total
        return carry

    lax.fori_loop(0, width // 512, normed_tile, 0)

    def input_rows(start):
        some = pl.ds(start, 32)
        values = x_ref[some, :].astype(F32)
        grad_in = gn[some, :]
        factor = lax.rsqrt(jnp.mean(values * values, axis=-1, keepdims=True) + EPS)
        scaled = grad_in * vecs_ref[0:1, :]
        inner = jnp.mean(scaled * values, axis=-1, keepdims=True)
        ig_ref[some, :] = gr_ref[some, :] + (
            factor * scaled - values * (factor * factor * factor) * inner
        )
        vec_ref[0:1, :] = vec_ref[0:1, :] + jnp.sum(grad_in * values * factor, axis=0, keepdims=True)

    chunked(tok, input_rows)

    def v_copy(target):
        return to_lane(vec_ref, vz.at[lane], v_send.at[target], v_recv.at[lane], target)

    for step in range(1, LANES):
        v_copy(lax.rem(lane + step, LANES)).start()

    for step in range(1, LANES):
        source = lax.rem(lane + step, LANES)
        to_lane(vz.at[source], vz.at[source], v_send.at[0], v_recv.at[source], source).wait_recv()
    for step in range(1, LANES):
        v_copy(lax.rem(lane + step, LANES)).wait_send()
    total = vec_ref[...]
    for step in range(1, LANES):
        total = total + vz[lax.rem(lane + step, LANES)]
    vd[chips] = total
    swap = to_dp(vd.at[chips], vd.at[chips + 1], vs_send.at[0], vs_recv.at[chips], sibling)
    swap.start()
    swap.wait()
    vd[chip] = vd[chips] + vd[chips + 1]

    def vs_copy(mask):
        return to_dp(
            vd.at[chip], vd.at[chip], vs_send.at[mask], vs_recv.at[chip], 2 * flipped(chip, mask) + core
        )

    for mask in range(1, chips):
        vs_copy(mask).start()
    for mask in range(1, chips):
        c = flipped(chip, mask)
        to_dp(vd.at[c], vd.at[c], vs_send.at[0], vs_recv.at[c], sibling).wait_recv()
    for mask in range(1, chips):
        vs_copy(mask).wait_send()
    total = vd[0]
    for c in range(1, chips):
        total = total + vd[c]
    vec_ref[...] = total

    for step in range(1, LANES):
        other = lax.rem(lane + step, LANES)
        to_lane(zsum, woz_ref.at[:, lane_cols(other, quarter)], zg_send.at[0], zg_recv.at[other], other).wait_recv()
        to_lane(wqz_ref.at[other], wqz_ref.at[other], zq_send.at[0], zq_recv.at[other], other).wait_recv()
        gq_copy(other).wait_send()
        gkv_copy(other).wait_send()
        zr_copy(other).wait_send()
        zg_copy(other).wait_send()
        zq_copy(other).wait_send()
    out_sum.end()
    qkv_sum.end()
    for k in range(len(mats)):
        for mask in range(chips):
            c = flipped(chip, mask)
            ff_pair(k, c).wait_send()
            if mask:
                to_dp(fland.at[k, c], fland.at[k, c], fs_send.at[k, 0], fs_recv.at[k, c], sibling).wait_recv()
                ff_send(k, mask).wait_send()


def back(
    chips, mats, grad_resid, mlp_vec, hidden_in, vecs, qkv, log_sum, cos_row, sin_row, seg_col,
    seg_row, grad_low, grad_att, attended, wq_full, wk_full, wv_full, normed_row, mlp_grads,
):
    tok, width = hidden_in.shape
    row = tok * LANES
    gwid = qkv.shape[1]
    hw = gwid - 2 * HD
    ff = mlp_grads.shape[2]
    own = width // (2 * chips)
    half = width // 2
    anywhere = pl.BlockSpec(memory_space=pl.ANY)
    vmem = pl.BlockSpec(memory_space=pltpu.VMEM)
    dma = pltpu.SemaphoreType.DMA
    shape = jax.ShapeDtypeStruct
    vmem_outs = [
        shape((tok, width), F32),
        shape((8, width), F32),
        shape((own, width), BF16),
        shape((LANES, own, gwid), BF16),
    ]
    hbm_outs = [shape((len(mats), chips, own, ff), BF16)] * 3
    return pl.pallas_call(
        functools.partial(back_kernel, chips, mats),
        out_shape=vmem_outs + hbm_outs,
        in_specs=[vmem] * 10 + [anywhere] * 8,
        out_specs=[vmem] * len(vmem_outs) + [anywhere] * len(hbm_outs),
        scratch_shapes=[
            pltpu.VMEM((tok, width), BF16),
            pltpu.VMEM((width, width + 2 * KV_HEADS * HD), BF16),
            pltpu.VMEM((row, width), BF16),
            pltpu.VMEM((tok, width), BF16),
            pltpu.VMEM((row, hw), BF16),
            pltpu.VMEM((row, HD), F32),
            pltpu.VMEM((row, HD), F32),
            pltpu.VMEM((row, gwid), BF16),
            pltpu.VMEM((tok, LANES * gwid), BF16),
            pltpu.VMEM((hw // HD, 8, row), F32),
            pltpu.VMEM((width, width), BF16),
            pltpu.VMEM((half, width), BF16),
            pltpu.VMEM((half, width), BF16),
            pltpu.VMEM((own, width), BF16),
            pltpu.VMEM((LANES, own, width // LANES), BF16),
            pltpu.VMEM((own, width // LANES), BF16),
            pltpu.VMEM((width, gwid), BF16),
            pltpu.VMEM((half, gwid), BF16),
            pltpu.VMEM((half, gwid), BF16),
            pltpu.VMEM((2, own, ff), BF16),
            pltpu.VMEM((LANES, 8, width), F32),
            pltpu.VMEM((chips + 2, 8, width), F32),
            pltpu.VMEM((tok, width), F32),
            dma((7,)),
            dma((LANES,)),
            dma((LANES,)),
            dma((LANES,)),
            dma((LANES,)),
            *[dma((chips,))] * 8,
            *[dma((LANES,))] * 6,
            *[dma((len(mats), chips))] * 4,
            dma((3,)),
            dma((LANES,)),
            dma((LANES,)),
            dma((chips,)),
            dma((chips + 1,)),
        ],
        compiler_params=pltpu.CompilerParams(
            collective_id=2, has_side_effects=True, vmem_limit_bytes=61 * 2**20
        ),
        cost_estimate=pl.CostEstimate(
            flops=20 * row * width * gwid, bytes_accessed=12 * width * ff, transcendentals=row * width
        ),
        name="back",
    )(
        grad_resid, mlp_vec, hidden_in, vecs, qkv, log_sum, cos_row, sin_row, seg_col, seg_row,
        grad_low, grad_att, attended, wq_full, wk_full, wv_full, normed_row, mlp_grads,
    )


def body(
    hidden_in,
    segment_ids,
    position_ids,
    out_grad,
    attn_norm,
    w_query,
    w_key,
    w_value,
    b_query,
    b_key,
    b_value,
    w_out,
    mlp_norm,
    w_gate,
    w_up,
    w_down,
):
    chips = lax.axis_size("dp") // 2
    dp, lane = lax.axis_index("dp"), lax.axis_index("seq")
    local_tok, width = hidden_in.shape
    kv_group = LANES // KV_HEADS
    query_width = HEADS // LANES * HD

    def side_by_side(vectors, step, size):
        return sum(
            lax.pad(v, jnp.zeros((), v.dtype), [(k * step, size - k * step - v.shape[0], 0)])
            for k, v in enumerate(vectors)
        )

    vec = side_by_side((attn_norm, mlp_norm, b_query, b_key, b_value), 2 * HD, 16 * HD).reshape(16, HD)
    ids = side_by_side((position_ids, segment_ids), local_tok, 8 * local_tok).reshape(8, local_tok)
    inv_freq = ROPE_BASE ** (-(np.arange(HD // 2, dtype=np.float32) * np.float32(2.0 / HD)))
    freqs = np.tile(np.concatenate([inv_freq, inv_freq]).astype(np.float32)[None, :], (8, 1))
    (
        resid, mlp_local, vecs, qkv, attended, log_sum, cos_row, sin_row, seg_col, seg_row,
        normed_row, grad_rows, _, _, wo_full, gate_full, up_full, down_full,
    ) = front(
        chips, hidden_in, ids, freqs, out_grad, vec, w_query, w_key, w_value, w_out.T, w_gate, w_up, w_down
    )
    total, grad_resid, mlp_vec, grad_low, grad_att, down_part, _, ff_grads, _, wq_full, wk_full, wv_full = feed_forward(
        chips, mlp_local, grad_rows, gate_full, up_full, down_full, w_query, w_key, w_value, resid, out_grad,
        wo_full, vecs,
    )
    block_out = total.astype(jnp.bfloat16)
    input_grad, vec_grads, out_grad_rows, qkv_grads, _, _, down_grads = back(
        chips, (0,), grad_resid, mlp_vec, hidden_in, vecs, qkv, log_sum, cos_row, sin_row, seg_col,
        seg_row, grad_low, grad_att, attended, wq_full, wk_full, wv_full, normed_row, down_part,
    )
    gate_grad, up_grad, down_grad = (
        jnp.sum(part.astype(jnp.float32), axis=0) for part in (ff_grads[0], ff_grads[1], down_grads[0])
    )
    own = width // (2 * chips)
    kv_own = KV_HEADS * HD // (2 * chips)
    query_grad = jnp.concatenate(
        [qkv_grads[k, :, :query_width] for k in range(LANES)], axis=1
    ).astype(jnp.float32)

    def kv_grad(offset):
        parts = qkv_grads[:, :, offset : offset + HD].astype(jnp.float32)
        return jnp.concatenate(
            [
                jnp.sum(parts[k * kv_group : (k + 1) * kv_group], axis=0)
                for k in range(KV_HEADS)
            ],
            axis=1,
        )

    def own_vec(k, size):
        return lax.dynamic_slice(vec_grads, (k, dp * size), (1, size))[0]

    return (
        block_out,
        input_grad,
        own_vec(0, own),
        query_grad,
        kv_grad(query_width),
        kv_grad(query_width + HD),
        own_vec(2, own),
        own_vec(3, kv_own),
        own_vec(4, kv_own),
        out_grad_rows.astype(jnp.float32).T,
        own_vec(1, own),
        gate_grad,
        up_grad,
        down_grad,
    )


def solution(mesh):
    return jax.shard_map(
        body,
        mesh=mesh,
        in_specs=(
            P(("dp", "seq"), None),
            P(("dp", "seq")),
            P(("dp", "seq")),
            P(("dp", "seq"), None),
            P("dp"),
            P("dp", None),
            P("dp", None),
            P("dp", None),
            P("dp"),
            P("dp"),
            P("dp"),
            P(None, "dp"),
            P("dp"),
            P("dp", "seq"),
            P("dp", "seq"),
            P("dp", "seq"),
        ),
        out_specs=(
            P(("dp", "seq"), None),
            P(("dp", "seq"), None),
            P("dp"),
            P("dp", None),
            P("dp", None),
            P("dp", None),
            P("dp"),
            P("dp"),
            P("dp"),
            P(None, "dp"),
            P("dp"),
            P("dp", "seq"),
            P("dp", "seq"),
            P("dp", "seq"),
        ),
        check_vma=False,
    )
```

```python
import functools

import jax
import jax.numpy as jnp
import numpy as np
from jax import lax
from jax.experimental import pallas as pl
from jax.experimental.pallas import tpu as pltpu
from jax.sharding import PartitionSpec as P

HEADS = 12
KV_HEADS = 2
HD = 128
EPS = 1e-06
ROPE_BASE = 1000000.0
NEG_FILL = -1e30
MESH_ID = pl.DeviceIdType.MESH
LANES = 4
BF16 = jnp.bfloat16
F32 = jnp.float32


def nn(left, right):
    return jnp.dot(left, right, preferred_element_type=F32)


def nt(left, right):
    return lax.dot_general(left, right, (((1,), (1,)), ((), ())), preferred_element_type=F32)


def rows_of(index, size):
    return pl.ds(pl.multiple_of(index * size, size), size)


def digit(codes, lane):
    return lax.rem(lax.shift_right_logical(jnp.int32(codes), 2 * lane), 4)


def order_of(step, lane):
    tables = ((0, 1, 2, 3), (1, 0, 2, 3), (2, 3, 1, 0), (3, 2, 1, 0))
    codes = [sum(tables[k][i] * 4**k for k in range(LANES)) for i in range(LANES)]
    out = digit(codes[0], lane)
    for i in range(1, LANES):
        out = jnp.where(step == i, digit(codes[i], lane), out)
    return out


def flipped(chip, mask):
    out = chip
    for bit in range(8):
        if mask >> bit & 1:
            out = out + (1 - 2 * lax.rem(chip // 2**bit, 2)) * 2**bit
    return out


def meet_all(chips):
    dp, lane = lax.axis_index("dp"), lax.axis_index("seq")
    chip, core = dp // 2, lax.rem(dp, 2)
    barrier = pltpu.get_barrier_semaphore()
    for mask in range(1, chips):
        pl.semaphore_signal(
            barrier, 1, device_id={"dp": 2 * flipped(chip, mask) + core}, device_id_type=MESH_ID
        )
    pl.semaphore_signal(barrier, 1, device_id={"dp": 2 * chip + 1 - core}, device_id_type=MESH_ID)
    for step in range(1, LANES):
        pl.semaphore_signal(
            barrier, 1, device_id={"seq": lax.rem(lane + step, LANES)}, device_id_type=MESH_ID
        )
    pl.semaphore_wait(barrier, chips + LANES - 1)


class Gather:
    def __init__(self, chips, shard, full, send, fwd, recv, half_send, half_recv, halves=True):
        self.dp = lax.axis_index("dp")
        self.chip, self.core = self.dp // 2, lax.rem(self.dp, 2)
        self.chips, self.shard, self.full = chips, shard, full
        self.send, self.fwd, self.recv = send, fwd, recv
        self.half_send, self.half_recv = half_send, half_recv
        self.rows = shard.shape[0]
        self.square = chips == 4 and halves
        self.masks = (1, 2) if self.square else tuple(range(1, chips))

    def device(self, mask, other=False):
        return 2 * flipped(self.chip, mask) + (1 - self.core if other else self.core)

    def to(self, src, dst, send, recv, target):
        return pltpu.make_async_remote_copy(
            src, dst, send, recv, device_id={"dp": target}, device_id_type=MESH_ID
        )

    def own_copy(self, mask):
        return self.to(
            self.shard, self.full.at[rows_of(self.dp, self.rows)], self.send.at[mask],
            self.recv.at[self.dp], self.device(mask) if mask else self.device(0, True),
        )

    def hand_on(self, source):
        part = self.full.at[rows_of(source, self.rows)]
        return self.to(part, part, self.fwd.at[source // 2], self.recv.at[source], self.device(0, True))

    def half_copy(self, source, half, target):
        size = self.rows // 2
        part = self.full.at[rows_of(2 * source + half, size)]
        return self.to(part, part, self.half_send.at[half], self.half_recv.at[half], target)

    def begin(self):
        for mask in self.masks + (0,):
            self.own_copy(mask).start()

    def relay(self):
        for mask in self.masks:
            source = self.device(mask)
            self.hand_on(source).wait_recv()
            if self.square:
                self.half_copy(source, mask - 1, self.device(3 - mask)).start()
            self.hand_on(source).start()

    def relay_across(self):
        if self.square:
            source = self.device(3)
            for half in range(2):
                self.half_copy(source, half, self.device(1)).wait_recv()
            self.hand_on(source).start()

    def end(self):
        for mask in range(self.chips):
            self.hand_on(self.device(mask, True)).wait_recv()
        for mask in self.masks + (0,):
            self.own_copy(mask).wait_send()
        for mask in range(1, self.chips):
            self.hand_on(self.device(mask)).wait_send()
        if self.square:
            for half in range(2):
                self.half_copy(self.device(half + 1), half, self.device(2 - half)).wait_send()


def spread(out, shards, devices, first, size, count):
    width = out.shape[1]
    column = lax.broadcasted_iota(jnp.int32, (HD, width), 1)
    value = lax.broadcasted_iota(jnp.int32, (HD, width), 0)
    owner = lax.broadcasted_iota(jnp.int32, (devices, width), 1) // size
    mine = owner == lax.broadcasted_iota(jnp.int32, (devices, width), 0)
    for n in range(count):
        total = jnp.zeros((devices, width), F32)
        for part in range(2 if size > HD else 1):
            place = (lax.rem(column, size) == value + part * HD).astype(F32).astype(BF16)
            row = 2 * (first + n) + part
            rows = jnp.concatenate([shards[k * 16 : k * 16 + 16, :][row : row + 1] for k in range(devices)], axis=0)
            total = total + nn(rows, place)
        out[first + n : first + n + 1, :] = jnp.sum(jnp.where(mine, total, 0.0), axis=0, keepdims=True)


def front_kernel(
    chips,
    x_hbm, ids_hbm, freq_ref, og_hbm, vec_hbm, wq_hbm, wk_hbm, wv_hbm, wo_hbm, wg_hbm, wu_hbm, wd_hbm,
    resid_ref, mlp_ref, vecs_ref, qkv_ref, att_ref, lse_ref, cos_ref, sin_ref, segc_ref, segr_ref,
    nrm_hbm, ogf, vecf, wqkvf, wof, wgf, wuf, wdf,
    xb, ids, nrm, wqkv, wo, vecb, ab, own_vec, own_qkv, own_wo, own_gate, own_up, own_down, own_og,
    load_sem, dp_send, dp_fwd, dp_recv, half_send, half_recv, x_send, x_recv, i_send, i_recv, o_send, o_recv, a_send, a_recv,
):
    dp, lane = lax.axis_index("dp"), lax.axis_index("seq")
    chip, core = dp // 2, lax.rem(dp, 2)
    sibling = 2 * chip + 1 - core
    tok, width = x_hbm.shape
    heads = qkv_ref.shape[1] // HD - 2
    has_left, has_right = lane > 0, lane < LANES - 1
    left, right = jnp.maximum(lane - 1, 0), jnp.minimum(lane + 1, LANES - 1)
    here = rows_of(lane, tok)

    first_loads = [
        pltpu.make_async_copy(x_hbm, xb.at[here], load_sem.at[0]),
        pltpu.make_async_copy(ids_hbm, ids.at[lane], load_sem.at[1]),
        pltpu.make_async_copy(og_hbm, own_og, load_sem.at[2]),
    ]
    shards = (vec_hbm, own_qkv, wo_hbm, wg_hbm, wu_hbm, wd_hbm)
    fulls = (vecf, wqkvf, wof, wgf, wuf, wdf)
    own_parts = (own_vec, own_qkv, own_wo, own_gate, own_up, own_down)
    own_loads = [
        pltpu.make_async_copy(s, v, load_sem.at[3 + k])
        for k, (s, v) in enumerate(zip(shards, own_parts))
        if k != 1
    ]
    kv_at = pl.multiple_of(lane * KV_HEADS // LANES * HD, HD)
    qkv_loads = [
        pltpu.make_async_copy(
            wq_hbm.at[:, pl.ds(pl.multiple_of(lane * heads * HD, HD), heads * HD)],
            own_qkv.at[:, pl.ds(0, heads * HD)], load_sem.at[4],
        ),
        pltpu.make_async_copy(
            wk_hbm.at[:, pl.ds(kv_at, HD)], own_qkv.at[:, pl.ds(heads * HD, HD)], load_sem.at[13]
        ),
        pltpu.make_async_copy(
            wv_hbm.at[:, pl.ds(kv_at, HD)], own_qkv.at[:, pl.ds((heads + 1) * HD, HD)], load_sem.at[14]
        ),
    ]
    own_copies = [
        pltpu.make_async_copy(v, f.at[rows_of(dp, v.shape[0])], load_sem.at[3 + k])
        for k, (v, f) in enumerate(zip(own_parts, fulls))
    ]
    og_copy = pltpu.make_async_copy(own_og, ogf.at[here], load_sem.at[2])
    for copy in qkv_loads + first_loads + own_loads:
        copy.start()
    lse_ref[...] = jnp.zeros_like(lse_ref)
    meet_all(chips)

    gathers = [
        Gather(
            chips, shard, full, dp_send.at[k], dp_fwd.at[k], dp_recv.at[k], half_send.at[k], half_recv.at[k], k > 0
        )
        for k, (shard, full) in enumerate(zip(shards, fulls))
    ]

    def line_copy(buf, send, recv, block, way):
        part = buf(block)
        return pltpu.make_async_remote_copy(
            part, part, send.at[way, block], recv.at[block],
            device_id={"seq": right if way == 0 else left}, device_id_type=MESH_ID,
        )

    x_line = (lambda b: xb.at[rows_of(b, tok)], x_send, x_recv)
    i_line = (lambda b: ids.at[b], i_send, i_recv)
    o_line = (lambda b: ogf.at[rows_of(b, tok)], o_send, o_recv)

    def line_begin(*lines):
        @pl.when(has_right)
        def _():
            for line in lines:
                line_copy(*line, lane, 0).start()

        @pl.when(has_left)
        def _():
            for line in lines:
                line_copy(*line, lane, 1).start()

    def line_step(step, *lines):
        @pl.when(lane - step >= 0)
        def _():
            block = jnp.maximum(lane - step, 0)
            for line in lines:
                line_copy(*line, block, 0).wait_recv()

            @pl.when(has_right)
            def _():
                for line in lines:
                    line_copy(*line, block, 0).start()

        @pl.when(lane + step < LANES)
        def _():
            block = jnp.minimum(lane + step, LANES - 1)
            for line in lines:
                line_copy(*line, block, 1).wait_recv()

            @pl.when(has_left)
            def _():
                for line in lines:
                    line_copy(*line, block, 1).start()

    def line_end(*lines):
        for block in range(LANES):
            @pl.when(jnp.logical_and(has_right, block <= lane))
            def _(block=block):
                for line in lines:
                    line_copy(*line, block, 0).wait_send()

            @pl.when(jnp.logical_and(has_left, block >= lane))
            def _(block=block):
                for line in lines:
                    line_copy(*line, block, 1).wait_send()

    with jax.named_scope("first_sends"):
        gathers[0].begin()
        for copy in qkv_loads:
            copy.wait()
        gathers[1].begin()
    first_loads[0].wait()
    first_loads[1].wait()
    line_begin(i_line, x_line)
    for load in own_loads:
        load.wait()
    for copy in own_copies:
        copy.start()
    first_loads[2].wait()
    og_copy.start()
    with jax.named_scope("first_relay"):
        gathers[0].relay()
        gathers[1].relay()
    gathers[2].begin()
    gathers[3].begin()
    with jax.named_scope("first_end"):
        gathers[1].relay_across()
        for copy in own_copies + [og_copy]:
            copy.wait()
        gathers[0].end()
        gathers[1].end()
    vec_load = pltpu.make_async_copy(vecf, vecb, load_sem.at[9])
    wqkv_load = pltpu.make_async_copy(wqkvf, wqkv, load_sem.at[10])
    vec_load.start()
    wqkv_load.start()
    vec_load.wait()
    devices = 2 * chips
    spread(vecs_ref, vecb, devices, 0, width // devices, 3)
    spread(vecs_ref, vecb, devices, 3, KV_HEADS * HD // devices, 2)
    wqkv_load.wait()
    bias = jnp.concatenate(
        [
            vecs_ref[2:3, pl.ds(pl.multiple_of(lane * heads * HD, HD), heads * HD)],
            vecs_ref[3:4, pl.ds(pl.multiple_of(lane * KV_HEADS // LANES * HD, HD), HD)],
            vecs_ref[4:5, pl.ds(pl.multiple_of(lane * KV_HEADS // LANES * HD, HD), HD)],
        ],
        axis=1,
    )
    lane_sign = jnp.where(lax.broadcasted_iota(jnp.int32, (1, HD), 1) < HD // 2, -1.0, 1.0)

    def block_step(step, carry):
        block = order_of(step, lane)
        mine = rows_of(block, tok)
        id_rows = ids[block].astype(F32)
        segr_ref[:, mine] = jnp.broadcast_to(id_rows[1:2, :], (8, tok))
        segc_ref[mine, :] = jnp.broadcast_to(id_rows[1:2, :], (HD, tok)).T
        angles = jnp.broadcast_to(id_rows[0:1, :], (HD, tok)).T * freq_ref[0:1, :]
        cos_ref[mine, :] = jnp.cos(angles)
        sin_ref[mine, :] = jnp.sin(angles) * lane_sign

        def norm(i, c):
            some = pl.ds(pl.multiple_of(block * tok + i * 32, 32), 32)
            x = xb[some, :].astype(F32)
            factor = lax.rsqrt(jnp.mean(x * x, axis=-1, keepdims=True) + EPS)
            nrm[some, :] = (x * factor * vecs_ref[0:1, :]).astype(BF16)
            return c

        lax.fori_loop(0, tok // 32, norm, 0)

        @pl.when(step < LANES - 1)
        def _():
            with jax.named_scope("row_arrival"):
                @pl.when(step == LANES - 2)
                def _():
                    line_begin(o_line)

                line_step(step + 1, i_line, x_line)

        @pl.when(step == 1)
        def _():
            with jax.named_scope("w_out_relay"):
                gathers[2].relay()
            gathers[4].begin()

        pre = nn(nrm[mine, :], wqkv[...]) + bias
        cosine, sine = cos_ref[mine, :], sin_ref[mine, :]
        for h in range(heads + 1):
            cols = slice(h * HD, (h + 1) * HD)
            part = pre[:, cols]
            qkv_ref[mine, cols] = (part * cosine + pltpu.roll(part, HD // 2, 1) * sine).astype(BF16)
        cols = slice((heads + 1) * HD, (heads + 2) * HD)
        qkv_ref[mine, cols] = pre[:, cols].astype(BF16)
        return carry

    lax.fori_loop(0, LANES, block_step, 0)
    nrm_copy = pltpu.make_async_copy(nrm, nrm_hbm, load_sem.at[11])
    nrm_copy.start()
    with jax.named_scope("w_out_across"):
        gathers[2].relay_across()
    with jax.named_scope("gate_relay"):
        gathers[3].relay()
    gathers[5].begin()

    def att_send(i):
        cols = pl.ds(pl.multiple_of(lane * heads * HD, HD), heads * HD)
        return pltpu.make_async_remote_copy(
            ab.at[pl.ds(i * tok, tok)], att_ref.at[:, cols], a_send.at[i], a_recv.at[lane],
            device_id={"seq": i}, device_id_type=MESH_ID,
        )

    sub = 128
    for i in (3, 0, 2, 1):
        keys = (i + 1) * tok

        def att_step(t, carry, i=i, keys=keys):
            h = t // (tok // sub)
            start = i * tok + lax.rem(t, tok // sub) * sub
            some = pl.ds(pl.multiple_of(start, sub), sub)
            cols = pl.ds(pl.multiple_of(h * HD, HD), HD)
            scores = nt(qkv_ref[some, cols], qkv_ref[0:keys, heads * HD : (heads + 1) * HD]) * HD**-0.5
            same = segc_ref[some, 0:1] == segr_ref[0:1, 0:keys]
            behind = (
                lax.broadcasted_iota(jnp.int32, (sub, keys), 0) + start
                >= lax.broadcasted_iota(jnp.int32, (sub, keys), 1)
            )
            scores = jnp.where(jnp.logical_and(same, behind), scores, NEG_FILL)
            peak = jnp.max(scores, axis=-1, keepdims=True)
            exps = jnp.exp(scores - peak)
            totals = jnp.sum(exps, axis=-1, keepdims=True)
            prob = (exps * (1.0 / totals)).astype(BF16)
            ab[some, cols] = nn(prob, qkv_ref[0:keys, (heads + 1) * HD :]).astype(BF16)
            at_head = lax.broadcasted_iota(jnp.int32, (sub, HD), 1) == h
            lse_ref[some, :] = jnp.where(at_head, peak + jnp.log(totals), lse_ref[some, :])
            return carry

        with jax.named_scope("attention"):
            lax.fori_loop(0, heads * (tok // sub), att_step, 0)

        @pl.when(lane != i)
        def _(i=i):
            att_send(i).start()

    with jax.named_scope("cotangent_1"):
        line_step(1, o_line)
    own_cols = pl.ds(pl.multiple_of(lane * heads * HD, HD), heads * HD)
    att_ref[:, own_cols] = ab[here, :]
    with jax.named_scope("gate_across"):
        gathers[3].relay_across()
    with jax.named_scope("w_out_end"):
        gathers[2].end()
    wo_load = pltpu.make_async_copy(wof, wo, load_sem.at[12])
    wo_load.start()
    wo_load.wait()
    for i in range(LANES):
        @pl.when(lane != i)
        def _(i=i):
            pltpu.make_async_remote_copy(
                ab.at[pl.ds(0, tok)], att_ref.at[:, pl.ds(i * heads * HD, heads * HD)],
                a_send.at[0], a_recv.at[i], device_id={"seq": i}, device_id_type=MESH_ID,
            ).wait_recv()

    def out_tile(t, carry):
        cols = pl.ds(pl.multiple_of(t * 512, 512), 512)
        resid_ref[:, cols] = xb[here, cols].astype(F32) + nt(att_ref[...], wo[cols, :])
        return carry

    with jax.named_scope("out_project"):
        lax.fori_loop(0, width // 512, out_tile, 0)

    def mlp_norm(i, carry):
        some = pl.ds(pl.multiple_of(i * 32, 32), 32)
        x = resid_ref[some, :]
        factor = lax.rsqrt(jnp.mean(x * x, axis=-1, keepdims=True) + EPS)
        mlp_ref[some, :] = (x * factor * vecs_ref[1:2, :]).astype(BF16)
        return carry

    lax.fori_loop(0, tok // 32, mlp_norm, 0)
    with jax.named_scope("cotangent_2"):
        line_step(2, o_line)
    with jax.named_scope("up_down_relay"):
        gathers[4].relay()
        gathers[5].relay()
    with jax.named_scope("cotangent_3"):
        line_step(3, o_line)
    with jax.named_scope("weights_end"):
        gathers[4].relay_across()
        gathers[5].relay_across()
        for which in (3, 4, 5):
            gathers[which].end()
    nrm_copy.wait()
    line_end(i_line, x_line, o_line)
    for i in range(LANES):
        @pl.when(lane != i)
        def _(i=i):
            att_send(i).wait_send()


def front(chips, hidden_in, ids, freqs, out_grad, vec, w_query, w_key, w_value, wo, w_gate, w_up, w_down):
    tok, width = hidden_in.shape
    row = tok * LANES
    qkv_width = w_query.shape[1] // LANES + 2 * HD
    own_qkv = jax.ShapeDtypeStruct((w_query.shape[0], qkv_width), BF16)
    ff = w_gate.shape[1]
    anywhere = pl.BlockSpec(memory_space=pl.ANY)
    vmem = pl.BlockSpec(memory_space=pltpu.VMEM)
    dma = pltpu.SemaphoreType.DMA
    shape = jax.ShapeDtypeStruct
    vmem_outs = [
        shape((tok, width), F32),
        shape((tok, width), BF16),
        shape((16, width), F32),
        shape((row, qkv_width), BF16),
        shape((tok, width), BF16),
        shape((row, HD), F32),
        shape((row, HD), F32),
        shape((row, HD), F32),
        shape((row, HD), F32),
        shape((8, row), F32),
    ]
    hbm_outs = [
        shape((row, width), BF16),
        shape((row, width), BF16),
        shape((2 * chips * 16, HD), BF16),
        shape((width, qkv_width), BF16),
        shape((width, width), BF16),
        shape((width, ff), BF16),
        shape((width, ff), BF16),
        shape((width, ff), BF16),
    ]
    return pl.pallas_call(
        functools.partial(front_kernel, chips),
        out_shape=vmem_outs + hbm_outs,
        in_specs=[anywhere, anywhere, vmem] + [anywhere] * 9,
        out_specs=[vmem] * len(vmem_outs) + [anywhere] * len(hbm_outs),
        scratch_shapes=[
            pltpu.VMEM((row, width), BF16),
            pltpu.VMEM((LANES, 8, tok), jnp.int32),
            pltpu.VMEM((row, width), BF16),
            pltpu.VMEM((width, qkv_width), BF16),
            pltpu.VMEM((width, width), BF16),
            pltpu.VMEM((2 * chips * 16, HD), BF16),
            pltpu.VMEM((row, qkv_width - 2 * HD), BF16),
            *[pltpu.VMEM(part.shape, BF16) for part in (vec, own_qkv, wo, w_gate, w_up, w_down, out_grad)],
            dma((15,)),
            dma((6, chips)),
            dma((6, chips)),
            dma((6, 2 * chips)),
            dma((6, 2)),
            dma((6, 2)),
            dma((2, LANES)),
            dma((LANES,)),
            dma((2, LANES)),
            dma((LANES,)),
            dma((2, LANES)),
            dma((LANES,)),
            dma((LANES,)),
            dma((LANES,)),
        ],
        compiler_params=pltpu.CompilerParams(
            collective_id=1, has_side_effects=True, vmem_limit_bytes=56 * 2**20
        ),
        cost_estimate=pl.CostEstimate(
            flops=10 * row * width * qkv_width, bytes_accessed=12 * width * ff, transcendentals=row * width
        ),
        name="front",
    )(hidden_in, ids, freqs, out_grad, vec, w_query, w_key, w_value, wo, w_gate, w_up, w_down)


def ff_kernel(
    chips,
    x_hbm, og_hbm, wg_hbm, wu_hbm, wd_hbm, wq_hbm, wk_hbm, wv_hbm, resid_hbm, own_og_hbm, wo_hbm, vecs_ref,
    mo_ref, gm_ref, vec_ref, grl_hbm, ga_hbm, gw_hbm, fpair, fland_gate, fland_up, fmid, wqf, wkf, wvf,
    xb, og, wg, wu, wd, hid, gg, gu, pb, rb, rf,
    load_sem, ag_send, ag_recv, rb_send, rb_recv, rf_send, rf_recv, out_sem,
    dp_send, dp_fwd, dp_recv, half_send, half_recv, own_sem, fp_send, fp_recv, fk_sem, fs_send, fs_recv, fl_sem,
    p1_send, p1_recv, p2_send, p2_recv, a_send, a_recv, late_sem,
):
    lane, dp = lax.axis_index("seq"), lax.axis_index("dp")
    chip, core = dp // 2, lax.rem(dp, 2)
    tok, width = x_hbm.shape
    units = wg_hbm.shape[1]
    tile = 512
    full_tiles = units // tile
    tail = units - full_tiles * tile
    wtile = 384
    pieces = width // tile
    has_left, has_right = lane > 0, lane < LANES - 1
    is_end = jnp.logical_or(lane == 0, lane == LANES - 1)
    is_mid = jnp.logical_not(is_end)
    left, right = jnp.maximum(lane - 1, 0), jnp.minimum(lane + 1, LANES - 1)

    loads = [
        pltpu.make_async_copy(src, dst, load_sem.at[k])
        for k, (src, dst) in enumerate(
            ((wg_hbm, wg), (wu_hbm, wu), (wd_hbm, wd), (og_hbm, og))
        )
    ]
    own = pltpu.make_async_copy(x_hbm, xb.at[rows_of(lane, tok)], load_sem.at[4])
    own.start()
    for copy in loads:
        copy.start()

    attn_shards = ((wq_hbm, wqf), (wk_hbm, wkf), (wv_hbm, wvf))
    attn_loads, attn_own, begin = [], [], 0
    for k, (shard, full) in enumerate(attn_shards):
        kept = hid.at[pl.ds(0, shard.shape[0]), pl.ds(begin, shard.shape[1])]
        attn_loads.append(pltpu.make_async_copy(shard, kept, own_sem.at[k]))
        attn_own.append(pltpu.make_async_copy(kept, full.at[rows_of(dp, shard.shape[0])], own_sem.at[k]))
        begin += shard.shape[1]
    resid_load = pltpu.make_async_copy(resid_hbm, mo_ref, late_sem.at[0])
    resid_load.start()
    vec_ref[...] = jnp.zeros_like(vec_ref)
    for copy in attn_loads:
        copy.start()
    meet_all(chips)
    gathers = [
        Gather(
            chips, shard, full, dp_send.at[k], dp_fwd.at[k], dp_recv.at[k], half_send.at[k], half_recv.at[k]
        )
        for k, (shard, full) in enumerate(attn_shards)
    ]
    own.wait()

    def gather_copy(block, way):
        part = xb.at[rows_of(block, tok)]
        return pltpu.make_async_remote_copy(
            part, part, ag_send.at[way, block], ag_recv.at[block],
            device_id={"seq": right if way == 0 else left}, device_id_type=MESH_ID,
        )

    @pl.when(has_right)
    def _():
        gather_copy(lane, 0).start()

    @pl.when(has_left)
    def _():
        gather_copy(lane, 1).start()

    def arrivals(step):
        @pl.when(lane - step >= 0)
        def _():
            block = jnp.maximum(lane - step, 0)
            gather_copy(block, 0).wait_recv()

            @pl.when(has_right)
            def _():
                gather_copy(block, 0).start()

        @pl.when(lane + step < LANES)
        def _():
            block = jnp.minimum(lane + step, LANES - 1)
            gather_copy(block, 1).wait_recv()

            @pl.when(has_left)
            def _():
                gather_copy(block, 1).start()

    def cols_of(piece):
        return pl.ds(pl.multiple_of(piece * tile, tile), tile)

    def sum_send(part, landing, send, recv, block, piece):
        goes_left = block < lane
        target = jnp.where(goes_left, left, right)
        slot = jnp.where(jnp.logical_and(goes_left, target == block), LANES, block)
        return pltpu.make_async_remote_copy(
            part.at[rows_of(block, tok), cols_of(piece)], landing.at[rows_of(slot, tok), cols_of(piece)],
            send.at[block, piece], recv.at[slot, piece],
            device_id={"seq": target}, device_id_type=MESH_ID,
        )

    def sum_arrived(part, landing, send, recv, slot, piece):
        there = landing.at[rows_of(slot, tok), cols_of(piece)]
        pltpu.make_async_remote_copy(
            there, there, send.at[0, piece], recv.at[slot, piece], device_id={"seq": left}, device_id_type=MESH_ID
        ).wait_recv()

    def sum_pass(part, landing, send, recv, block):
        @pl.when(is_mid)
        def _():
            def one(piece, c):
                sum_arrived(part, landing, send, recv, block, piece)

                def add(i, carry):
                    mine = pl.ds(pl.multiple_of(block * tok + i * 64, 64), 64)
                    cols = cols_of(piece)
                    total = part[mine, cols].astype(F32) + landing[mine, cols].astype(F32)
                    part[mine, cols] = total.astype(BF16)
                    return carry

                lax.fori_loop(0, tok // 64, add, 0)
                sum_send(part, landing, send, recv, block, piece).start()
                return c

            lax.fori_loop(0, pieces, one, 0)

    def sum_last(part, landing, send, recv, out, onto=False):
        def begin(i, carry):
            here = pl.ds(pl.multiple_of(i * 32, 32), 32)
            mine = pl.ds(pl.multiple_of(lane * tok + i * 32, 32), 32)
            own_part = part[mine, :width].astype(F32)
            out[here, :] = out[here, :] + own_part if onto else own_part
            return carry

        lax.fori_loop(0, tok // 32, begin, 0)

        def take(slot):
            def one(piece, c):
                sum_arrived(part, landing, send, recv, slot, piece)

                def add(i, carry):
                    here = pl.ds(pl.multiple_of(i * 64, 64), 64)
                    there = pl.ds(pl.multiple_of(slot * tok + i * 64, 64), 64)
                    cols = cols_of(piece)
                    out[here, cols] = out[here, cols] + landing[there, cols].astype(F32)
                    return carry

                lax.fori_loop(0, tok // 64, add, 0)
                return c

            lax.fori_loop(0, pieces, one, 0)

        @pl.when(has_left)
        def _():
            take(lane)

        @pl.when(has_right)
        def _():
            take(jnp.int32(LANES))

    back = (pb, rb, rb_send, rb_recv)
    ahead = (og, rf, rf_send, rf_recv)
    for gather in gathers:
        gather.begin()
    for load, copy in zip(attn_loads, attn_own):
        load.wait()
        copy.start()
    with jax.named_scope("weights_load"):
        for copy in loads + attn_own:
            copy.wait()

    def down_part(block):
        mine = rows_of(block, tok)

        def down_tile(t, c):
            cols = cols_of(t)
            og[mine, cols] = nt(hid[mine, :], wd[cols, :]).astype(BF16)
            return c

        lax.fori_loop(0, pieces, down_tile, 0)

    def block_step(step, carry):
        block = order_of(step, lane)
        mine = rows_of(block, tok)

        def act(cols):
            gate = nn(xb[mine, :], wg[:, cols])
            up = nn(xb[mine, :], wu[:, cols])
            grad = nn(og[mine, :], wd[:, cols])
            sig = jax.nn.sigmoid(gate)
            silu = gate * sig
            hid[mine, cols] = (silu * up).astype(BF16)
            gg[mine, cols] = (grad * up * sig * (1.0 + gate * (1.0 - sig))).astype(BF16)
            gu[mine, cols] = (grad * silu).astype(BF16)

        def act_tile(t, c):
            act(pl.ds(pl.multiple_of(t * tile, tile), tile))
            return c

        with jax.named_scope("activations"):
            lax.fori_loop(0, full_tiles, act_tile, 0)
            if tail:
                act(pl.ds(full_tiles * tile, tail))

        @pl.when(step < LANES - 2)
        def _():
            with jax.named_scope("row_arrival"):
                arrivals(step + 1)

        @pl.when(step == 1)
        def _():
            with jax.named_scope("attn_relay"):
                for gather in gathers:
                    gather.relay()

        @pl.when(step == 2)
        def _():
            with jax.named_scope("attn_across"):
                for gather in gathers:
                    gather.relay_across()

        def back_tile(t, c):
            cols = pl.ds(pl.multiple_of(t * tile, tile), tile)
            pb[mine, cols] = (nt(gg[mine, :], wg[cols, :]) + nt(gu[mine, :], wu[cols, :])).astype(BF16)

            @pl.when(jnp.logical_and(is_end, step > 0))
            def _():
                sum_send(*back, block, t).start()

            return c

        with jax.named_scope("input_grad_part"):
            lax.fori_loop(0, width // tile, back_tile, 0)

        @pl.when(step < LANES - 1)
        def _():
            down_part(block)

        @pl.when(step == LANES - 2)
        def _():
            with jax.named_scope("row_arrival"):
                arrivals(LANES - 1)


        return carry

    lax.fori_loop(0, LANES, block_step, 0)

    wtiles = width // wtile
    part_rows = width // (2 * chips)
    tile_chips = wtile // (2 * part_rows)

    square = chips == 4
    fland = (fland_gate, fland_up)
    half = part_rows // 2

    def tile_at(step):
        base, mask = chip // (chips // wtiles), wtiles - 1 - step
        return lax.rem(base + mask, 2) + 2 * lax.rem(base // 2 + mask // 2, 2)

    def held(which, c):
        return rows_of(which * chips + c, part_rows)

    def pair_send(which, c, r):
        theirs = pl.ds(pl.multiple_of(which * wtile + (2 * r + 1 - core) * part_rows, 16), part_rows)
        return pltpu.make_async_remote_copy(
            wu.at[theirs], fpair.at[which, c], fp_send.at[which, c], fp_recv.at[which, c],
            device_id={"dp": 2 * chip + 1 - core}, device_id_type=MESH_ID,
        )

    def pair_keep(which, c, r):
        mine = pl.ds(pl.multiple_of(which * wtile + (2 * r + core) * part_rows, 16), part_rows)
        return pltpu.make_async_copy(wu.at[mine], wg.at[held(which, c)], fk_sem.at[which, c])

    def to_chip(src, dst, send, recv, mask):
        return pltpu.make_async_remote_copy(
            src, dst, send, recv, device_id={"dp": 2 * flipped(chip, mask) + core}, device_id_type=MESH_ID
        )

    def chip_keep(which):
        return pltpu.make_async_copy(
            wg.at[held(which, chip)], fland[which].at[0], fl_sem.at[which]
        )

    def chip_send(which, mask):
        return to_chip(
            wg.at[held(which, flipped(chip, mask))], fland[which].at[mask], fs_send.at[which, mask],
            fs_recv.at[which, mask], mask,
        )

    def part_of(which, mask, upper):
        return wg.at[pl.ds(pl.multiple_of((which * chips + flipped(chip, mask)) * part_rows + upper * half, 16), half)]

    def first_hop(which, mask, upper):
        if mask == 3:
            landing = fmid.at[which, upper]
        else:
            landing = fland[which].at[1, pl.ds(upper * half, half)]
        k = 2 * (mask == 3) + upper
        return to_chip(part_of(which, mask, upper), landing, p1_send.at[which, k], p1_recv.at[which, k], 1 + upper)

    def second_hop(which, upper):
        mask = 2 - upper
        return to_chip(
            part_of(which, mask, upper), fland[which].at[2, pl.ds(upper * half, half)],
            p2_send.at[which, upper], p2_recv.at[which, upper], mask,
        )

    def load_slot(which):
        return wu.at[pl.ds(3 * wtile + which * part_rows, part_rows)]

    def add_in(which, first, rows):
        def add(i, carry):
            mine = pl.ds(pl.multiple_of(first + i * 16, 16), 16)
            other = pl.ds(pl.multiple_of(3 * wtile + which * part_rows + i * 16, 16), 16)
            wg[mine, :] = (wg[mine, :].astype(F32) + wu[other, :].astype(F32)).astype(BF16)
            return carry

        lax.fori_loop(0, rows // 16, add, 0)

    def pass_halves(upper):
        arrived = []
        for which in range(2):
            first_hop(which, 3, upper).wait_recv()
            arrived.append(
                pltpu.make_async_copy(
                    fmid.at[which, upper], wu.at[pl.ds(3 * wtile + which * part_rows, half)], load_sem.at[which]
                )
            )
            arrived[which].start()
        for which in range(2):
            arrived[which].wait()
            c = flipped(chip, 2 - upper)
            add_in(which, (which * chips + c) * part_rows + upper * half, half)
            second_hop(which, upper).start()

    def pair_load(which, c):
        return pltpu.make_async_copy(fpair.at[which, c], load_slot(which), load_sem.at[which])

    def load_pairs(step, r=0):
        for which in range(2):
            c = tile_at(step) * tile_chips + r
            pair_send(which, c, r).wait_recv()
            pair_load(which, c).start()

    def add_pairs(step):
        k = tile_at(step)
        for r in range(tile_chips):
            c = k * tile_chips + r
            if r:
                load_pairs(step, r)
            for which in range(2):
                pair_keep(which, c, r).wait()
                pair_load(which, c).wait()
                add_in(which, (which * chips + c) * part_rows, part_rows)
                if not square:
                    continue
                if step == 0:
                    first_hop(which, 3, 0).start()
                    first_hop(which, 3, 1).start()
                elif step == 1:
                    first_hop(which, 2, 1).start()
                elif step == 2:
                    first_hop(which, 1, 0).start()
                else:
                    chip_keep(which).start()

    def product(stage_ref, stage, lhs, rhs):
        def tile_of(cols):
            stage_ref[stage, cols] = nn(wu[lhs], rhs[:, cols]).astype(BF16)

        def one(t, c):
            tile_of(pl.ds(pl.multiple_of(t * tile, tile), tile))
            return c

        lax.fori_loop(0, full_tiles, one, 0)
        if tail:
            tile_of(pl.ds(full_tiles * tile, tail))

    turned = (pl.ds(2 * wtile, wtile), pl.ds(0, LANES * tok))

    def grad_tile(step):
        k = tile_at(step)
        if step:
            for which in range(2):
                for r in range(tile_chips):
                    before = tile_at(step - 1) * tile_chips + r
                    pair_send(which, before, r).wait_send()
        wu[turned] = xb[:, rows_of(k, wtile)].T
        for which, rhs in enumerate((gg, gu)):
            product(wu, pl.ds(which * wtile, wtile), turned, rhs)
            for r in range(tile_chips):
                pair_send(which, k * tile_chips + r, r).start()
                pair_keep(which, k * tile_chips + r, r).start()

    def down_grad_out(step):
        stage = rows_of(lax.rem(step, 2), wtile)
        return pltpu.make_async_copy(
            gg.at[stage], gw_hbm.at[0, rows_of(step, wtile)], out_sem.at[lax.rem(step, 2)]
        )

    def down_grad_tile(step, carry):
        @pl.when(step > 1)
        def _():
            down_grad_out(step - 2).wait()

        wu[turned] = xb[:, rows_of(step, wtile)].T
        product(gg, rows_of(lax.rem(step, 2), wtile), turned, hid)
        down_grad_out(step).start()
        return carry

    mid_near, mid_far, mid_back = 3 - lane, 6 - 3 * lane, 3 * lane - 3
    down_part(order_of(LANES - 1, lane))

    @pl.when(is_end)
    def _():
        for step in range(LANES - 1, 0, -1):
            for piece in range(pieces):
                sum_send(*ahead, order_of(step, lane), piece).start()

    sum_pass(*back, mid_near)
    wo = wd.at[:, pl.ds(0, width)]
    wo_load = pltpu.make_async_copy(wo_hbm, wo, late_sem.at[1])
    wo_load.start()
    grad_tile(0)
    load_pairs(0)
    add_pairs(0)
    grad_tile(1)
    load_pairs(1)
    sum_pass(*back, mid_far)
    add_pairs(1)
    grad_tile(2)
    load_pairs(2)
    sum_pass(*back, mid_back)
    sum_pass(*ahead, mid_far)
    add_pairs(2)
    grad_tile(3)
    for block in range(LANES):
        @pl.when(jnp.logical_and(has_right, block <= lane))
        def _(block=block):
            gather_copy(block, 0).wait_send()

        @pl.when(jnp.logical_and(has_left, block >= lane))
        def _(block=block):
            gather_copy(block, 1).wait_send()

    again = pltpu.make_async_copy(og_hbm, xb, load_sem.at[3])
    again.start()
    load_pairs(3)
    sum_last(*back, gm_ref)
    for block in range(LANES):
        @pl.when(block != lane)
        def _(block=block):
            for piece in range(pieces):
                sum_send(*back, block, piece).wait_send()

    own_og, grl, gao = (pb.at[pl.ds(k * tok, tok)] for k in range(3))
    og_load = pltpu.make_async_copy(own_og_hbm, own_og, late_sem.at[2])
    og_load.start()
    og_load.wait()
    resid_load.wait()

    def resid_rows(i, carry):
        some = pl.ds(pl.multiple_of(i * 32, 32), 32)
        values = mo_ref[some, :]
        grad_in = gm_ref[some, :]
        factor = lax.rsqrt(jnp.mean(values * values, axis=-1, keepdims=True) + EPS)
        scaled = grad_in * vecs_ref[1:2, :]
        inner = jnp.mean(scaled * values, axis=-1, keepdims=True)
        grad = own_og[some, :].astype(F32) + (factor * scaled - values * (factor * factor * factor) * inner)
        gm_ref[some, :] = grad
        grl[some, :] = grad.astype(BF16)
        vec_ref[1:2, :] = vec_ref[1:2, :] + jnp.sum(grad_in * values * factor, axis=0, keepdims=True)
        return carry

    lax.fori_loop(0, tok // 32, resid_rows, 0)
    grl_out = pltpu.make_async_copy(grl, grl_hbm, late_sem.at[2])
    grl_out.start()
    wo_load.wait()
    hw = width // LANES

    def head_cols(which):
        return pl.ds(pl.multiple_of(which * hw, hw), hw)

    def a_copy(target):
        return pltpu.make_async_remote_copy(
            gao.at[:, head_cols(target)], ga_hbm.at[rows_of(lane, tok)], a_send.at[target], a_recv.at[lane],
            device_id={"seq": target}, device_id_type=MESH_ID,
        )

    for step in range(1, LANES + 1):
        target = lax.rem(lane + step, LANES)
        gao[:, head_cols(target)] = nn(grl[...], wo[:, head_cols(target)]).astype(BF16)
        if step < LANES:
            a_copy(target).start()
    ga_own = pltpu.make_async_copy(gao.at[:, head_cols(lane)], ga_hbm.at[rows_of(lane, tok)], late_sem.at[1])
    ga_own.start()
    add_pairs(3)
    sum_pass(*ahead, mid_near)
    sum_pass(*ahead, mid_back)
    if square:
        pass_halves(0)
        pass_halves(1)
    else:
        for which in range(2):
            chip_keep(which).start()
            for mask in range(1, chips):
                chip_send(which, mask).start()
    again.wait()
    lax.fori_loop(0, wtiles, down_grad_tile, 0)
    sum_last(*ahead, mo_ref, True)
    grl_out.wait()
    ga_own.wait()
    for step in range(1, LANES):
        other = lax.rem(lane + step, LANES)
        a_copy(other).wait_send()
        pltpu.make_async_remote_copy(
            gao.at[:, head_cols(other)], ga_hbm.at[rows_of(other, tok)], a_send.at[0], a_recv.at[other],
            device_id={"seq": other}, device_id_type=MESH_ID,
        ).wait_recv()
    for gather in gathers:
        gather.end()
    down_grad_out(wtiles - 2).wait()
    down_grad_out(wtiles - 1).wait()
    for which in range(2):
        for r in range(tile_chips):
            last = tile_at(wtiles - 1) * tile_chips + r
            pair_send(which, last, r).wait_send()
        chip_keep(which).wait()
        if square:
            for mask, upper in ((3, 0), (3, 1), (2, 1), (1, 0)):
                first_hop(which, mask, upper).wait_send()
                if mask != 3:
                    first_hop(which, mask, upper).wait_recv()
            for upper in range(2):
                second_hop(which, upper).wait()
        else:
            for mask in range(1, chips):
                chip_send(which, mask).wait()

    for block in range(LANES):
        @pl.when(block != lane)
        def _(block=block):
            for piece in range(pieces):
                sum_send(*ahead, block, piece).wait_send()


def feed_forward(
    chips, mlp_local, grad_rows, gate_full, up_full, down_full, w_query, w_key, w_value, resid, out_grad, wo_full, vecs
):
    tok, width = mlp_local.shape
    units = gate_full.shape[1]
    row = tok * LANES
    own = width // (2 * chips)
    anywhere = pl.BlockSpec(memory_space=pl.ANY)
    vmem = pl.BlockSpec(memory_space=pltpu.VMEM)
    dma = pltpu.SemaphoreType.DMA
    shape = jax.ShapeDtypeStruct
    return pl.pallas_call(
        functools.partial(ff_kernel, chips),
        out_shape=(
            shape((tok, width), F32),
            shape((tok, width), F32),
            shape((8, width), F32),
            shape((tok, width), BF16),
            shape((row, width // LANES), BF16),
            shape((1, width, units), BF16),
            shape((2, chips, own, units), BF16),
            shape((3 if chips == 4 else chips, own, units), BF16),
            shape((3 if chips == 4 else chips, own, units), BF16),
            shape((2, 2, own // 2, units), BF16),
            shape((width, w_query.shape[1]), BF16),
            shape((width, w_key.shape[1]), BF16),
            shape((width, w_value.shape[1]), BF16),
        ),
        in_specs=[anywhere] * 11 + [vmem],
        out_specs=(vmem, vmem, vmem) + (anywhere,) * 10,
        scratch_shapes=[
            pltpu.VMEM((row, width), BF16),
            pltpu.VMEM((row, width), BF16),
            pltpu.VMEM((width, units), BF16),
            pltpu.VMEM((width, units), BF16),
            pltpu.VMEM((width, units), BF16),
            pltpu.VMEM((row, units), BF16),
            pltpu.VMEM((row, units), BF16),
            pltpu.VMEM((row, units), BF16),
            pltpu.VMEM((row, width), BF16),
            pltpu.VMEM((row + tok, width), BF16),
            pltpu.VMEM((row + tok, width), BF16),
            dma((5,)),
            dma((2, LANES)),
            dma((LANES,)),
            dma((LANES, width // 512)),
            dma((LANES + 1, width // 512)),
            dma((LANES, width // 512)),
            dma((LANES + 1, width // 512)),
            dma((2,)),
            dma((3, chips)),
            dma((3, chips)),
            dma((3, 2 * chips)),
            dma((3, 2)),
            dma((3, 2)),
            dma((3,)),
            *[dma((2, chips))] * 5,
            dma((2,)),
            dma((2, 4)),
            dma((2, 4)),
            dma((2, 2)),
            dma((2, 2)),
            dma((LANES,)),
            dma((LANES,)),
            dma((3,)),
        ],
        compiler_params=pltpu.CompilerParams(
            collective_id=3, has_side_effects=True, vmem_limit_bytes=60 * 2**20
        ),
        cost_estimate=pl.CostEstimate(
            flops=18 * row * width * units, bytes_accessed=12 * width * units, transcendentals=row * units
        ),
        name="feed_forward",
    )(
        mlp_local, grad_rows, gate_full, up_full, down_full, w_query, w_key, w_value, resid, out_grad, wo_full, vecs
    )


def chunked(rows, body, size=32):
    lax.fori_loop(0, rows // size, lambda i, c: (body(pl.multiple_of(i * size, size)), c)[1], 0)


def tn(left, right):
    return lax.dot_general(left, right, (((0,), (0,)), ((), ())), preferred_element_type=F32)


def back_kernel(
    chips, mats,
    gr_ref, mlp_vec_ref, x_ref, vecs_ref, qkv_ref, lse_ref, cos_ref, sin_ref, segc_ref, segr_ref,
    grl_hbm, ga_hbm, att_hbm, wq_hbm, wk_hbm, wv_hbm, nrm_hbm, gw_hbm,
    ig_ref, vec_ref, woz_ref, wqz_ref, fland,
    att, wfull, nrm, grl, ga, gk, gv, g, gl, lt,
    wop, wopair, woland, wores, zin, zsum,
    wqp, wqpair, wqland, theirs, mine, pairs, vz, vd, gn,
    load_sem, g_send, g_recv, h_send, h_recv,
    po_send, po_recv, so_send, so_recv, pq_send, pq_recv, sq_send, sq_recv,
    zr_send, zr_recv, zg_send, zg_recv, zq_send, zq_recv,
    fp_send, fp_recv, fs_send, fs_recv, slot_sem, v_send, v_recv, vs_send, vs_recv,
):
    dp, lane = lax.axis_index("dp"), lax.axis_index("seq")
    chip, core = dp // 2, lax.rem(dp, 2)
    sibling = 2 * chip + 1 - core
    tok, width = x_ref.shape
    row = tok * LANES
    part_rows = width // (2 * chips)
    heads = qkv_ref.shape[1] // HD - 2
    hw = heads * HD
    gwid = hw + 2 * HD
    here = rows_of(lane, tok)

    def lane_cols(which, size):
        return pl.ds(pl.multiple_of(which * size, size), size)

    loads = [
        pltpu.make_async_copy(src, dst, load_sem.at[k])
        for k, (src, dst) in enumerate(
            (
                (grl_hbm, grl),
                (att_hbm, att),
                (ga_hbm, ga),
                (nrm_hbm, nrm),
                (wq_hbm, wfull.at[:, pl.ds(0, LANES * hw)]),
                (wk_hbm, wfull.at[:, pl.ds(LANES * hw, KV_HEADS * HD)]),
                (wv_hbm, wfull.at[:, pl.ds(LANES * hw + KV_HEADS * HD, KV_HEADS * HD)]),
            )
        )
    ]
    for copy in loads:
        copy.start()
    vec_ref[...] = mlp_vec_ref[...]
    meet_all(chips)

    def to_dp(src, dst, send, recv, target):
        return pltpu.make_async_remote_copy(
            src, dst, send, recv, device_id={"dp": target}, device_id_type=MESH_ID
        )

    def to_lane(src, dst, send, recv, target):
        return pltpu.make_async_remote_copy(
            src, dst, send, recv, device_id={"seq": target}, device_id_type=MESH_ID
        )

    def ff_load(k, c, other):
        kept, sem = (theirs, slot_sem.at[0, k, c]) if other else (mine, slot_sem.at[1, k, c])
        rows = rows_of(2 * c + (1 - core if other else core), part_rows)
        return pltpu.make_async_copy(gw_hbm.at[mats[k], rows], kept.at[k, c], sem)

    def ff_pair(k, c):
        return to_dp(theirs.at[k, c], pairs.at[k, c], fp_send.at[k, c], fp_recv.at[k, c], sibling)

    def ff_send(k, mask):
        c = flipped(chip, mask)
        return to_dp(
            mine.at[k, c], fland.at[k, chip], fs_send.at[k, c], fs_recv.at[k, chip], 2 * c + core
        )

    def ff_own(k):
        return pltpu.make_async_copy(mine.at[k, chip], fland.at[k, chip], slot_sem.at[0, k, chip])

    ff_turns = [(k, mask) for k in range(len(mats)) for mask in list(range(chips - 1, 0, -1)) + [0]]
    for k, mask in ff_turns:
        ff_load(k, flipped(chip, mask), True).start()
        ff_load(k, flipped(chip, mask), False).start()
    for k, mask in ff_turns:
        c = flipped(chip, mask)
        ff_load(k, c, True).wait()
        ff_pair(k, c).start()

    def ff_add(k, mask):
        c = flipped(chip, mask)
        ff_load(k, c, False).wait()
        ff_pair(k, c).wait_recv()

        def add(start):
            some = pl.ds(start, 16)
            mine[k, c, some, :] = (mine[k, c, some, :].astype(F32) + pairs[k, c, some, :].astype(F32)).astype(BF16)

        chunked(part_rows, add, 16)
        if mask:
            ff_send(k, mask).start()
        else:
            ff_own(k).start()

    loads[0].wait()
    loads[1].wait()

    def out_grad_tile(i, carry):
        some = lane_cols(i, 384)
        for n in range(width // 512):
            cols = slice(n * 512, (n + 1) * 512)
            wop[some, cols] = tn(grl[:, some], att[:, cols]).astype(BF16)
        return carry

    lax.fori_loop(0, width // 384, out_grad_tile, 0)

    class Sum:
        def __init__(self, partial, pair, land, pair_send, pair_recv, send, recv):
            self.partial, self.pair, self.land = partial, pair, land
            self.pair_send, self.pair_recv, self.send, self.recv = pair_send, pair_recv, send, recv

        def pair_copy(self, c):
            return to_dp(
                self.partial.at[rows_of(2 * c + 1 - core, part_rows)], self.pair.at[rows_of(c, part_rows)],
                self.pair_send.at[c], self.pair_recv.at[c], sibling,
            )

        def send_copy(self, mask):
            c = flipped(chip, mask)
            return to_dp(
                self.partial.at[rows_of(2 * c + core, part_rows)], self.land.at[rows_of(chip, part_rows)],
                self.send.at[c], self.recv.at[chip], 2 * c + core,
            )

        def begin(self):
            for mask in range(chips):
                self.pair_copy(flipped(chip, mask)).start()

        def middle(self):
            for mask in list(range(1, chips)) + [0]:
                c = flipped(chip, mask)
                self.pair_copy(c).wait_recv()

                def add(start, c=c):
                    mine = pl.ds(pl.multiple_of((2 * c + core) * part_rows + start, 16), 16)
                    other = pl.ds(pl.multiple_of(c * part_rows + start, 16), 16)
                    self.partial[mine, :] = (
                        self.partial[mine, :].astype(F32) + self.pair[other, :].astype(F32)
                    ).astype(BF16)

                chunked(part_rows, add, 16)
                if mask:
                    self.send_copy(mask).start()

        def last(self, out):
            for mask in range(1, chips):
                c = flipped(chip, mask)
                to_dp(
                    self.land.at[rows_of(c, part_rows)], self.land.at[rows_of(c, part_rows)],
                    self.send.at[0], self.recv.at[c], sibling,
                ).wait_recv()

            def add(start):
                some = pl.ds(start, 16)
                total = self.partial[pl.ds(pl.multiple_of(dp * part_rows + start, 16), 16), :].astype(F32)
                for mask in range(1, chips):
                    c = flipped(chip, mask)
                    total = total + self.land[
                        pl.ds(pl.multiple_of(c * part_rows + start, 16), 16), :
                    ].astype(F32)
                out(some, total.astype(BF16))

            chunked(part_rows, add, 16)

        def end(self):
            for mask in range(chips):
                self.pair_copy(flipped(chip, mask)).wait_send()
                if mask:
                    self.send_copy(mask).wait_send()

    out_sum = Sum(wop, wopair, woland, po_send, po_recv, so_send, so_recv)
    qkv_sum = Sum(wqp, wqpair, wqland, pq_send, pq_recv, sq_send, sq_recv)
    out_sum.begin()

    def turn(i, carry):
        some = rows_of(i, tok)
        turned = lse_ref[some, :].T
        for h in range(heads):
            lt[h, :, some] = jnp.broadcast_to(turned[h : h + 1, :], (8, tok))
        return carry

    lax.fori_loop(0, LANES, turn, 0)
    gk[...] = jnp.zeros_like(gk)
    gv[...] = jnp.zeros_like(gv)
    out_sum.middle()
    loads[2].wait()

    def out_store(some, value):
        wores[some, :] = value

    quarter = width // LANES

    def zr_copy(target):
        return to_lane(
            wores.at[:, lane_cols(target, quarter)], zin.at[lane], zr_send.at[target], zr_recv.at[lane], target
        )

    def own_out():
        out_sum.last(out_store)
        for step in range(1, LANES):
            zr_copy(lax.rem(lane + step, LANES)).start()
        zin[lane] = wores[:, lane_cols(lane, quarter)]

    def gq_copy(target):
        return to_lane(
            g.at[rows_of(target, tok), pl.ds(0, hw)],
            gl.at[:, pl.ds(pl.multiple_of(lane * gwid, HD), hw)],
            g_send.at[target], g_recv.at[lane], target,
        )

    def gkv_copy(target):
        return to_lane(
            g.at[rows_of(target, tok), pl.ds(hw, 2 * HD)],
            gl.at[:, pl.ds(pl.multiple_of(lane * gwid + hw, HD), 2 * HD)],
            h_send.at[target], h_recv.at[lane], target,
        )

    sub = 128
    scale = HD**-0.5
    for i in (3, 0, 2, 1):
        keys = (i + 1) * tok

        def att_step(t, carry, i=i, keys=keys):
            h = t // (tok // sub)
            start = i * tok + lax.rem(t, tok // sub) * sub
            some = pl.ds(pl.multiple_of(start, sub), sub)
            cols = lane_cols(h, HD)
            key, value = qkv_ref[0:keys, hw : hw + HD], qkv_ref[0:keys, hw + HD :]
            query, grad = qkv_ref[some, cols], ga[some, cols]
            scores = nt(key, query) * scale
            same = segc_ref[0:keys, 0:1] == segr_ref[0:1, some]
            behind = (
                lax.broadcasted_iota(jnp.int32, (keys, sub), 1) + start
                >= lax.broadcasted_iota(jnp.int32, (keys, sub), 0)
            )
            scores = jnp.where(jnp.logical_and(same, behind), scores, NEG_FILL)
            prob = jnp.exp(scores - lt[h, 0:1, some])
            grad_prob = nt(value, grad)
            inner = jnp.sum(prob * grad_prob, axis=0, keepdims=True)
            grad_scores = (prob * (grad_prob - inner)).astype(BF16)
            gq = (tn(grad_scores, key) * scale).astype(BF16).astype(F32)
            gk[0:keys, :] = gk[0:keys, :] + nn(grad_scores, query)
            gv[0:keys, :] = gv[0:keys, :] + nn(prob.astype(BF16), grad)
            g[some, cols] = (
                gq * cos_ref[some, :] + pltpu.roll(gq * sin_ref[some, :], HD // 2, 1)
            ).astype(BF16)
            return carry

        lax.fori_loop(0, heads * (tok // sub), att_step, 0)

        @pl.when(lane != i)
        def _(i=i):
            gq_copy(jnp.int32(i)).start()

    def close(start):
        some = pl.ds(start, 32)
        grad = (gk[some, :] * scale).astype(BF16).astype(F32)
        g[some, hw : hw + HD] = (
            grad * cos_ref[some, :] + pltpu.roll(grad * sin_ref[some, :], HD // 2, 1)
        ).astype(BF16)
        g[some, hw + HD :] = gv[some, :].astype(BF16)

    chunked(row, close)

    for step in range(1, LANES):
        gkv_copy(lax.rem(lane + step, LANES)).start()
    gl[:, lane_cols(lane, gwid)] = g[here, :]
    loads[3].wait()

    def qkv_grad_tile(i, carry):
        some = lane_cols(i, 384)
        wqp[some, :] = tn(nrm[:, some], g[...]).astype(BF16)
        return carry

    lax.fori_loop(0, width // 384, qkv_grad_tile, 0)
    qkv_sum.begin()
    sums = jnp.zeros((1, gwid), F32)
    for i in range(row // 128):
        sums = sums + jnp.sum(g[i * 128 : (i + 1) * 128, :].astype(F32), axis=0, keepdims=True)
    kv_head = lane * KV_HEADS // LANES
    vec_ref[2:3, lane_cols(lane, hw)] = sums[:, :hw]
    vec_ref[3:4, lane_cols(kv_head, HD)] = sums[:, hw : hw + HD]
    vec_ref[4:5, lane_cols(kv_head, HD)] = sums[:, hw + HD :]

    def qkv_store(some, value):
        wqz_ref[lane, some, :] = value

    def zq_copy(target):
        return to_lane(
            wqz_ref.at[lane], wqz_ref.at[lane], zq_send.at[target], zq_recv.at[lane], target
        )

    own_out()
    qkv_sum.middle()
    for turn in ff_turns:
        ff_add(*turn)
    qkv_sum.last(qkv_store)
    for step in range(1, LANES):
        zq_copy(lax.rem(lane + step, LANES)).start()
    for step in range(1, LANES):
        source = lax.rem(lane + step, LANES)
        to_lane(zin.at[source], zin.at[source], zr_send.at[0], zr_recv.at[source], source).wait_recv()
    total = zin[0].astype(F32)
    for j in range(1, LANES):
        total = total + zin[j].astype(F32)
    zsum[...] = total.astype(BF16)
    woz_ref[:, lane_cols(lane, quarter)] = zsum[...]

    def zg_copy(target):
        return to_lane(
            zsum, woz_ref.at[:, lane_cols(lane, quarter)], zg_send.at[target], zg_recv.at[lane], target
        )

    for step in range(1, LANES):
        zg_copy(lax.rem(lane + step, LANES)).start()

    for copy in loads[4:]:
        copy.wait()
    for step in range(1, LANES):
        source = lax.rem(lane + step, LANES)
        for begin, size, recv in ((0, hw, g_recv), (hw, 2 * HD, h_recv)):
            to_lane(
                g.at[here, pl.ds(begin, size)], gl.at[:, pl.ds(pl.multiple_of(source * gwid + begin, HD), size)],
                g_send.at[0], recv.at[source], source,
            ).wait_recv()
    group = LANES // KV_HEADS

    def kv_total(kv, offset):
        parts = [
            gl[:, (kv * group + j) * gwid + offset : (kv * group + j) * gwid + offset + HD].astype(F32)
            for j in range(group)
        ]
        return sum(parts[1:], parts[0]).astype(BF16)

    kv_grads = [kv_total(kv, hw + offset) for offset in (0, HD) for kv in range(KV_HEADS)]
    kv_grads = jnp.concatenate(kv_grads, axis=1)

    def normed_tile(i, carry):
        some = lane_cols(i, 512)
        total = nt(kv_grads, wfull[some, LANES * hw :])
        for j in range(LANES):
            total = total + nt(gl[:, j * gwid : j * gwid + hw], wfull[some, j * hw : (j + 1) * hw])
        gn[:, some] = total
        return carry

    lax.fori_loop(0, width // 512, normed_tile, 0)

    def input_rows(start):
        some = pl.ds(start, 32)
        values = x_ref[some, :].astype(F32)
        grad_in = gn[some, :]
        factor = lax.rsqrt(jnp.mean(values * values, axis=-1, keepdims=True) + EPS)
        scaled = grad_in * vecs_ref[0:1, :]
        inner = jnp.mean(scaled * values, axis=-1, keepdims=True)
        ig_ref[some, :] = gr_ref[some, :] + (
            factor * scaled - values * (factor * factor * factor) * inner
        )
        vec_ref[0:1, :] = vec_ref[0:1, :] + jnp.sum(grad_in * values * factor, axis=0, keepdims=True)

    chunked(tok, input_rows)

    def v_copy(target):
        return to_lane(vec_ref, vz.at[lane], v_send.at[target], v_recv.at[lane], target)

    for step in range(1, LANES):
        v_copy(lax.rem(lane + step, LANES)).start()

    for step in range(1, LANES):
        source = lax.rem(lane + step, LANES)
        to_lane(vz.at[source], vz.at[source], v_send.at[0], v_recv.at[source], source).wait_recv()
    for step in range(1, LANES):
        v_copy(lax.rem(lane + step, LANES)).wait_send()
    total = vec_ref[...]
    for step in range(1, LANES):
        total = total + vz[lax.rem(lane + step, LANES)]
    vd[chips] = total
    swap = to_dp(vd.at[chips], vd.at[chips + 1], vs_send.at[0], vs_recv.at[chips], sibling)
    swap.start()
    swap.wait()
    vd[chip] = vd[chips] + vd[chips + 1]

    def vs_copy(mask):
        return to_dp(
            vd.at[chip], vd.at[chip], vs_send.at[mask], vs_recv.at[chip], 2 * flipped(chip, mask) + core
        )

    for mask in range(1, chips):
        vs_copy(mask).start()
    for mask in range(1, chips):
        c = flipped(chip, mask)
        to_dp(vd.at[c], vd.at[c], vs_send.at[0], vs_recv.at[c], sibling).wait_recv()
    for mask in range(1, chips):
        vs_copy(mask).wait_send()
    total = vd[0]
    for c in range(1, chips):
        total = total + vd[c]
    vec_ref[...] = total

    for step in range(1, LANES):
        other = lax.rem(lane + step, LANES)
        to_lane(zsum, woz_ref.at[:, lane_cols(other, quarter)], zg_send.at[0], zg_recv.at[other], other).wait_recv()
        to_lane(wqz_ref.at[other], wqz_ref.at[other], zq_send.at[0], zq_recv.at[other], other).wait_recv()
        gq_copy(other).wait_send()
        gkv_copy(other).wait_send()
        zr_copy(other).wait_send()
        zg_copy(other).wait_send()
        zq_copy(other).wait_send()
    out_sum.end()
    qkv_sum.end()
    for k in range(len(mats)):
        ff_own(k).wait()
        for mask in range(chips):
            c = flipped(chip, mask)
            ff_pair(k, c).wait_send()
            if mask:
                to_dp(fland.at[k, c], fland.at[k, c], fs_send.at[k, 0], fs_recv.at[k, c], sibling).wait_recv()
                ff_send(k, mask).wait_send()


def back(
    chips, mats, grad_resid, mlp_vec, hidden_in, vecs, qkv, log_sum, cos_row, sin_row, seg_col,
    seg_row, grad_low, grad_att, attended, wq_full, wk_full, wv_full, normed_row, mlp_grads,
):
    tok, width = hidden_in.shape
    row = tok * LANES
    gwid = qkv.shape[1]
    hw = gwid - 2 * HD
    ff = mlp_grads.shape[2]
    own = width // (2 * chips)
    half = width // 2
    anywhere = pl.BlockSpec(memory_space=pl.ANY)
    vmem = pl.BlockSpec(memory_space=pltpu.VMEM)
    dma = pltpu.SemaphoreType.DMA
    shape = jax.ShapeDtypeStruct
    vmem_outs = [
        shape((tok, width), F32),
        shape((8, width), F32),
        shape((own, width), BF16),
        shape((LANES, own, gwid), BF16),
    ]
    hbm_outs = [shape((len(mats), chips, own, ff), BF16)]
    return pl.pallas_call(
        functools.partial(back_kernel, chips, mats),
        out_shape=vmem_outs + hbm_outs,
        in_specs=[vmem] * 10 + [anywhere] * 8,
        out_specs=[vmem] * len(vmem_outs) + [anywhere] * len(hbm_outs),
        scratch_shapes=[
            pltpu.VMEM((tok, width), BF16),
            pltpu.VMEM((width, width + 2 * KV_HEADS * HD), BF16),
            pltpu.VMEM((row, width), BF16),
            pltpu.VMEM((tok, width), BF16),
            pltpu.VMEM((row, hw), BF16),
            pltpu.VMEM((row, HD), F32),
            pltpu.VMEM((row, HD), F32),
            pltpu.VMEM((row, gwid), BF16),
            pltpu.VMEM((tok, LANES * gwid), BF16),
            pltpu.VMEM((hw // HD, 8, row), F32),
            pltpu.VMEM((width, width), BF16),
            pltpu.VMEM((half, width), BF16),
            pltpu.VMEM((half, width), BF16),
            pltpu.VMEM((own, width), BF16),
            pltpu.VMEM((LANES, own, width // LANES), BF16),
            pltpu.VMEM((own, width // LANES), BF16),
            pltpu.VMEM((width, gwid), BF16),
            pltpu.VMEM((half, gwid), BF16),
            pltpu.VMEM((half, gwid), BF16),
            *[pltpu.VMEM((len(mats), chips, own, ff), BF16)] * 3,
            pltpu.VMEM((LANES, 8, width), F32),
            pltpu.VMEM((chips + 2, 8, width), F32),
            pltpu.VMEM((tok, width), F32),
            dma((7,)),
            dma((LANES,)),
            dma((LANES,)),
            dma((LANES,)),
            dma((LANES,)),
            *[dma((chips,))] * 8,
            *[dma((LANES,))] * 6,
            *[dma((len(mats), chips))] * 4,
            dma((2, len(mats), chips)),
            dma((LANES,)),
            dma((LANES,)),
            dma((chips,)),
            dma((chips + 1,)),
        ],
        compiler_params=pltpu.CompilerParams(
            collective_id=2, has_side_effects=True, vmem_limit_bytes=61 * 2**20
        ),
        cost_estimate=pl.CostEstimate(
            flops=20 * row * width * gwid, bytes_accessed=12 * width * ff, transcendentals=row * width
        ),
        name="back",
    )(
        grad_resid, mlp_vec, hidden_in, vecs, qkv, log_sum, cos_row, sin_row, seg_col, seg_row,
        grad_low, grad_att, attended, wq_full, wk_full, wv_full, normed_row, mlp_grads,
    )


def body(
    hidden_in,
    segment_ids,
    position_ids,
    out_grad,
    attn_norm,
    w_query,
    w_key,
    w_value,
    b_query,
    b_key,
    b_value,
    w_out,
    mlp_norm,
    w_gate,
    w_up,
    w_down,
):
    chips = lax.axis_size("dp") // 2
    dp, lane = lax.axis_index("dp"), lax.axis_index("seq")
    local_tok, width = hidden_in.shape
    kv_group = LANES // KV_HEADS
    query_width = HEADS // LANES * HD

    def side_by_side(vectors, step, size):
        return sum(
            lax.pad(v, jnp.zeros((), v.dtype), [(k * step, size - k * step - v.shape[0], 0)])
            for k, v in enumerate(vectors)
        )

    vec = side_by_side((attn_norm, mlp_norm, b_query, b_key, b_value), 2 * HD, 16 * HD).reshape(16, HD)
    ids = side_by_side((position_ids, segment_ids), local_tok, 8 * local_tok).reshape(8, local_tok)
    inv_freq = ROPE_BASE ** (-(np.arange(HD // 2, dtype=np.float32) * np.float32(2.0 / HD)))
    freqs = np.tile(np.concatenate([inv_freq, inv_freq]).astype(np.float32)[None, :], (8, 1))
    (
        resid, mlp_local, vecs, qkv, attended, log_sum, cos_row, sin_row, seg_col, seg_row,
        normed_row, grad_rows, _, _, wo_full, gate_full, up_full, down_full,
    ) = front(
        chips, hidden_in, ids, freqs, out_grad, vec, w_query, w_key, w_value, w_out.T, w_gate, w_up, w_down
    )
    (
        total, grad_resid, mlp_vec, grad_low, grad_att, down_part, _, gate_grads, up_grads, _,
        wq_full, wk_full, wv_full,
    ) = feed_forward(
        chips, mlp_local, grad_rows, gate_full, up_full, down_full, w_query, w_key, w_value, resid, out_grad,
        wo_full, vecs,
    )
    block_out = total.astype(jnp.bfloat16)
    input_grad, vec_grads, out_grad_rows, qkv_grads, down_grads = back(
        chips, (0,), grad_resid, mlp_vec, hidden_in, vecs, qkv, log_sum, cos_row, sin_row, seg_col,
        seg_row, grad_low, grad_att, attended, wq_full, wk_full, wv_full, normed_row, down_part,
    )
    def chip_sum(parts):
        return jnp.sum(parts.astype(jnp.float32), axis=0)

    gate_grads, vec_grads = lax.optimization_barrier((gate_grads, vec_grads))
    gate_grad = chip_sum(gate_grads)
    gate_grad, up_grads = lax.optimization_barrier((gate_grad, up_grads))
    up_grad, down_grad = chip_sum(up_grads), chip_sum(down_grads[0])
    own = width // (2 * chips)
    kv_own = KV_HEADS * HD // (2 * chips)
    query_grad = jnp.concatenate(
        [qkv_grads[k, :, :query_width] for k in range(LANES)], axis=1
    ).astype(jnp.float32)

    def kv_grad(offset):
        parts = qkv_grads[:, :, offset : offset + HD].astype(jnp.float32)
        return jnp.concatenate(
            [
                jnp.sum(parts[k * kv_group : (k + 1) * kv_group], axis=0)
                for k in range(KV_HEADS)
            ],
            axis=1,
        )

    def own_vec(k, size):
        return lax.dynamic_slice(vec_grads, (k, dp * size), (1, size))[0]

    return (
        block_out,
        input_grad,
        own_vec(0, own),
        query_grad,
        kv_grad(query_width),
        kv_grad(query_width + HD),
        own_vec(2, own),
        own_vec(3, kv_own),
        own_vec(4, kv_own),
        out_grad_rows.astype(jnp.float32).T,
        own_vec(1, own),
        gate_grad,
        up_grad,
        down_grad,
    )


def solution(mesh):
    return jax.shard_map(
        body,
        mesh=mesh,
        in_specs=(
            P(("dp", "seq"), None),
            P(("dp", "seq")),
            P(("dp", "seq")),
            P(("dp", "seq"), None),
            P("dp"),
            P("dp", None),
            P("dp", None),
            P("dp", None),
            P("dp"),
            P("dp"),
            P("dp"),
            P(None, "dp"),
            P("dp"),
            P("dp", "seq"),
            P("dp", "seq"),
            P("dp", "seq"),
        ),
        out_specs=(
            P(("dp", "seq"), None),
            P(("dp", "seq"), None),
            P("dp"),
            P("dp", None),
            P("dp", None),
            P("dp", None),
            P("dp"),
            P("dp"),
            P("dp"),
            P(None, "dp"),
            P("dp"),
            P("dp", "seq"),
            P("dp", "seq"),
            P("dp", "seq"),
        ),
        check_vma=False,
    )
```

```python
import functools

import jax
import jax.numpy as jnp
import numpy as np
from jax import lax
from jax.experimental import pallas as pl
from jax.experimental.pallas import tpu as pltpu
from jax.sharding import PartitionSpec as P

HEADS = 12
KV_HEADS = 2
HD = 128
EPS = 1e-06
ROPE_BASE = 1000000.0
NEG_FILL = -1e30
MESH_ID = pl.DeviceIdType.MESH
LANES = 4
BF16 = jnp.bfloat16
F32 = jnp.float32


def nn(left, right):
    return jnp.dot(left, right, preferred_element_type=F32)


def nt(left, right):
    return lax.dot_general(left, right, (((1,), (1,)), ((), ())), preferred_element_type=F32)


def rows_of(index, size):
    return pl.ds(pl.multiple_of(index * size, size), size)


def digit(codes, lane):
    return lax.rem(lax.shift_right_logical(jnp.int32(codes), 2 * lane), 4)


def order_of(step, lane):
    tables = ((0, 1, 2, 3), (1, 0, 2, 3), (2, 3, 1, 0), (3, 2, 1, 0))
    codes = [sum(tables[k][i] * 4**k for k in range(LANES)) for i in range(LANES)]
    out = digit(codes[0], lane)
    for i in range(1, LANES):
        out = jnp.where(step == i, digit(codes[i], lane), out)
    return out


def flipped(chip, mask):
    out = chip
    for bit in range(8):
        if mask >> bit & 1:
            out = out + (1 - 2 * lax.rem(chip // 2**bit, 2)) * 2**bit
    return out


def meet_all(chips):
    dp, lane = lax.axis_index("dp"), lax.axis_index("seq")
    chip, core = dp // 2, lax.rem(dp, 2)
    barrier = pltpu.get_barrier_semaphore()
    for mask in range(1, chips):
        pl.semaphore_signal(
            barrier, 1, device_id={"dp": 2 * flipped(chip, mask) + core}, device_id_type=MESH_ID
        )
    pl.semaphore_signal(barrier, 1, device_id={"dp": 2 * chip + 1 - core}, device_id_type=MESH_ID)
    for step in range(1, LANES):
        pl.semaphore_signal(
            barrier, 1, device_id={"seq": lax.rem(lane + step, LANES)}, device_id_type=MESH_ID
        )
    pl.semaphore_wait(barrier, chips + LANES - 1)


class Gather:
    def __init__(self, chips, shard, full, send, fwd, recv, half_send, half_recv, halves=True):
        self.dp = lax.axis_index("dp")
        self.chip, self.core = self.dp // 2, lax.rem(self.dp, 2)
        self.chips, self.shard, self.full = chips, shard, full
        self.send, self.fwd, self.recv = send, fwd, recv
        self.half_send, self.half_recv = half_send, half_recv
        self.rows = shard.shape[0]
        self.square = chips == 4 and halves
        self.masks = (1, 2) if self.square else tuple(range(1, chips))

    def device(self, mask, other=False):
        return 2 * flipped(self.chip, mask) + (1 - self.core if other else self.core)

    def to(self, src, dst, send, recv, target):
        return pltpu.make_async_remote_copy(
            src, dst, send, recv, device_id={"dp": target}, device_id_type=MESH_ID
        )

    def own_copy(self, mask):
        return self.to(
            self.shard, self.full.at[rows_of(self.dp, self.rows)], self.send.at[mask],
            self.recv.at[self.dp], self.device(mask) if mask else self.device(0, True),
        )

    def hand_on(self, source):
        part = self.full.at[rows_of(source, self.rows)]
        return self.to(part, part, self.fwd.at[source // 2], self.recv.at[source], self.device(0, True))

    def half_copy(self, source, half, target):
        size = self.rows // 2
        part = self.full.at[rows_of(2 * source + half, size)]
        return self.to(part, part, self.half_send.at[half], self.half_recv.at[half], target)

    def begin(self):
        for mask in self.masks + (0,):
            self.own_copy(mask).start()

    def relay(self):
        for mask in self.masks:
            source = self.device(mask)
            self.hand_on(source).wait_recv()
            if self.square:
                self.half_copy(source, mask - 1, self.device(3 - mask)).start()
            self.hand_on(source).start()

    def relay_across(self):
        if self.square:
            source = self.device(3)
            for half in range(2):
                self.half_copy(source, half, self.device(1)).wait_recv()
            self.hand_on(source).start()

    def end(self):
        for mask in range(self.chips):
            self.hand_on(self.device(mask, True)).wait_recv()
        for mask in self.masks + (0,):
            self.own_copy(mask).wait_send()
        for mask in range(1, self.chips):
            self.hand_on(self.device(mask)).wait_send()
        if self.square:
            for half in range(2):
                self.half_copy(self.device(half + 1), half, self.device(2 - half)).wait_send()


def spread(out, shards, devices, first, size, count):
    width = out.shape[1]
    column = lax.broadcasted_iota(jnp.int32, (HD, width), 1)
    value = lax.broadcasted_iota(jnp.int32, (HD, width), 0)
    owner = lax.broadcasted_iota(jnp.int32, (devices, width), 1) // size
    mine = owner == lax.broadcasted_iota(jnp.int32, (devices, width), 0)
    for n in range(count):
        total = jnp.zeros((devices, width), F32)
        for part in range(2 if size > HD else 1):
            place = (lax.rem(column, size) == value + part * HD).astype(F32).astype(BF16)
            row = 2 * (first + n) + part
            rows = jnp.concatenate([shards[k * 16 : k * 16 + 16, :][row : row + 1] for k in range(devices)], axis=0)
            total = total + nn(rows, place)
        out[first + n : first + n + 1, :] = jnp.sum(jnp.where(mine, total, 0.0), axis=0, keepdims=True)


def front_kernel(
    chips,
    x_hbm, ids_hbm, freq_ref, og_hbm, vec_hbm, wq_hbm, wk_hbm, wv_hbm, wo_hbm, wg_hbm, wu_hbm, wd_hbm,
    resid_ref, mlp_ref, vecs_ref, qkv_ref, att_ref, lse_ref, cos_ref, sin_ref, segc_ref, segr_ref,
    nrm_hbm, ogf, vecf, wqkvf, wof, wgf, wuf, wdf,
    xb, ids, nrm, wqkv, wo, vecb, ab, own_vec, own_qkv, own_wo, own_gate, own_up, own_down, own_og,
    load_sem, dp_send, dp_fwd, dp_recv, half_send, half_recv, x_send, x_recv, i_send, i_recv, o_send, o_recv, a_send, a_recv,
):
    dp, lane = lax.axis_index("dp"), lax.axis_index("seq")
    chip, core = dp // 2, lax.rem(dp, 2)
    sibling = 2 * chip + 1 - core
    tok, width = x_hbm.shape
    heads = qkv_ref.shape[1] // HD - 2
    has_left, has_right = lane > 0, lane < LANES - 1
    left, right = jnp.maximum(lane - 1, 0), jnp.minimum(lane + 1, LANES - 1)
    here = rows_of(lane, tok)

    first_loads = [
        pltpu.make_async_copy(x_hbm, xb.at[here], load_sem.at[0]),
        pltpu.make_async_copy(ids_hbm, ids.at[lane], load_sem.at[1]),
        pltpu.make_async_copy(og_hbm, own_og, load_sem.at[2]),
    ]
    shards = (vec_hbm, own_qkv, wo_hbm, wg_hbm, wu_hbm, wd_hbm)
    fulls = (vecf, wqkvf, wof, wgf, wuf, wdf)
    own_parts = (own_vec, own_qkv, own_wo, own_gate, own_up, own_down)
    own_loads = [
        pltpu.make_async_copy(s, v, load_sem.at[3 + k])
        for k, (s, v) in enumerate(zip(shards, own_parts))
        if k != 1
    ]
    kv_at = pl.multiple_of(lane * KV_HEADS // LANES * HD, HD)
    qkv_loads = [
        pltpu.make_async_copy(
            wq_hbm.at[:, pl.ds(pl.multiple_of(lane * heads * HD, HD), heads * HD)],
            own_qkv.at[:, pl.ds(0, heads * HD)], load_sem.at[4],
        ),
        pltpu.make_async_copy(
            wk_hbm.at[:, pl.ds(kv_at, HD)], own_qkv.at[:, pl.ds(heads * HD, HD)], load_sem.at[13]
        ),
        pltpu.make_async_copy(
            wv_hbm.at[:, pl.ds(kv_at, HD)], own_qkv.at[:, pl.ds((heads + 1) * HD, HD)], load_sem.at[14]
        ),
    ]
    own_copies = [
        pltpu.make_async_copy(v, f.at[rows_of(dp, v.shape[0])], load_sem.at[3 + k])
        for k, (v, f) in enumerate(zip(own_parts, fulls))
    ]
    og_copy = pltpu.make_async_copy(own_og, ogf.at[here], load_sem.at[2])
    for copy in qkv_loads + first_loads + own_loads:
        copy.start()
    lse_ref[...] = jnp.zeros_like(lse_ref)
    meet_all(chips)

    gathers = [
        Gather(
            chips, shard, full, dp_send.at[k], dp_fwd.at[k], dp_recv.at[k], half_send.at[k], half_recv.at[k], k > 0
        )
        for k, (shard, full) in enumerate(zip(shards, fulls))
    ]

    def line_copy(buf, send, recv, block, way):
        part = buf(block)
        return pltpu.make_async_remote_copy(
            part, part, send.at[way, block], recv.at[block],
            device_id={"seq": right if way == 0 else left}, device_id_type=MESH_ID,
        )

    x_line = (lambda b: xb.at[rows_of(b, tok)], x_send, x_recv)
    i_line = (lambda b: ids.at[b], i_send, i_recv)
    o_line = (lambda b: ogf.at[rows_of(b, tok)], o_send, o_recv)

    def line_begin(*lines):
        @pl.when(has_right)
        def _():
            for line in lines:
                line_copy(*line, lane, 0).start()

        @pl.when(has_left)
        def _():
            for line in lines:
                line_copy(*line, lane, 1).start()

    def line_step(step, *lines):
        @pl.when(lane - step >= 0)
        def _():
            block = jnp.maximum(lane - step, 0)
            for line in lines:
                line_copy(*line, block, 0).wait_recv()

            @pl.when(has_right)
            def _():
                for line in lines:
                    line_copy(*line, block, 0).start()

        @pl.when(lane + step < LANES)
        def _():
            block = jnp.minimum(lane + step, LANES - 1)
            for line in lines:
                line_copy(*line, block, 1).wait_recv()

            @pl.when(has_left)
            def _():
                for line in lines:
                    line_copy(*line, block, 1).start()

    def line_end(*lines):
        for block in range(LANES):
            @pl.when(jnp.logical_and(has_right, block <= lane))
            def _(block=block):
                for line in lines:
                    line_copy(*line, block, 0).wait_send()

            @pl.when(jnp.logical_and(has_left, block >= lane))
            def _(block=block):
                for line in lines:
                    line_copy(*line, block, 1).wait_send()

    first_loads[0].wait()
    first_loads[1].wait()
    line_begin(i_line, x_line)
    with jax.named_scope("first_sends"):
        gathers[0].begin()
        for copy in qkv_loads:
            copy.wait()
        gathers[1].begin()
    for load in own_loads:
        load.wait()
    for copy in own_copies:
        copy.start()
    first_loads[2].wait()
    og_copy.start()
    with jax.named_scope("first_relay"):
        gathers[0].relay()
        gathers[1].relay()
    gathers[2].begin()
    gathers[3].begin()
    with jax.named_scope("first_end"):
        gathers[1].relay_across()
        for copy in own_copies + [og_copy]:
            copy.wait()
        gathers[0].end()
        gathers[1].end()
    vec_load = pltpu.make_async_copy(vecf, vecb, load_sem.at[9])
    wqkv_load = pltpu.make_async_copy(wqkvf, wqkv, load_sem.at[10])
    vec_load.start()
    wqkv_load.start()
    vec_load.wait()
    devices = 2 * chips
    spread(vecs_ref, vecb, devices, 0, width // devices, 3)
    spread(vecs_ref, vecb, devices, 3, KV_HEADS * HD // devices, 2)
    wqkv_load.wait()
    bias = jnp.concatenate(
        [
            vecs_ref[2:3, pl.ds(pl.multiple_of(lane * heads * HD, HD), heads * HD)],
            vecs_ref[3:4, pl.ds(pl.multiple_of(lane * KV_HEADS // LANES * HD, HD), HD)],
            vecs_ref[4:5, pl.ds(pl.multiple_of(lane * KV_HEADS // LANES * HD, HD), HD)],
        ],
        axis=1,
    )
    lane_sign = jnp.where(lax.broadcasted_iota(jnp.int32, (1, HD), 1) < HD // 2, -1.0, 1.0)

    def block_step(step, carry):
        block = order_of(step, lane)
        mine = rows_of(block, tok)
        id_rows = ids[block].astype(F32)
        segr_ref[:, mine] = jnp.broadcast_to(id_rows[1:2, :], (8, tok))
        segc_ref[mine, :] = jnp.broadcast_to(id_rows[1:2, :], (HD, tok)).T
        angles = jnp.broadcast_to(id_rows[0:1, :], (HD, tok)).T * freq_ref[0:1, :]
        cos_ref[mine, :] = jnp.cos(angles)
        sin_ref[mine, :] = jnp.sin(angles) * lane_sign

        def norm(i, c):
            some = pl.ds(pl.multiple_of(block * tok + i * 32, 32), 32)
            x = xb[some, :].astype(F32)
            factor = lax.rsqrt(jnp.mean(x * x, axis=-1, keepdims=True) + EPS)
            nrm[some, :] = (x * factor * vecs_ref[0:1, :]).astype(BF16)
            return c

        lax.fori_loop(0, tok // 32, norm, 0)

        @pl.when(step < LANES - 1)
        def _():
            with jax.named_scope("row_arrival"):
                @pl.when(step == LANES - 2)
                def _():
                    line_begin(o_line)

                line_step(step + 1, i_line, x_line)

        @pl.when(step == 1)
        def _():
            with jax.named_scope("w_out_relay"):
                gathers[2].relay()
            gathers[4].begin()

        pre = nn(nrm[mine, :], wqkv[...]) + bias
        cosine, sine = cos_ref[mine, :], sin_ref[mine, :]
        for h in range(heads + 1):
            cols = slice(h * HD, (h + 1) * HD)
            part = pre[:, cols]
            qkv_ref[mine, cols] = (part * cosine + pltpu.roll(part, HD // 2, 1) * sine).astype(BF16)
        cols = slice((heads + 1) * HD, (heads + 2) * HD)
        qkv_ref[mine, cols] = pre[:, cols].astype(BF16)
        return carry

    lax.fori_loop(0, LANES, block_step, 0)
    nrm_copy = pltpu.make_async_copy(nrm, nrm_hbm, load_sem.at[11])
    nrm_copy.start()
    with jax.named_scope("w_out_across"):
        gathers[2].relay_across()
    with jax.named_scope("gate_relay"):
        gathers[3].relay()
    gathers[5].begin()

    def att_send(i):
        cols = pl.ds(pl.multiple_of(lane * heads * HD, HD), heads * HD)
        return pltpu.make_async_remote_copy(
            ab.at[pl.ds(i * tok, tok)], att_ref.at[:, cols], a_send.at[i], a_recv.at[lane],
            device_id={"seq": i}, device_id_type=MESH_ID,
        )

    sub = 128
    for i in (3, 0, 2, 1):
        keys = (i + 1) * tok

        def att_step(t, carry, i=i, keys=keys):
            h = t // (tok // sub)
            start = i * tok + lax.rem(t, tok // sub) * sub
            some = pl.ds(pl.multiple_of(start, sub), sub)
            cols = pl.ds(pl.multiple_of(h * HD, HD), HD)
            scores = nt(qkv_ref[some, cols], qkv_ref[0:keys, heads * HD : (heads + 1) * HD]) * HD**-0.5
            same = segc_ref[some, 0:1] == segr_ref[0:1, 0:keys]
            behind = (
                lax.broadcasted_iota(jnp.int32, (sub, keys), 0) + start
                >= lax.broadcasted_iota(jnp.int32, (sub, keys), 1)
            )
            scores = jnp.where(jnp.logical_and(same, behind), scores, NEG_FILL)
            peak = jnp.max(scores, axis=-1, keepdims=True)
            exps = jnp.exp(scores - peak)
            totals = jnp.sum(exps, axis=-1, keepdims=True)
            prob = (exps * (1.0 / totals)).astype(BF16)
            ab[some, cols] = nn(prob, qkv_ref[0:keys, (heads + 1) * HD :]).astype(BF16)
            at_head = lax.broadcasted_iota(jnp.int32, (sub, HD), 1) == h
            lse_ref[some, :] = jnp.where(at_head, peak + jnp.log(totals), lse_ref[some, :])
            return carry

        with jax.named_scope("attention"):
            lax.fori_loop(0, heads * (tok // sub), att_step, 0)

        @pl.when(lane != i)
        def _(i=i):
            att_send(i).start()

    with jax.named_scope("cotangent_1"):
        line_step(1, o_line)
    own_cols = pl.ds(pl.multiple_of(lane * heads * HD, HD), heads * HD)
    att_ref[:, own_cols] = ab[here, :]
    with jax.named_scope("gate_across"):
        gathers[3].relay_across()
    with jax.named_scope("w_out_end"):
        gathers[2].end()
    wo_load = pltpu.make_async_copy(wof, wo, load_sem.at[12])
    wo_load.start()
    wo_load.wait()
    for i in range(LANES):
        @pl.when(lane != i)
        def _(i=i):
            pltpu.make_async_remote_copy(
                ab.at[pl.ds(0, tok)], att_ref.at[:, pl.ds(i * heads * HD, heads * HD)],
                a_send.at[0], a_recv.at[i], device_id={"seq": i}, device_id_type=MESH_ID,
            ).wait_recv()

    def out_tile(t, carry):
        cols = pl.ds(pl.multiple_of(t * 512, 512), 512)
        resid_ref[:, cols] = xb[here, cols].astype(F32) + nt(att_ref[...], wo[cols, :])
        return carry

    with jax.named_scope("out_project"):
        lax.fori_loop(0, width // 512, out_tile, 0)

    def mlp_norm(i, carry):
        some = pl.ds(pl.multiple_of(i * 32, 32), 32)
        x = resid_ref[some, :]
        factor = lax.rsqrt(jnp.mean(x * x, axis=-1, keepdims=True) + EPS)
        mlp_ref[some, :] = (x * factor * vecs_ref[1:2, :]).astype(BF16)
        return carry

    lax.fori_loop(0, tok // 32, mlp_norm, 0)
    with jax.named_scope("cotangent_2"):
        line_step(2, o_line)
    with jax.named_scope("up_down_relay"):
        gathers[4].relay()
        gathers[5].relay()
    with jax.named_scope("cotangent_3"):
        line_step(3, o_line)
    with jax.named_scope("weights_end"):
        gathers[4].relay_across()
        gathers[5].relay_across()
        for which in (3, 4, 5):
            gathers[which].end()
    nrm_copy.wait()
    line_end(i_line, x_line, o_line)
    for i in range(LANES):
        @pl.when(lane != i)
        def _(i=i):
            att_send(i).wait_send()


def front(chips, hidden_in, ids, freqs, out_grad, vec, w_query, w_key, w_value, wo, w_gate, w_up, w_down):
    tok, width = hidden_in.shape
    row = tok * LANES
    qkv_width = w_query.shape[1] // LANES + 2 * HD
    own_qkv = jax.ShapeDtypeStruct((w_query.shape[0], qkv_width), BF16)
    ff = w_gate.shape[1]
    anywhere = pl.BlockSpec(memory_space=pl.ANY)
    vmem = pl.BlockSpec(memory_space=pltpu.VMEM)
    dma = pltpu.SemaphoreType.DMA
    shape = jax.ShapeDtypeStruct
    vmem_outs = [
        shape((tok, width), F32),
        shape((tok, width), BF16),
        shape((16, width), F32),
        shape((row, qkv_width), BF16),
        shape((tok, width), BF16),
        shape((row, HD), F32),
        shape((row, HD), F32),
        shape((row, HD), F32),
        shape((row, HD), F32),
        shape((8, row), F32),
    ]
    hbm_outs = [
        shape((row, width), BF16),
        shape((row, width), BF16),
        shape((2 * chips * 16, HD), BF16),
        shape((width, qkv_width), BF16),
        shape((width, width), BF16),
        shape((width, ff), BF16),
        shape((width, ff), BF16),
        shape((width, ff), BF16),
    ]
    return pl.pallas_call(
        functools.partial(front_kernel, chips),
        out_shape=vmem_outs + hbm_outs,
        in_specs=[anywhere, anywhere, vmem] + [anywhere] * 9,
        out_specs=[vmem] * len(vmem_outs) + [anywhere] * len(hbm_outs),
        scratch_shapes=[
            pltpu.VMEM((row, width), BF16),
            pltpu.VMEM((LANES, 8, tok), jnp.int32),
            pltpu.VMEM((row, width), BF16),
            pltpu.VMEM((width, qkv_width), BF16),
            pltpu.VMEM((width, width), BF16),
            pltpu.VMEM((2 * chips * 16, HD), BF16),
            pltpu.VMEM((row, qkv_width - 2 * HD), BF16),
            *[pltpu.VMEM(part.shape, BF16) for part in (vec, own_qkv, wo, w_gate, w_up, w_down, out_grad)],
            dma((15,)),
            dma((6, chips)),
            dma((6, chips)),
            dma((6, 2 * chips)),
            dma((6, 2)),
            dma((6, 2)),
            dma((2, LANES)),
            dma((LANES,)),
            dma((2, LANES)),
            dma((LANES,)),
            dma((2, LANES)),
            dma((LANES,)),
            dma((LANES,)),
            dma((LANES,)),
        ],
        compiler_params=pltpu.CompilerParams(
            collective_id=1, has_side_effects=True, vmem_limit_bytes=56 * 2**20
        ),
        cost_estimate=pl.CostEstimate(
            flops=10 * row * width * qkv_width, bytes_accessed=12 * width * ff, transcendentals=row * width
        ),
        name="front",
    )(hidden_in, ids, freqs, out_grad, vec, w_query, w_key, w_value, wo, w_gate, w_up, w_down)


def ff_kernel(
    chips,
    x_hbm, og_hbm, wg_hbm, wu_hbm, wd_hbm, wq_hbm, wk_hbm, wv_hbm, resid_hbm, own_og_hbm, wo_hbm, vecs_ref,
    mo_ref, gm_ref, vec_ref, grl_hbm, ga_hbm, gw_hbm, fpair, fland_gate, fland_up, fmid, wqf, wkf, wvf,
    xb, og, wg, wu, wd, hid, gg, gu, pb, rb, rf,
    load_sem, ag_send, ag_recv, rb_send, rb_recv, rf_send, rf_recv, out_sem,
    dp_send, dp_fwd, dp_recv, half_send, half_recv, own_sem, fp_send, fp_recv, fk_sem, fs_send, fs_recv, fl_sem,
    p1_send, p1_recv, p2_send, p2_recv, a_send, a_recv, late_sem,
):
    lane, dp = lax.axis_index("seq"), lax.axis_index("dp")
    chip, core = dp // 2, lax.rem(dp, 2)
    tok, width = x_hbm.shape
    units = wg_hbm.shape[1]
    tile = 512
    full_tiles = units // tile
    tail = units - full_tiles * tile
    wtile = 384
    pieces = width // tile
    has_left, has_right = lane > 0, lane < LANES - 1
    is_end = jnp.logical_or(lane == 0, lane == LANES - 1)
    is_mid = jnp.logical_not(is_end)
    left, right = jnp.maximum(lane - 1, 0), jnp.minimum(lane + 1, LANES - 1)

    loads = [
        pltpu.make_async_copy(src, dst, load_sem.at[k])
        for k, (src, dst) in enumerate(
            ((wg_hbm, wg), (wu_hbm, wu), (wd_hbm, wd), (og_hbm, og))
        )
    ]
    own = pltpu.make_async_copy(x_hbm, xb.at[rows_of(lane, tok)], load_sem.at[4])
    own.start()
    for copy in loads:
        copy.start()

    attn_shards = ((wq_hbm, wqf), (wk_hbm, wkf), (wv_hbm, wvf))
    attn_loads, attn_own, begin = [], [], 0
    for k, (shard, full) in enumerate(attn_shards):
        kept = hid.at[pl.ds(0, shard.shape[0]), pl.ds(begin, shard.shape[1])]
        attn_loads.append(pltpu.make_async_copy(shard, kept, own_sem.at[k]))
        attn_own.append(pltpu.make_async_copy(kept, full.at[rows_of(dp, shard.shape[0])], own_sem.at[k]))
        begin += shard.shape[1]
    resid_load = pltpu.make_async_copy(resid_hbm, mo_ref, late_sem.at[0])
    resid_load.start()
    vec_ref[...] = jnp.zeros_like(vec_ref)
    for copy in attn_loads:
        copy.start()
    meet_all(chips)
    gathers = [
        Gather(
            chips, shard, full, dp_send.at[k], dp_fwd.at[k], dp_recv.at[k], half_send.at[k], half_recv.at[k]
        )
        for k, (shard, full) in enumerate(attn_shards)
    ]
    own.wait()

    def gather_copy(block, way):
        part = xb.at[rows_of(block, tok)]
        return pltpu.make_async_remote_copy(
            part, part, ag_send.at[way, block], ag_recv.at[block],
            device_id={"seq": right if way == 0 else left}, device_id_type=MESH_ID,
        )

    @pl.when(has_right)
    def _():
        gather_copy(lane, 0).start()

    @pl.when(has_left)
    def _():
        gather_copy(lane, 1).start()

    def arrivals(step):
        @pl.when(lane - step >= 0)
        def _():
            block = jnp.maximum(lane - step, 0)
            gather_copy(block, 0).wait_recv()

            @pl.when(has_right)
            def _():
                gather_copy(block, 0).start()

        @pl.when(lane + step < LANES)
        def _():
            block = jnp.minimum(lane + step, LANES - 1)
            gather_copy(block, 1).wait_recv()

            @pl.when(has_left)
            def _():
                gather_copy(block, 1).start()

    def cols_of(piece):
        return pl.ds(pl.multiple_of(piece * tile, tile), tile)

    def sum_send(part, landing, send, recv, block, piece):
        goes_left = block < lane
        target = jnp.where(goes_left, left, right)
        slot = jnp.where(jnp.logical_and(goes_left, target == block), LANES, block)
        return pltpu.make_async_remote_copy(
            part.at[rows_of(block, tok), cols_of(piece)], landing.at[rows_of(slot, tok), cols_of(piece)],
            send.at[block, piece], recv.at[slot, piece],
            device_id={"seq": target}, device_id_type=MESH_ID,
        )

    def sum_arrived(part, landing, send, recv, slot, piece):
        there = landing.at[rows_of(slot, tok), cols_of(piece)]
        pltpu.make_async_remote_copy(
            there, there, send.at[0, piece], recv.at[slot, piece], device_id={"seq": left}, device_id_type=MESH_ID
        ).wait_recv()

    def sum_pass(part, landing, send, recv, block):
        @pl.when(is_mid)
        def _():
            def one(piece, c):
                sum_arrived(part, landing, send, recv, block, piece)

                def add(i, carry):
                    mine = pl.ds(pl.multiple_of(block * tok + i * 64, 64), 64)
                    cols = cols_of(piece)
                    part[mine, cols] = part[mine, cols] + landing[mine, cols]
                    return carry

                lax.fori_loop(0, tok // 64, add, 0)
                sum_send(part, landing, send, recv, block, piece).start()
                return c

            lax.fori_loop(0, pieces, one, 0)

    def sum_last(part, landing, send, recv, out, onto=False):
        def begin(i, carry):
            here = pl.ds(pl.multiple_of(i * 32, 32), 32)
            mine = pl.ds(pl.multiple_of(lane * tok + i * 32, 32), 32)
            own_part = part[mine, :width].astype(F32)
            out[here, :] = out[here, :] + own_part if onto else own_part
            return carry

        lax.fori_loop(0, tok // 32, begin, 0)

        def take(slot):
            def one(piece, c):
                sum_arrived(part, landing, send, recv, slot, piece)

                def add(i, carry):
                    here = pl.ds(pl.multiple_of(i * 64, 64), 64)
                    there = pl.ds(pl.multiple_of(slot * tok + i * 64, 64), 64)
                    cols = cols_of(piece)
                    out[here, cols] = out[here, cols] + landing[there, cols].astype(F32)
                    return carry

                lax.fori_loop(0, tok // 64, add, 0)
                return c

            lax.fori_loop(0, pieces, one, 0)

        @pl.when(has_left)
        def _():
            take(lane)

        @pl.when(has_right)
        def _():
            take(jnp.int32(LANES))

    back = (pb, rb, rb_send, rb_recv)
    ahead = (og, rf, rf_send, rf_recv)
    for gather in gathers:
        gather.begin()
    for load, copy in zip(attn_loads, attn_own):
        load.wait()
        copy.start()
    with jax.named_scope("weights_load"):
        for copy in loads + attn_own:
            copy.wait()

    def down_part(block):
        mine = rows_of(block, tok)

        def down_tile(t, c):
            cols = cols_of(t)
            og[mine, cols] = nt(hid[mine, :], wd[cols, :]).astype(BF16)
            return c

        lax.fori_loop(0, pieces, down_tile, 0)

    def block_step(step, carry):
        block = order_of(step, lane)
        mine = rows_of(block, tok)

        def act(cols):
            gate = nn(xb[mine, :], wg[:, cols])
            up = nn(xb[mine, :], wu[:, cols])
            grad = nn(og[mine, :], wd[:, cols])
            sig = jax.nn.sigmoid(gate)
            silu = gate * sig
            hid[mine, cols] = (silu * up).astype(BF16)
            gg[mine, cols] = (grad * up * sig * (1.0 + gate * (1.0 - sig))).astype(BF16)
            gu[mine, cols] = (grad * silu).astype(BF16)

        def act_tile(t, c):
            act(pl.ds(pl.multiple_of(t * tile, tile), tile))
            return c

        with jax.named_scope("activations"):
            lax.fori_loop(0, full_tiles, act_tile, 0)
            if tail:
                act(pl.ds(full_tiles * tile, tail))

        @pl.when(step < LANES - 2)
        def _():
            with jax.named_scope("row_arrival"):
                arrivals(step + 1)

        @pl.when(step == 1)
        def _():
            with jax.named_scope("attn_relay"):
                for gather in gathers:
                    gather.relay()

        @pl.when(step == 2)
        def _():
            with jax.named_scope("attn_across"):
                for gather in gathers:
                    gather.relay_across()

        def back_tile(t, c):
            cols = pl.ds(pl.multiple_of(t * tile, tile), tile)
            pb[mine, cols] = (nt(gg[mine, :], wg[cols, :]) + nt(gu[mine, :], wu[cols, :])).astype(BF16)

            @pl.when(jnp.logical_and(is_end, step > 0))
            def _():
                sum_send(*back, block, t).start()

            return c

        with jax.named_scope("input_grad_part"):
            lax.fori_loop(0, width // tile, back_tile, 0)

        @pl.when(step < LANES - 1)
        def _():
            down_part(block)

        @pl.when(step == LANES - 2)
        def _():
            with jax.named_scope("row_arrival"):
                arrivals(LANES - 1)


        return carry

    lax.fori_loop(0, LANES, block_step, 0)

    wtiles = width // wtile
    part_rows = width // (2 * chips)
    tile_chips = wtile // (2 * part_rows)

    square = chips == 4
    fland = (fland_gate, fland_up)
    half = part_rows // 2

    def tile_at(step):
        base, mask = chip // (chips // wtiles), wtiles - 1 - step
        return lax.rem(base + mask, 2) + 2 * lax.rem(base // 2 + mask // 2, 2)

    def held(which, c):
        return rows_of(which * chips + c, part_rows)

    def pair_send(which, c, r):
        theirs = pl.ds(pl.multiple_of(which * wtile + (2 * r + 1 - core) * part_rows, 16), part_rows)
        return pltpu.make_async_remote_copy(
            wu.at[theirs], fpair.at[which, c], fp_send.at[which, c], fp_recv.at[which, c],
            device_id={"dp": 2 * chip + 1 - core}, device_id_type=MESH_ID,
        )

    def pair_keep(which, c, r):
        mine = pl.ds(pl.multiple_of(which * wtile + (2 * r + core) * part_rows, 16), part_rows)
        return pltpu.make_async_copy(wu.at[mine], wg.at[held(which, c)], fk_sem.at[which, c])

    def to_chip(src, dst, send, recv, mask):
        return pltpu.make_async_remote_copy(
            src, dst, send, recv, device_id={"dp": 2 * flipped(chip, mask) + core}, device_id_type=MESH_ID
        )

    def chip_keep(which):
        return pltpu.make_async_copy(
            wg.at[held(which, chip)], fland[which].at[0], fl_sem.at[which]
        )

    def chip_send(which, mask):
        return to_chip(
            wg.at[held(which, flipped(chip, mask))], fland[which].at[mask], fs_send.at[which, mask],
            fs_recv.at[which, mask], mask,
        )

    def part_of(which, mask, upper):
        return wg.at[pl.ds(pl.multiple_of((which * chips + flipped(chip, mask)) * part_rows + upper * half, 16), half)]

    def first_hop(which, mask, upper):
        if mask == 3:
            landing = fmid.at[which, upper]
        else:
            landing = fland[which].at[1, pl.ds(upper * half, half)]
        k = 2 * (mask == 3) + upper
        return to_chip(part_of(which, mask, upper), landing, p1_send.at[which, k], p1_recv.at[which, k], 1 + upper)

    def second_hop(which, upper):
        mask = 2 - upper
        return to_chip(
            part_of(which, mask, upper), fland[which].at[2, pl.ds(upper * half, half)],
            p2_send.at[which, upper], p2_recv.at[which, upper], mask,
        )

    def load_slot(which):
        return wu.at[pl.ds(3 * wtile + which * part_rows, part_rows)]

    def add_in(which, first, rows):
        def add(i, carry):
            mine = pl.ds(pl.multiple_of(first + i * 16, 16), 16)
            other = pl.ds(pl.multiple_of(3 * wtile + which * part_rows + i * 16, 16), 16)
            wg[mine, :] = wg[mine, :] + wu[other, :]
            return carry

        lax.fori_loop(0, rows // 16, add, 0)

    def pass_halves(upper):
        arrived = []
        for which in range(2):
            first_hop(which, 3, upper).wait_recv()
            arrived.append(
                pltpu.make_async_copy(
                    fmid.at[which, upper], wu.at[pl.ds(3 * wtile + which * part_rows, half)], load_sem.at[which]
                )
            )
            arrived[which].start()
        for which in range(2):
            arrived[which].wait()
            c = flipped(chip, 2 - upper)
            add_in(which, (which * chips + c) * part_rows + upper * half, half)
            second_hop(which, upper).start()

    def pair_load(which, c):
        return pltpu.make_async_copy(fpair.at[which, c], load_slot(which), load_sem.at[which])

    def load_pairs(step, r=0):
        for which in range(2):
            c = tile_at(step) * tile_chips + r
            pair_send(which, c, r).wait_recv()
            pair_load(which, c).start()

    def add_pairs(step):
        k = tile_at(step)
        for r in range(tile_chips):
            c = k * tile_chips + r
            if r:
                load_pairs(step, r)
            for which in range(2):
                pair_keep(which, c, r).wait()
                pair_load(which, c).wait()
                add_in(which, (which * chips + c) * part_rows, part_rows)
                if not square:
                    continue
                if step == 0:
                    first_hop(which, 3, 0).start()
                    first_hop(which, 3, 1).start()
                elif step == 1:
                    first_hop(which, 2, 1).start()
                elif step == 2:
                    first_hop(which, 1, 0).start()
                else:
                    chip_keep(which).start()

    def product(stage_ref, stage, lhs, rhs):
        def tile_of(cols):
            stage_ref[stage, cols] = nn(wu[lhs], rhs[:, cols]).astype(BF16)

        def one(t, c):
            tile_of(pl.ds(pl.multiple_of(t * tile, tile), tile))
            return c

        lax.fori_loop(0, full_tiles, one, 0)
        if tail:
            tile_of(pl.ds(full_tiles * tile, tail))

    turned = (pl.ds(2 * wtile, wtile), pl.ds(0, LANES * tok))

    def grad_tile(step):
        k = tile_at(step)
        if step:
            for which in range(2):
                for r in range(tile_chips):
                    before = tile_at(step - 1) * tile_chips + r
                    pair_send(which, before, r).wait_send()
        wu[turned] = xb[:, rows_of(k, wtile)].T
        for which, rhs in enumerate((gg, gu)):
            product(wu, pl.ds(which * wtile, wtile), turned, rhs)
            for r in range(tile_chips):
                pair_send(which, k * tile_chips + r, r).start()
                pair_keep(which, k * tile_chips + r, r).start()

    def down_grad_out(step):
        stage = rows_of(lax.rem(step, 2), wtile)
        return pltpu.make_async_copy(
            gg.at[stage], gw_hbm.at[0, rows_of(step, wtile)], out_sem.at[lax.rem(step, 2)]
        )

    def down_grad_tile(step, carry):
        @pl.when(step > 1)
        def _():
            down_grad_out(step - 2).wait()

        wu[turned] = xb[:, rows_of(step, wtile)].T
        product(gg, rows_of(lax.rem(step, 2), wtile), turned, hid)
        down_grad_out(step).start()
        return carry

    mid_near, mid_far, mid_back = 3 - lane, 6 - 3 * lane, 3 * lane - 3
    down_part(order_of(LANES - 1, lane))

    @pl.when(is_end)
    def _():
        for step in range(LANES - 1, 0, -1):
            for piece in range(pieces):
                sum_send(*ahead, order_of(step, lane), piece).start()

    sum_pass(*back, mid_near)
    wo = wd.at[:, pl.ds(0, width)]
    wo_load = pltpu.make_async_copy(wo_hbm, wo, late_sem.at[1])
    wo_load.start()
    grad_tile(0)
    load_pairs(0)
    add_pairs(0)
    grad_tile(1)
    load_pairs(1)
    sum_pass(*back, mid_far)
    add_pairs(1)
    grad_tile(2)
    load_pairs(2)
    sum_pass(*back, mid_back)
    sum_pass(*ahead, mid_far)
    add_pairs(2)
    grad_tile(3)
    for block in range(LANES):
        @pl.when(jnp.logical_and(has_right, block <= lane))
        def _(block=block):
            gather_copy(block, 0).wait_send()

        @pl.when(jnp.logical_and(has_left, block >= lane))
        def _(block=block):
            gather_copy(block, 1).wait_send()

    again = pltpu.make_async_copy(og_hbm, xb, load_sem.at[3])
    again.start()
    load_pairs(3)
    sum_last(*back, gm_ref)
    for block in range(LANES):
        @pl.when(block != lane)
        def _(block=block):
            for piece in range(pieces):
                sum_send(*back, block, piece).wait_send()

    own_og, grl, gao = (pb.at[pl.ds(k * tok, tok)] for k in range(3))
    og_load = pltpu.make_async_copy(own_og_hbm, own_og, late_sem.at[2])
    og_load.start()
    og_load.wait()
    resid_load.wait()

    def resid_rows(i, carry):
        some = pl.ds(pl.multiple_of(i * 32, 32), 32)
        values = mo_ref[some, :]
        grad_in = gm_ref[some, :]
        factor = lax.rsqrt(jnp.mean(values * values, axis=-1, keepdims=True) + EPS)
        scaled = grad_in * vecs_ref[1:2, :]
        inner = jnp.mean(scaled * values, axis=-1, keepdims=True)
        grad = own_og[some, :].astype(F32) + (factor * scaled - values * (factor * factor * factor) * inner)
        gm_ref[some, :] = grad
        grl[some, :] = grad.astype(BF16)
        vec_ref[1:2, :] = vec_ref[1:2, :] + jnp.sum(grad_in * values * factor, axis=0, keepdims=True)
        return carry

    lax.fori_loop(0, tok // 32, resid_rows, 0)
    grl_out = pltpu.make_async_copy(grl, grl_hbm, late_sem.at[2])
    grl_out.start()
    wo_load.wait()
    hw = width // LANES

    def head_cols(which):
        return pl.ds(pl.multiple_of(which * hw, hw), hw)

    def a_copy(target):
        return pltpu.make_async_remote_copy(
            gao.at[:, head_cols(target)], ga_hbm.at[rows_of(lane, tok)], a_send.at[target], a_recv.at[lane],
            device_id={"seq": target}, device_id_type=MESH_ID,
        )

    for step in range(1, LANES + 1):
        target = lax.rem(lane + step, LANES)
        gao[:, head_cols(target)] = nn(grl[...], wo[:, head_cols(target)]).astype(BF16)
        if step < LANES:
            a_copy(target).start()
    ga_own = pltpu.make_async_copy(gao.at[:, head_cols(lane)], ga_hbm.at[rows_of(lane, tok)], late_sem.at[1])
    ga_own.start()
    add_pairs(3)
    sum_pass(*ahead, mid_near)
    sum_pass(*ahead, mid_back)
    if square:
        pass_halves(0)
        pass_halves(1)
    else:
        for which in range(2):
            chip_keep(which).start()
            for mask in range(1, chips):
                chip_send(which, mask).start()
    again.wait()
    lax.fori_loop(0, wtiles, down_grad_tile, 0)
    sum_last(*ahead, mo_ref, True)
    grl_out.wait()
    ga_own.wait()
    for step in range(1, LANES):
        other = lax.rem(lane + step, LANES)
        a_copy(other).wait_send()
        pltpu.make_async_remote_copy(
            gao.at[:, head_cols(other)], ga_hbm.at[rows_of(other, tok)], a_send.at[0], a_recv.at[other],
            device_id={"seq": other}, device_id_type=MESH_ID,
        ).wait_recv()
    for gather in gathers:
        gather.end()
    down_grad_out(wtiles - 2).wait()
    down_grad_out(wtiles - 1).wait()
    for which in range(2):
        for r in range(tile_chips):
            last = tile_at(wtiles - 1) * tile_chips + r
            pair_send(which, last, r).wait_send()
        chip_keep(which).wait()
        if square:
            for mask, upper in ((3, 0), (3, 1), (2, 1), (1, 0)):
                first_hop(which, mask, upper).wait_send()
                if mask != 3:
                    first_hop(which, mask, upper).wait_recv()
            for upper in range(2):
                second_hop(which, upper).wait()
        else:
            for mask in range(1, chips):
                chip_send(which, mask).wait()

    for block in range(LANES):
        @pl.when(block != lane)
        def _(block=block):
            for piece in range(pieces):
                sum_send(*ahead, block, piece).wait_send()


def feed_forward(
    chips, mlp_local, grad_rows, gate_full, up_full, down_full, w_query, w_key, w_value, resid, out_grad, wo_full, vecs
):
    tok, width = mlp_local.shape
    units = gate_full.shape[1]
    row = tok * LANES
    own = width // (2 * chips)
    anywhere = pl.BlockSpec(memory_space=pl.ANY)
    vmem = pl.BlockSpec(memory_space=pltpu.VMEM)
    dma = pltpu.SemaphoreType.DMA
    shape = jax.ShapeDtypeStruct
    return pl.pallas_call(
        functools.partial(ff_kernel, chips),
        out_shape=(
            shape((tok, width), F32),
            shape((tok, width), F32),
            shape((8, width), F32),
            shape((tok, width), BF16),
            shape((row, width // LANES), BF16),
            shape((1, width, units), BF16),
            shape((2, chips, own, units), BF16),
            shape((3 if chips == 4 else chips, own, units), BF16),
            shape((3 if chips == 4 else chips, own, units), BF16),
            shape((2, 2, own // 2, units), BF16),
            shape((width, w_query.shape[1]), BF16),
            shape((width, w_key.shape[1]), BF16),
            shape((width, w_value.shape[1]), BF16),
        ),
        in_specs=[anywhere] * 11 + [vmem],
        out_specs=(vmem, vmem, vmem) + (anywhere,) * 10,
        scratch_shapes=[
            pltpu.VMEM((row, width), BF16),
            pltpu.VMEM((row, width), BF16),
            pltpu.VMEM((width, units), BF16),
            pltpu.VMEM((width, units), BF16),
            pltpu.VMEM((width, units), BF16),
            pltpu.VMEM((row, units), BF16),
            pltpu.VMEM((row, units), BF16),
            pltpu.VMEM((row, units), BF16),
            pltpu.VMEM((row, width), BF16),
            pltpu.VMEM((row + tok, width), BF16),
            pltpu.VMEM((row + tok, width), BF16),
            dma((5,)),
            dma((2, LANES)),
            dma((LANES,)),
            dma((LANES, width // 512)),
            dma((LANES + 1, width // 512)),
            dma((LANES, width // 512)),
            dma((LANES + 1, width // 512)),
            dma((2,)),
            dma((3, chips)),
            dma((3, chips)),
            dma((3, 2 * chips)),
            dma((3, 2)),
            dma((3, 2)),
            dma((3,)),
            *[dma((2, chips))] * 5,
            dma((2,)),
            dma((2, 4)),
            dma((2, 4)),
            dma((2, 2)),
            dma((2, 2)),
            dma((LANES,)),
            dma((LANES,)),
            dma((3,)),
        ],
        compiler_params=pltpu.CompilerParams(
            collective_id=3, has_side_effects=True, vmem_limit_bytes=60 * 2**20
        ),
        cost_estimate=pl.CostEstimate(
            flops=18 * row * width * units, bytes_accessed=12 * width * units, transcendentals=row * units
        ),
        name="feed_forward",
    )(
        mlp_local, grad_rows, gate_full, up_full, down_full, w_query, w_key, w_value, resid, out_grad, wo_full, vecs
    )


def chunked(rows, body, size=32):
    lax.fori_loop(0, rows // size, lambda i, c: (body(pl.multiple_of(i * size, size)), c)[1], 0)


def tn(left, right):
    return lax.dot_general(left, right, (((0,), (0,)), ((), ())), preferred_element_type=F32)


def back_kernel(
    chips, mats,
    gr_ref, mlp_vec_ref, x_ref, vecs_ref, qkv_ref, lse_ref, cos_ref, sin_ref, segc_ref, segr_ref,
    grl_hbm, ga_hbm, att_hbm, wq_hbm, wk_hbm, wv_hbm, nrm_hbm, gw_hbm,
    ig_ref, vec_ref, woz_ref, wqz_ref, fland,
    att, wfull, nrm, grl, ga, gk, gv, g, gl, lt,
    wop, wopair, woland, wores, zin, zsum,
    wqp, wqpair, wqland, theirs, mine, pairs, vz, vd, gn,
    load_sem, g_send, g_recv, h_send, h_recv,
    po_send, po_recv, so_send, so_recv, pq_send, pq_recv, sq_send, sq_recv,
    zr_send, zr_recv, zg_send, zg_recv, zq_send, zq_recv,
    fp_send, fp_recv, fs_send, fs_recv, slot_sem, v_send, v_recv, vs_send, vs_recv,
):
    dp, lane = lax.axis_index("dp"), lax.axis_index("seq")
    chip, core = dp // 2, lax.rem(dp, 2)
    sibling = 2 * chip + 1 - core
    tok, width = x_ref.shape
    row = tok * LANES
    part_rows = width // (2 * chips)
    heads = qkv_ref.shape[1] // HD - 2
    hw = heads * HD
    gwid = hw + 2 * HD
    here = rows_of(lane, tok)

    def lane_cols(which, size):
        return pl.ds(pl.multiple_of(which * size, size), size)

    loads = [
        pltpu.make_async_copy(src, dst, load_sem.at[k])
        for k, (src, dst) in enumerate(
            (
                (grl_hbm, grl),
                (att_hbm, att),
                (ga_hbm, ga),
                (nrm_hbm, nrm),
                (wq_hbm, wfull.at[:, pl.ds(0, LANES * hw)]),
                (wk_hbm, wfull.at[:, pl.ds(LANES * hw, KV_HEADS * HD)]),
                (wv_hbm, wfull.at[:, pl.ds(LANES * hw + KV_HEADS * HD, KV_HEADS * HD)]),
            )
        )
    ]
    for copy in loads:
        copy.start()
    vec_ref[...] = mlp_vec_ref[...]
    meet_all(chips)

    def to_dp(src, dst, send, recv, target):
        return pltpu.make_async_remote_copy(
            src, dst, send, recv, device_id={"dp": target}, device_id_type=MESH_ID
        )

    def to_lane(src, dst, send, recv, target):
        return pltpu.make_async_remote_copy(
            src, dst, send, recv, device_id={"seq": target}, device_id_type=MESH_ID
        )

    def ff_load(k, c, other):
        kept, sem = (theirs, slot_sem.at[0, k, c]) if other else (mine, slot_sem.at[1, k, c])
        rows = rows_of(2 * c + (1 - core if other else core), part_rows)
        return pltpu.make_async_copy(gw_hbm.at[mats[k], rows], kept.at[k, c], sem)

    def ff_pair(k, c):
        return to_dp(theirs.at[k, c], pairs.at[k, c], fp_send.at[k, c], fp_recv.at[k, c], sibling)

    def ff_send(k, mask):
        c = flipped(chip, mask)
        return to_dp(
            mine.at[k, c], fland.at[k, chip], fs_send.at[k, c], fs_recv.at[k, chip], 2 * c + core
        )

    def ff_own(k):
        return pltpu.make_async_copy(mine.at[k, chip], fland.at[k, chip], slot_sem.at[0, k, chip])

    ff_turns = [(k, mask) for k in range(len(mats)) for mask in list(range(chips - 1, 0, -1)) + [0]]
    for k, mask in ff_turns:
        ff_load(k, flipped(chip, mask), True).start()
        ff_load(k, flipped(chip, mask), False).start()
    for k, mask in ff_turns:
        c = flipped(chip, mask)
        ff_load(k, c, True).wait()
        ff_pair(k, c).start()

    def ff_add(k, mask):
        c = flipped(chip, mask)
        ff_load(k, c, False).wait()
        ff_pair(k, c).wait_recv()

        def add(start):
            some = pl.ds(start, 16)
            mine[k, c, some, :] = mine[k, c, some, :] + pairs[k, c, some, :]

        chunked(part_rows, add, 16)
        if mask:
            ff_send(k, mask).start()
        else:
            ff_own(k).start()

    loads[0].wait()
    loads[1].wait()

    def out_grad_tile(i, carry):
        some = lane_cols(i, 384)
        for n in range(width // 512):
            cols = slice(n * 512, (n + 1) * 512)
            wop[some, cols] = tn(grl[:, some], att[:, cols]).astype(BF16)
        return carry

    lax.fori_loop(0, width // 384, out_grad_tile, 0)

    class Sum:
        def __init__(self, partial, pair, land, pair_send, pair_recv, send, recv):
            self.partial, self.pair, self.land = partial, pair, land
            self.pair_send, self.pair_recv, self.send, self.recv = pair_send, pair_recv, send, recv

        def pair_copy(self, c):
            return to_dp(
                self.partial.at[rows_of(2 * c + 1 - core, part_rows)], self.pair.at[rows_of(c, part_rows)],
                self.pair_send.at[c], self.pair_recv.at[c], sibling,
            )

        def send_copy(self, mask):
            c = flipped(chip, mask)
            return to_dp(
                self.partial.at[rows_of(2 * c + core, part_rows)], self.land.at[rows_of(chip, part_rows)],
                self.send.at[c], self.recv.at[chip], 2 * c + core,
            )

        def begin(self):
            for mask in range(chips):
                self.pair_copy(flipped(chip, mask)).start()

        def middle(self):
            for mask in list(range(1, chips)) + [0]:
                c = flipped(chip, mask)
                self.pair_copy(c).wait_recv()

                def add(start, c=c):
                    mine = pl.ds(pl.multiple_of((2 * c + core) * part_rows + start, 16), 16)
                    other = pl.ds(pl.multiple_of(c * part_rows + start, 16), 16)
                    self.partial[mine, :] = self.partial[mine, :] + self.pair[other, :]

                chunked(part_rows, add, 16)
                if mask:
                    self.send_copy(mask).start()

        def last(self, out):
            for mask in range(1, chips):
                c = flipped(chip, mask)
                to_dp(
                    self.land.at[rows_of(c, part_rows)], self.land.at[rows_of(c, part_rows)],
                    self.send.at[0], self.recv.at[c], sibling,
                ).wait_recv()

            def add(start):
                some = pl.ds(start, 16)
                total = self.partial[pl.ds(pl.multiple_of(dp * part_rows + start, 16), 16), :].astype(F32)
                for mask in range(1, chips):
                    c = flipped(chip, mask)
                    total = total + self.land[
                        pl.ds(pl.multiple_of(c * part_rows + start, 16), 16), :
                    ].astype(F32)
                out(some, total.astype(BF16))

            chunked(part_rows, add, 16)

        def end(self):
            for mask in range(chips):
                self.pair_copy(flipped(chip, mask)).wait_send()
                if mask:
                    self.send_copy(mask).wait_send()

    out_sum = Sum(wop, wopair, woland, po_send, po_recv, so_send, so_recv)
    qkv_sum = Sum(wqp, wqpair, wqland, pq_send, pq_recv, sq_send, sq_recv)
    out_sum.begin()

    def turn(i, carry):
        some = rows_of(i, tok)
        turned = lse_ref[some, :].T
        for h in range(heads):
            lt[h, :, some] = jnp.broadcast_to(turned[h : h + 1, :], (8, tok))
        return carry

    lax.fori_loop(0, LANES, turn, 0)
    gk[...] = jnp.zeros_like(gk)
    gv[...] = jnp.zeros_like(gv)
    out_sum.middle()
    loads[2].wait()

    def out_store(some, value):
        wores[some, :] = value

    quarter = width // LANES

    def zr_copy(target):
        return to_lane(
            wores.at[:, lane_cols(target, quarter)], zin.at[lane], zr_send.at[target], zr_recv.at[lane], target
        )

    def own_out():
        out_sum.last(out_store)
        for step in range(1, LANES):
            zr_copy(lax.rem(lane + step, LANES)).start()
        zin[lane] = wores[:, lane_cols(lane, quarter)]

    def gq_copy(target):
        return to_lane(
            g.at[rows_of(target, tok), pl.ds(0, hw)],
            gl.at[:, pl.ds(pl.multiple_of(lane * gwid, HD), hw)],
            g_send.at[target], g_recv.at[lane], target,
        )

    def gkv_copy(target):
        return to_lane(
            g.at[rows_of(target, tok), pl.ds(hw, 2 * HD)],
            gl.at[:, pl.ds(pl.multiple_of(lane * gwid + hw, HD), 2 * HD)],
            h_send.at[target], h_recv.at[lane], target,
        )

    sub = 128
    scale = HD**-0.5
    for i in (3, 0, 2, 1):
        keys = (i + 1) * tok

        def att_step(t, carry, i=i, keys=keys):
            h = t // (tok // sub)
            start = i * tok + lax.rem(t, tok // sub) * sub
            some = pl.ds(pl.multiple_of(start, sub), sub)
            cols = lane_cols(h, HD)
            key, value = qkv_ref[0:keys, hw : hw + HD], qkv_ref[0:keys, hw + HD :]
            query, grad = qkv_ref[some, cols], ga[some, cols]
            scores = nt(key, query) * scale
            same = segc_ref[0:keys, 0:1] == segr_ref[0:1, some]
            behind = (
                lax.broadcasted_iota(jnp.int32, (keys, sub), 1) + start
                >= lax.broadcasted_iota(jnp.int32, (keys, sub), 0)
            )
            scores = jnp.where(jnp.logical_and(same, behind), scores, NEG_FILL)
            prob = jnp.exp(scores - lt[h, 0:1, some])
            grad_prob = nt(value, grad)
            inner = jnp.sum(prob * grad_prob, axis=0, keepdims=True)
            grad_scores = (prob * (grad_prob - inner)).astype(BF16)
            gq = (tn(grad_scores, key) * scale).astype(BF16).astype(F32)
            gk[0:keys, :] = gk[0:keys, :] + nn(grad_scores, query)
            gv[0:keys, :] = gv[0:keys, :] + nn(prob.astype(BF16), grad)
            g[some, cols] = (
                gq * cos_ref[some, :] + pltpu.roll(gq * sin_ref[some, :], HD // 2, 1)
            ).astype(BF16)
            return carry

        lax.fori_loop(0, heads * (tok // sub), att_step, 0)

        @pl.when(lane != i)
        def _(i=i):
            gq_copy(jnp.int32(i)).start()

    def close(start):
        some = pl.ds(start, 32)
        grad = (gk[some, :] * scale).astype(BF16).astype(F32)
        g[some, hw : hw + HD] = (
            grad * cos_ref[some, :] + pltpu.roll(grad * sin_ref[some, :], HD // 2, 1)
        ).astype(BF16)
        g[some, hw + HD :] = gv[some, :].astype(BF16)

    chunked(row, close)

    for step in range(1, LANES):
        gkv_copy(lax.rem(lane + step, LANES)).start()
    gl[:, lane_cols(lane, gwid)] = g[here, :]
    loads[3].wait()

    def qkv_grad_tile(i, carry):
        some = lane_cols(i, 384)
        wqp[some, :] = tn(nrm[:, some], g[...]).astype(BF16)
        return carry

    lax.fori_loop(0, width // 384, qkv_grad_tile, 0)
    qkv_sum.begin()
    sums = jnp.zeros((1, gwid), F32)
    for i in range(row // 128):
        sums = sums + jnp.sum(g[i * 128 : (i + 1) * 128, :].astype(F32), axis=0, keepdims=True)
    kv_head = lane * KV_HEADS // LANES
    vec_ref[2:3, lane_cols(lane, hw)] = sums[:, :hw]
    vec_ref[3:4, lane_cols(kv_head, HD)] = sums[:, hw : hw + HD]
    vec_ref[4:5, lane_cols(kv_head, HD)] = sums[:, hw + HD :]

    def qkv_store(some, value):
        wqz_ref[lane, some, :] = value

    def zq_copy(target):
        return to_lane(
            wqz_ref.at[lane], wqz_ref.at[lane], zq_send.at[target], zq_recv.at[lane], target
        )

    qkv_sum.middle()
    own_out()
    for turn in ff_turns:
        ff_add(*turn)
    qkv_sum.last(qkv_store)
    for step in range(1, LANES):
        zq_copy(lax.rem(lane + step, LANES)).start()
    for step in range(1, LANES):
        source = lax.rem(lane + step, LANES)
        to_lane(zin.at[source], zin.at[source], zr_send.at[0], zr_recv.at[source], source).wait_recv()
    total = zin[0].astype(F32)
    for j in range(1, LANES):
        total = total + zin[j].astype(F32)
    zsum[...] = total.astype(BF16)
    woz_ref[:, lane_cols(lane, quarter)] = zsum[...]

    def zg_copy(target):
        return to_lane(
            zsum, woz_ref.at[:, lane_cols(lane, quarter)], zg_send.at[target], zg_recv.at[lane], target
        )

    for step in range(1, LANES):
        zg_copy(lax.rem(lane + step, LANES)).start()

    for copy in loads[4:]:
        copy.wait()
    for step in range(1, LANES):
        source = lax.rem(lane + step, LANES)
        for begin, size, recv in ((0, hw, g_recv), (hw, 2 * HD, h_recv)):
            to_lane(
                g.at[here, pl.ds(begin, size)], gl.at[:, pl.ds(pl.multiple_of(source * gwid + begin, HD), size)],
                g_send.at[0], recv.at[source], source,
            ).wait_recv()
    group = LANES // KV_HEADS

    def kv_total(kv, offset):
        parts = [
            gl[:, (kv * group + j) * gwid + offset : (kv * group + j) * gwid + offset + HD].astype(F32)
            for j in range(group)
        ]
        return sum(parts[1:], parts[0]).astype(BF16)

    kv_grads = [kv_total(kv, hw + offset) for offset in (0, HD) for kv in range(KV_HEADS)]
    kv_grads = jnp.concatenate(kv_grads, axis=1)

    def normed_tile(i, carry):
        some = lane_cols(i, 512)
        total = nt(kv_grads, wfull[some, LANES * hw :])
        for j in range(LANES):
            total = total + nt(gl[:, j * gwid : j * gwid + hw], wfull[some, j * hw : (j + 1) * hw])
        gn[:, some] = total
        return carry

    lax.fori_loop(0, width // 512, normed_tile, 0)

    def input_rows(start):
        some = pl.ds(start, 32)
        values = x_ref[some, :].astype(F32)
        grad_in = gn[some, :]
        factor = lax.rsqrt(jnp.mean(values * values, axis=-1, keepdims=True) + EPS)
        scaled = grad_in * vecs_ref[0:1, :]
        inner = jnp.mean(scaled * values, axis=-1, keepdims=True)
        ig_ref[some, :] = gr_ref[some, :] + (
            factor * scaled - values * (factor * factor * factor) * inner
        )
        vec_ref[0:1, :] = vec_ref[0:1, :] + jnp.sum(grad_in * values * factor, axis=0, keepdims=True)

    chunked(tok, input_rows)

    def v_copy(target):
        return to_lane(vec_ref, vz.at[lane], v_send.at[target], v_recv.at[lane], target)

    for step in range(1, LANES):
        v_copy(lax.rem(lane + step, LANES)).start()

    for step in range(1, LANES):
        source = lax.rem(lane + step, LANES)
        to_lane(vz.at[source], vz.at[source], v_send.at[0], v_recv.at[source], source).wait_recv()
    for step in range(1, LANES):
        v_copy(lax.rem(lane + step, LANES)).wait_send()
    total = vec_ref[...]
    for step in range(1, LANES):
        total = total + vz[lax.rem(lane + step, LANES)]
    vd[chips] = total
    swap = to_dp(vd.at[chips], vd.at[chips + 1], vs_send.at[0], vs_recv.at[chips], sibling)
    swap.start()
    swap.wait()
    vd[chip] = vd[chips] + vd[chips + 1]

    def vs_copy(mask):
        return to_dp(
            vd.at[chip], vd.at[chip], vs_send.at[mask], vs_recv.at[chip], 2 * flipped(chip, mask) + core
        )

    for mask in range(1, chips):
        vs_copy(mask).start()
    for mask in range(1, chips):
        c = flipped(chip, mask)
        to_dp(vd.at[c], vd.at[c], vs_send.at[0], vs_recv.at[c], sibling).wait_recv()
    for mask in range(1, chips):
        vs_copy(mask).wait_send()
    total = vd[0]
    for c in range(1, chips):
        total = total + vd[c]
    vec_ref[...] = total

    for step in range(1, LANES):
        other = lax.rem(lane + step, LANES)
        to_lane(zsum, woz_ref.at[:, lane_cols(other, quarter)], zg_send.at[0], zg_recv.at[other], other).wait_recv()
        to_lane(wqz_ref.at[other], wqz_ref.at[other], zq_send.at[0], zq_recv.at[other], other).wait_recv()
        gq_copy(other).wait_send()
        gkv_copy(other).wait_send()
        zr_copy(other).wait_send()
        zg_copy(other).wait_send()
        zq_copy(other).wait_send()
    out_sum.end()
    qkv_sum.end()
    for k in range(len(mats)):
        ff_own(k).wait()
        for mask in range(chips):
            c = flipped(chip, mask)
            ff_pair(k, c).wait_send()
            if mask:
                to_dp(fland.at[k, c], fland.at[k, c], fs_send.at[k, 0], fs_recv.at[k, c], sibling).wait_recv()
                ff_send(k, mask).wait_send()


def back(
    chips, mats, grad_resid, mlp_vec, hidden_in, vecs, qkv, log_sum, cos_row, sin_row, seg_col,
    seg_row, grad_low, grad_att, attended, wq_full, wk_full, wv_full, normed_row, mlp_grads,
):
    tok, width = hidden_in.shape
    row = tok * LANES
    gwid = qkv.shape[1]
    hw = gwid - 2 * HD
    ff = mlp_grads.shape[2]
    own = width // (2 * chips)
    half = width // 2
    anywhere = pl.BlockSpec(memory_space=pl.ANY)
    vmem = pl.BlockSpec(memory_space=pltpu.VMEM)
    dma = pltpu.SemaphoreType.DMA
    shape = jax.ShapeDtypeStruct
    vmem_outs = [
        shape((tok, width), F32),
        shape((8, width), F32),
        shape((own, width), BF16),
        shape((LANES, own, gwid), BF16),
    ]
    hbm_outs = [shape((len(mats), chips, own, ff), BF16)]
    return pl.pallas_call(
        functools.partial(back_kernel, chips, mats),
        out_shape=vmem_outs + hbm_outs,
        in_specs=[vmem] * 10 + [anywhere] * 8,
        out_specs=[vmem] * len(vmem_outs) + [anywhere] * len(hbm_outs),
        scratch_shapes=[
            pltpu.VMEM((tok, width), BF16),
            pltpu.VMEM((width, width + 2 * KV_HEADS * HD), BF16),
            pltpu.VMEM((row, width), BF16),
            pltpu.VMEM((tok, width), BF16),
            pltpu.VMEM((row, hw), BF16),
            pltpu.VMEM((row, HD), F32),
            pltpu.VMEM((row, HD), F32),
            pltpu.VMEM((row, gwid), BF16),
            pltpu.VMEM((tok, LANES * gwid), BF16),
            pltpu.VMEM((hw // HD, 8, row), F32),
            pltpu.VMEM((width, width), BF16),
            pltpu.VMEM((half, width), BF16),
            pltpu.VMEM((half, width), BF16),
            pltpu.VMEM((own, width), BF16),
            pltpu.VMEM((LANES, own, width // LANES), BF16),
            pltpu.VMEM((own, width // LANES), BF16),
            pltpu.VMEM((width, gwid), BF16),
            pltpu.VMEM((half, gwid), BF16),
            pltpu.VMEM((half, gwid), BF16),
            *[pltpu.VMEM((len(mats), chips, own, ff), BF16)] * 3,
            pltpu.VMEM((LANES, 8, width), F32),
            pltpu.VMEM((chips + 2, 8, width), F32),
            pltpu.VMEM((tok, width), F32),
            dma((7,)),
            dma((LANES,)),
            dma((LANES,)),
            dma((LANES,)),
            dma((LANES,)),
            *[dma((chips,))] * 8,
            *[dma((LANES,))] * 6,
            *[dma((len(mats), chips))] * 4,
            dma((2, len(mats), chips)),
            dma((LANES,)),
            dma((LANES,)),
            dma((chips,)),
            dma((chips + 1,)),
        ],
        compiler_params=pltpu.CompilerParams(
            collective_id=2, has_side_effects=True, vmem_limit_bytes=61 * 2**20
        ),
        cost_estimate=pl.CostEstimate(
            flops=20 * row * width * gwid, bytes_accessed=12 * width * ff, transcendentals=row * width
        ),
        name="back",
    )(
        grad_resid, mlp_vec, hidden_in, vecs, qkv, log_sum, cos_row, sin_row, seg_col, seg_row,
        grad_low, grad_att, attended, wq_full, wk_full, wv_full, normed_row, mlp_grads,
    )


def body(
    hidden_in,
    segment_ids,
    position_ids,
    out_grad,
    attn_norm,
    w_query,
    w_key,
    w_value,
    b_query,
    b_key,
    b_value,
    w_out,
    mlp_norm,
    w_gate,
    w_up,
    w_down,
):
    chips = lax.axis_size("dp") // 2
    dp, lane = lax.axis_index("dp"), lax.axis_index("seq")
    local_tok, width = hidden_in.shape
    kv_group = LANES // KV_HEADS
    query_width = HEADS // LANES * HD

    def side_by_side(vectors, step, size):
        return sum(
            lax.pad(v, jnp.zeros((), v.dtype), [(k * step, size - k * step - v.shape[0], 0)])
            for k, v in enumerate(vectors)
        )

    vec = side_by_side((attn_norm, mlp_norm, b_query, b_key, b_value), 2 * HD, 16 * HD).reshape(16, HD)
    ids = side_by_side((position_ids, segment_ids), local_tok, 8 * local_tok).reshape(8, local_tok)
    inv_freq = ROPE_BASE ** (-(np.arange(HD // 2, dtype=np.float32) * np.float32(2.0 / HD)))
    freqs = np.tile(np.concatenate([inv_freq, inv_freq]).astype(np.float32)[None, :], (8, 1))
    (
        resid, mlp_local, vecs, qkv, attended, log_sum, cos_row, sin_row, seg_col, seg_row,
        normed_row, grad_rows, _, _, wo_full, gate_full, up_full, down_full,
    ) = front(
        chips, hidden_in, ids, freqs, out_grad, vec, w_query, w_key, w_value, w_out.T, w_gate, w_up, w_down
    )
    (
        total, grad_resid, mlp_vec, grad_low, grad_att, down_part, _, gate_grads, up_grads, _,
        wq_full, wk_full, wv_full,
    ) = feed_forward(
        chips, mlp_local, grad_rows, gate_full, up_full, down_full, w_query, w_key, w_value, resid, out_grad,
        wo_full, vecs,
    )
    block_out = total.astype(jnp.bfloat16)
    input_grad, vec_grads, out_grad_rows, qkv_grads, down_grads = back(
        chips, (0,), grad_resid, mlp_vec, hidden_in, vecs, qkv, log_sum, cos_row, sin_row, seg_col,
        seg_row, grad_low, grad_att, attended, wq_full, wk_full, wv_full, normed_row, down_part,
    )
    def chip_sum(parts):
        return jnp.sum(parts.astype(jnp.float32), axis=0)

    gate_grads, vec_grads = lax.optimization_barrier((gate_grads, vec_grads))
    gate_grad = chip_sum(gate_grads)
    gate_grad, up_grads = lax.optimization_barrier((gate_grad, up_grads))
    up_grad, down_grad = chip_sum(up_grads), chip_sum(down_grads[0])
    own = width // (2 * chips)
    kv_own = KV_HEADS * HD // (2 * chips)
    query_grad = jnp.concatenate(
        [qkv_grads[k, :, :query_width] for k in range(LANES)], axis=1
    ).astype(jnp.float32)

    def kv_grad(offset):
        parts = qkv_grads[:, :, offset : offset + HD].astype(jnp.float32)
        return jnp.concatenate(
            [
                jnp.sum(parts[k * kv_group : (k + 1) * kv_group], axis=0)
                for k in range(KV_HEADS)
            ],
            axis=1,
        )

    def own_vec(k, size):
        return lax.dynamic_slice(vec_grads, (k, dp * size), (1, size))[0]

    return (
        block_out,
        input_grad,
        own_vec(0, own),
        query_grad,
        kv_grad(query_width),
        kv_grad(query_width + HD),
        own_vec(2, own),
        own_vec(3, kv_own),
        own_vec(4, kv_own),
        out_grad_rows.astype(jnp.float32).T,
        own_vec(1, own),
        gate_grad,
        up_grad,
        down_grad,
    )


def solution(mesh):
    return jax.shard_map(
        body,
        mesh=mesh,
        in_specs=(
            P(("dp", "seq"), None),
            P(("dp", "seq")),
            P(("dp", "seq")),
            P(("dp", "seq"), None),
            P("dp"),
            P("dp", None),
            P("dp", None),
            P("dp", None),
            P("dp"),
            P("dp"),
            P("dp"),
            P(None, "dp"),
            P("dp"),
            P("dp", "seq"),
            P("dp", "seq"),
            P("dp", "seq"),
        ),
        out_specs=(
            P(("dp", "seq"), None),
            P(("dp", "seq"), None),
            P("dp"),
            P("dp", None),
            P("dp", None),
            P("dp", None),
            P("dp"),
            P("dp"),
            P("dp"),
            P(None, "dp"),
            P("dp"),
            P("dp", "seq"),
            P("dp", "seq"),
            P("dp", "seq"),
        ),
        check_vma=False,
    )
```
